32 devices in a mesh: dp: 16 (over z, x, core), tensor: 2 (over y).
Axes of the slice: x: 2, y: 2, z: 4, core: 2. Of those that a mesh axis runs over, the one named last changes fastest.
Arguments:
- patches: bfloat16 [25088, 1024], P('dp'), may hold values from -6 to 6
- cotangent: bfloat16 [25088, 1024], P('dp'), may hold values from -6 to 6
- clip_lengths: int32 [16, 8], P('dp'), may hold values from 0 to 1568, as said below
- attn_gain: float32 [1024], replicated, may hold values from 0.25 to 1.75
- attn_shift: float32 [1024], replicated, may hold values from -3 to 3
- qkv_weight: bfloat16 [1024, 3, 1024], P(None, None, 'tensor'), may hold values from -0.1875 to 0.1875
- qkv_bias: float32 [3, 1024], P(None, 'tensor'), may hold values from -3 to 3
- proj_weight: bfloat16 [1024, 1024], P('tensor'), may hold values from -2 to 2
- proj_bias: float32 [1024], replicated, may hold values from -3 to 3
- mlp_gain: float32 [1024], replicated, may hold values from 0.25 to 1.75
- mlp_shift: float32 [1024], replicated, may hold values from -3 to 3
- up_weight: bfloat16 [1024, 4096], P(None, 'tensor'), may hold values from -0.1875 to 0.1875
- up_bias: float32 [4096], P('tensor'), may hold values from -3 to 3
- down_weight: bfloat16 [4096, 1024], P('tensor'), may hold values from -0.09375 to 0.09375
- down_bias: float32 [1024], replicated, may hold values from -3 to 3
Outputs:
- block_out: bfloat16 [25088, 1024], P('dp')
- patch_grad: bfloat16 [25088, 1024], P('dp')
- attn_gain_grad: float32 [1024], replicated
- attn_shift_grad: float32 [1024], replicated
- qkv_weight_grad: float32 [1024, 3, 1024], P('dp', None, 'tensor')
- qkv_bias_grad: float32 [3, 1024], P(None, 'tensor')
- proj_weight_grad: float32 [1024, 1024], P('tensor', 'dp')
- proj_bias_grad: float32 [1024], replicated
- mlp_gain_grad: float32 [1024], replicated
- mlp_shift_grad: float32 [1024], replicated
- up_weight_grad: float32 [1024, 4096], P('dp', 'tensor')
- up_bias_grad: float32 [4096], P('tensor')
- down_weight_grad: float32 [4096, 1024], P('tensor', 'dp')
- down_bias_grad: float32 [1024], replicated
The draws below stay inside these ranges and needn't reach their ends.
Inputs may be any that keep to these rules, and one draw needn't show every extreme that they name: `clip_lengths`: each row holds one index of dp: either one video of 1568 tokens followed by zeros, or 8 images of 196 tokens each; every draw has rows of both kinds.
All inputs are finite; a program needn't handle non-finite values.
Results may differ from the reference program's by a relative error of at most 0.015.
Values may be sent and summed in bfloat16 or wider, within the bound.
A program may use at most 448 MiB of HBM per device.

```python
import jax
import jax.numpy as jnp
from jax import lax

D = 1024
HEADS = 16
HEAD_DIM = 64
FF = 4096
GRID = 14
IMG = 196
VID = 1568
SLOTS = 8
TOK_DEV = 1568
GROUPS = 16
TOKENS = 25088
N_TENSOR = 2


def draw_clip_lengths(key, part):
    key = jax.random.fold_in(key, 11)
    pick_key, first_key, second_key = jax.random.split(key, 3)
    holds_video = jax.random.randint(pick_key, (GROUPS,), 0, 10) < 3
    first_row = jax.random.randint(first_key, (), 0, GROUPS)
    second = (first_row + jax.random.randint(second_key, (), 1, GROUPS)) % GROUPS
    row_index = jnp.arange(GROUPS)
    holds_video = jnp.where(row_index == first_row, True, jnp.where(row_index == second, False, holds_video))
    slot_index = jnp.arange(SLOTS)
    video_row = jnp.where(slot_index == 0, VID, 0)
    image_row = jnp.full((SLOTS,), IMG)
    return jnp.where(holds_video[:, None], video_row[None, :], image_row[None, :]).astype(jnp.int32)


def levels(rng, extent, cuts, low, high):
    def one(dim, shards_of):
        steps = jax.random.uniform(jax.random.fold_in(jax.random.fold_in(rng, 6), dim), (shards_of,), jnp.float32, low / len(cuts), high / len(cuts))
        return jnp.repeat(jnp.exp(steps), extent[dim] // shards_of).reshape((-1,) + (1,) * (len(extent) - dim - 1))

    factor_of = one(*cuts[0])
    for cut in cuts[1:]:
        factor_of = factor_of * one(*cut)
    return factor_of


def gaussian(rng, extent, scale, reach, cuts=(), kind=jnp.bfloat16):
    values = scale * jax.random.normal(rng, extent, jnp.float32)
    if cuts:
        values = values * levels(rng, extent, cuts, -0.22, 0.18)
    return jnp.clip(values, -reach, reach).astype(kind)


def setup_inputs(seed: int = 0) -> dict:
    keys = jax.random.split(jax.random.key(seed), 16)
    return {
        "patches": gaussian(keys[0], (TOKENS, D), 1.0, 6.0, ((0, 16),)),
        "cotangent": gaussian(keys[1], (TOKENS, D), 1.0, 6.0, ((0, 16),)),
        "clip_lengths": draw_clip_lengths(jax.random.fold_in(keys[15], 71), 0),
        "attn_gain": jnp.clip(1.0 + 0.15 * jax.random.normal(keys[3], (D,), jnp.float32), 0.25, 1.75),
        "attn_shift": gaussian(keys[4], (D,), 0.5, 3.0, (), jnp.float32),
        "qkv_weight": gaussian(keys[5], (D, 3, D), D ** -0.5, 0.1875, ((2, 2),)),
        "qkv_bias": gaussian(keys[6], (3, D), 0.5, 3.0, ((1, 2),), jnp.float32),
        "proj_weight": gaussian(keys[7], (D, D), (max(D // 128, 4)) ** -0.5, 2.0, ((0, 2),)),
        "proj_bias": gaussian(keys[8], (D,), 0.5, 3.0, (), jnp.float32),
        "mlp_gain": jnp.clip(1.0 + 0.15 * jax.random.normal(keys[9], (D,), jnp.float32), 0.25, 1.75),
        "mlp_shift": gaussian(keys[10], (D,), 0.5, 3.0, (), jnp.float32),
        "up_weight": gaussian(keys[11], (D, FF), D ** -0.5, 0.1875, ((1, 2),)),
        "up_bias": gaussian(keys[12], (FF,), 0.5, 3.0, ((0, 2),), jnp.float32),
        "down_weight": gaussian(keys[13], (FF, D), FF ** -0.5, 0.09375, ((0, 2),)),
        "down_bias": gaussian(keys[14], (D,), 0.5, 3.0, (), jnp.float32),
    }


HIGHEST = lax.Precision.HIGHEST

@jax.custom_vjp
def low(v):
    return lax.optimization_barrier(v.astype(jnp.bfloat16)).astype(jnp.float32)

@jax.custom_vjp
def low_back(v):
    return v

def low_keep(v):
    return (low(v), None)

def low_pass(kept, grad):
    return (grad,)

def back_keep(v):
    return (v, None)

def back_low(kept, grad):
    return (low(grad),)
low.defvjp(low_keep, low_pass)
low_back.defvjp(back_keep, back_low)

def layer_norm(values, gain, shift):
    centre = values - lax.optimization_barrier(jnp.mean(values, axis=-1, keepdims=True))
    spread = lax.optimization_barrier(jnp.mean(centre * centre, axis=-1, keepdims=True))
    return centre * lax.rsqrt(spread + 1e-06) * gain + shift

def rotary_angles(offsets):
    pair_count = HEAD_DIM // 2
    side_pairs = pair_count * 11 // 32
    time_pairs = pair_count - 2 * side_pairs
    pair_index = jnp.arange(pair_count, dtype=jnp.int32)
    time_pair = pair_index < time_pairs
    height_pair = (pair_index >= time_pairs) & (pair_index < time_pairs + side_pairs)
    group_begin = jnp.where(time_pair, 0, jnp.where(height_pair, time_pairs, time_pairs + side_pairs))
    group_size = jnp.where(time_pair, time_pairs, side_pairs)
    inverse = jnp.power(10000.0, -(pair_index - group_begin).astype(jnp.float32) / group_size.astype(jnp.float32))
    frame_place = (offsets // IMG).astype(jnp.float32)
    row_place = (offsets % IMG // GRID).astype(jnp.float32)
    column_place = (offsets % GRID).astype(jnp.float32)
    position = jnp.where(time_pair[None, :], frame_place[:, None], jnp.where(height_pair[None, :], row_place[:, None], column_place[:, None]))
    angles = position * inverse[None, :]
    angles = jnp.concatenate([angles, angles], axis=1)
    return (jnp.cos(angles), jnp.sin(angles))

def rotate(values, cosine_table, sine_table):
    heads_view = values.reshape(values.shape[0], -1, HEAD_DIM)
    half_dim = HEAD_DIM // 2
    turned = jnp.concatenate([-heads_view[..., half_dim:], heads_view[..., :half_dim]], axis=-1)
    return heads_view * cosine_table[:, None, :] + turned * sine_table[:, None, :]

def forward(patches, attn_gain, attn_shift, qkv_weight, qkv_bias, proj_weight, proj_bias, mlp_gain, mlp_shift, up_weight, up_bias, down_weight, down_bias, cosine_table, sine_table, segment):
    normed = low(layer_norm(patches, attn_gain, attn_shift))
    mixed_rows = jnp.einsum('td,dsc->tsc', normed, qkv_weight, precision=HIGHEST) + qkv_bias
    mixed_rows = low_back(mixed_rows)
    queries = low(rotate(mixed_rows[:, 0], cosine_table, sine_table))
    key_rows = low(rotate(mixed_rows[:, 1], cosine_table, sine_table))
    values = low(mixed_rows[:, 2].reshape(TOK_DEV, HEADS, HEAD_DIM))
    same_clip = segment[:, None] == segment[None, :]
    scaling = HEAD_DIM ** (-0.5)

    def one_head(operands):
        query_head, key_head, value_head = operands
        scores = low_back(jnp.einsum('tc,sc->ts', query_head, key_head, precision=HIGHEST) * scaling)
        scores = jnp.where(same_clip, scores, -1e+30)
        row_top = lax.optimization_barrier(jnp.max(scores, axis=1, keepdims=True))
        weights = jnp.exp(scores - row_top)
        softmax_rows = weights / lax.optimization_barrier(jnp.sum(weights, axis=1, keepdims=True))
        return jnp.einsum('ts,sc->tc', low(softmax_rows), value_head, precision=HIGHEST)
    attended = lax.map(jax.checkpoint(one_head), (jnp.transpose(queries, (1, 0, 2)), jnp.transpose(key_rows, (1, 0, 2)), jnp.transpose(values, (1, 0, 2))))
    attended = jnp.transpose(attended, (1, 0, 2)).reshape(TOK_DEV, D)
    attended = low(low_back(attended))
    proj_parts = jnp.einsum('tnk,nkd->tnd', attended.reshape(TOK_DEV, N_TENSOR, D // N_TENSOR), proj_weight.reshape(N_TENSOR, D // N_TENSOR, D), precision=HIGHEST)
    branch = low_back(lax.optimization_barrier(jnp.sum(low(proj_parts), axis=1)) + proj_bias)
    residual = patches + branch
    normed_two = low(layer_norm(residual, mlp_gain, mlp_shift))
    upward = low_back(jnp.dot(normed_two, up_weight, precision=HIGHEST) + up_bias)
    activated = low(jax.nn.gelu(upward, approximate=False))
    down_parts = jnp.einsum('tnk,nkd->tnd', activated.reshape(TOK_DEV, N_TENSOR, FF // N_TENSOR), down_weight.reshape(N_TENSOR, FF // N_TENSOR, D), precision=HIGHEST)
    branch_two = low_back(lax.optimization_barrier(jnp.sum(low(down_parts), axis=1)) + down_bias)
    return residual + branch_two

def reference(patches, cotangent, clip_lengths, attn_gain, attn_shift, qkv_weight, qkv_bias, proj_weight, proj_bias, mlp_gain, mlp_shift, up_weight, up_bias, down_weight, down_bias):
    weight_list = tuple((item.astype(jnp.float32) for item in (attn_gain, attn_shift, qkv_weight, qkv_bias, proj_weight, proj_bias, mlp_gain, mlp_shift, up_weight, up_bias, down_weight, down_bias)))

    def per_group(totals, operands):
        patch_rows, cot_rows, length_row = operands
        bounds = jnp.cumsum(length_row).astype(jnp.int32)
        token_index = jnp.arange(TOK_DEV, dtype=jnp.int32)
        segment = lax.optimization_barrier(jnp.sum((token_index[:, None] >= bounds[None, :]).astype(jnp.int32), axis=1))
        starts = (bounds - length_row).astype(jnp.int32)
        offsets = token_index - jnp.take(starts, segment)
        cosine_table, sine_table = rotary_angles(offsets)

        def local_forward(rows_in, *weight_args):
            return forward(rows_in, *weight_args, cosine_table, sine_table, segment)
        result, pullback = jax.vjp(local_forward, patch_rows.astype(jnp.float32), *weight_list)
        gradients = pullback(cot_rows.astype(jnp.float32))
        totals = tuple([total_part + grad_part for total_part, grad_part in zip(totals, gradients[1:])])
        return (totals, (result.astype(jnp.bfloat16), gradients[0].astype(jnp.bfloat16)))
    initial = tuple((jnp.zeros_like(item) for item in weight_list))
    totals, outputs = lax.scan(per_group, initial, (patches.reshape(GROUPS, TOK_DEV, D), cotangent.reshape(GROUPS, TOK_DEV, D), clip_lengths))
    block_out = outputs[0].reshape(TOKENS, D)
    patch_grad = outputs[1].reshape(TOKENS, D)
    return (block_out, patch_grad, totals[0], totals[1], totals[2], totals[3], totals[4], totals[5], totals[6], totals[7], totals[8], totals[9], totals[10], totals[11])
```

```python
import functools
import math

import jax
import jax.numpy as jnp
from jax import lax
from jax.experimental import pallas as pl
from jax.experimental.pallas import tpu as pltpu
from jax.sharding import PartitionSpec as P

HEAD_DIM = 64
HALF_DIM = HEAD_DIM // 2
GRID = 14
IMG = 196
EPS = 1e-06
SCALING = HEAD_DIM ** (-0.5)
LOG2E = math.log2(math.e)
TILE = 256
FF_TILE = 512
FWD_CALLS = 4
BWD_CALLS = 4
VMEM_LIMIT = 60 * 1024 * 1024

bf16 = jnp.bfloat16
f32 = jnp.float32


def dot(left, right, left_dim, right_dim):
    return lax.dot_general(
        left, right, (((left_dim,), (right_dim,)), ((), ())), preferred_element_type=f32
    )


def rotary_angles(offsets):
    pair_count = HALF_DIM
    side_pairs = pair_count * 11 // 32
    time_pairs = pair_count - 2 * side_pairs
    pair_index = jnp.arange(pair_count, dtype=jnp.int32)
    time_pair = pair_index < time_pairs
    height_pair = (pair_index >= time_pairs) & (pair_index < time_pairs + side_pairs)
    group_begin = jnp.where(
        time_pair, 0, jnp.where(height_pair, time_pairs, time_pairs + side_pairs)
    )
    group_size = jnp.where(time_pair, time_pairs, side_pairs)
    inverse = jnp.power(
        10000.0, -(pair_index - group_begin).astype(f32) / group_size.astype(f32)
    )
    frame_place = (offsets // IMG).astype(f32)
    row_place = (offsets % IMG // GRID).astype(f32)
    column_place = (offsets % GRID).astype(f32)
    position = jnp.where(
        time_pair[:, None],
        frame_place[None, :],
        jnp.where(height_pair[:, None], row_place[None, :], column_place[None, :]),
    )
    angles = position * inverse[:, None]
    return (jnp.cos(angles), jnp.sin(angles))


def qkv_kernel(x_ref, gain_ref, shift_ref, w_ref, b_ref, cos_ref, sin_ref, normed_ref, out_ref):
    part = pl.program_id(0)

    @pl.when(part == 0)
    def _():
        x = x_ref[...].astype(f32)
        centre = x - jnp.mean(x, axis=1, keepdims=True)
        spread = jnp.mean(centre * centre, axis=1, keepdims=True)
        y = centre * lax.rsqrt(spread + EPS) * gain_ref[...] + shift_ref[...]
        normed_ref[...] = y.astype(bf16)

    mixed = dot(w_ref[...], normed_ref[...], 0, 1) + b_ref[...]
    cosine, sine = cos_ref[...], sin_ref[...]
    for begin in range(0, out_ref.shape[0], HEAD_DIM):
        low = mixed[begin : begin + HALF_DIM]
        high = mixed[begin + HALF_DIM : begin + HEAD_DIM]

        @pl.when(part < 2)
        def _():
            out_ref[begin : begin + HALF_DIM, :] = (low * cosine - high * sine).astype(bf16)
            out_ref[begin + HALF_DIM : begin + HEAD_DIM, :] = (high * cosine + low * sine).astype(
                bf16
            )

        @pl.when(part == 2)
        def _():
            out_ref[begin : begin + HALF_DIM, :] = low.astype(bf16)
            out_ref[begin + HALF_DIM : begin + HEAD_DIM, :] = high.astype(bf16)


def qkv_forward(patches, gain, shift, weight, bias, cosine, sine):
    tokens, width = patches.shape
    columns = weight.shape[1]
    part = columns // 3
    whole = lambda i: (0, 0)
    return pl.pallas_call(
        qkv_kernel,
        grid=(3,),
        out_shape=(
            jax.ShapeDtypeStruct((tokens, width), bf16),
            jax.ShapeDtypeStruct((columns, tokens), bf16),
        ),
        in_specs=[
            pl.BlockSpec((tokens, width), whole),
            pl.BlockSpec((1, width), whole),
            pl.BlockSpec((1, width), whole),
            pl.BlockSpec((width, part), lambda i: (0, i)),
            pl.BlockSpec((part, 1), lambda i: (i, 0)),
            pl.BlockSpec(cosine.shape, whole),
            pl.BlockSpec(sine.shape, whole),
        ],
        out_specs=(
            pl.BlockSpec((tokens, width), whole),
            pl.BlockSpec((part, tokens), lambda i: (i, 0)),
        ),
        compiler_params=pltpu.CompilerParams(vmem_limit_bytes=VMEM_LIMIT),
        cost_estimate=pl.CostEstimate(
            flops=2 * tokens * width * columns, bytes_accessed=14_000_000, transcendentals=0
        ),
        name="qkv_forward",
    )(patches, gain[None, :], shift[None, :], weight, bias[:, None], cosine, sine)


def query_tiles(tokens):
    return [(begin, min(begin + TILE, tokens)) for begin in range(0, tokens, TILE)]


def key_window(begin, end, tokens):
    low = begin // IMG * IMG // 128 * 128
    high = min(tokens, ((end - 1) // IMG + 1) * IMG)
    return low, min(tokens, (high + 127) // 128 * 128)


def attend_kernel(len_ref, q_ref, k_ref, v_ref, e_ref, half_ref, whole_ref, total_ref, out_scr):
    tokens = q_ref.shape[1]
    half = tokens // 2
    holds_video = len_ref[0, 0] == tokens

    def one_tile(begin, end, low, high, masked):
        scores = dot(k_ref[:, low:high], q_ref[:, begin:end], 0, 0)
        if masked:
            width = end - begin
            query = begin + lax.broadcasted_iota(jnp.int32, (1, width), 1)
            first = jnp.zeros((1, width), jnp.int32)
            for clip in range(1, tokens // IMG):
                first = jnp.where(query >= clip * IMG, clip * IMG, first)
            key = low + lax.broadcasted_iota(jnp.int32, (high - low, width), 0)
            scores = jnp.where((key >= first) & (key < first + IMG), scores, -1e30)
        top = jnp.max(scores, axis=0, keepdims=True)
        weights = jnp.exp2((scores - top) * (SCALING * LOG2E))
        weights_low = weights.astype(bf16)
        e_ref[0, low:high, begin:end] = weights_low
        if low > 0:
            e_ref[0, :low, begin:end] = jnp.zeros((low, end - begin), bf16)
        if high < tokens:
            e_ref[0, high:, begin:end] = jnp.zeros((tokens - high, end - begin), bf16)
        total = jnp.sum(weights, axis=0, keepdims=True)
        out = dot(v_ref[:, low:high], weights_low, 1, 0)
        out_scr[:, begin:end] = out / total
        total_ref[0, :, begin:end] = total

    @pl.when(holds_video)
    def _():
        for begin, end in query_tiles(tokens):
            one_tile(begin, end, 0, tokens, False)

    @pl.when(jnp.logical_not(holds_video))
    def _():
        for begin, end in query_tiles(tokens):
            low, high = key_window(begin, end, tokens)
            one_tile(begin, end, low, high, True)

    out = out_scr[...].astype(bf16)
    whole_ref[...] = out
    half_ref[0] = out[:, :half]
    half_ref[1] = out[:, half:]


def attend_forward(qkv, clip_lengths, first_head, heads):
    columns, tokens = qkv.shape
    local_heads = columns // 3 // HEAD_DIM
    half = tokens // 2
    block = lambda part: pl.BlockSpec(
        (HEAD_DIM, tokens), lambda i: (part * local_heads + first_head + i, 0)
    )
    return pl.pallas_call(
        attend_kernel,
        grid=(heads,),
        out_shape=(
            jax.ShapeDtypeStruct((heads, tokens, tokens), bf16),
            jax.ShapeDtypeStruct((2, heads * HEAD_DIM, half), bf16),
            jax.ShapeDtypeStruct((heads * HEAD_DIM, tokens), bf16),
            jax.ShapeDtypeStruct((heads, 1, tokens), f32),
        ),
        in_specs=[pl.BlockSpec(memory_space=pltpu.SMEM), block(0), block(1), block(2)],
        out_specs=(
            pl.BlockSpec((1, tokens, tokens), lambda i: (i, 0, 0)),
            pl.BlockSpec((2, HEAD_DIM, half), lambda i: (0, i, 0)),
            pl.BlockSpec((HEAD_DIM, tokens), lambda i: (i, 0)),
            pl.BlockSpec((1, 1, tokens), lambda i: (i, 0, 0)),
        ),
        scratch_shapes=[pltpu.VMEM((HEAD_DIM, tokens), f32)],
        compiler_params=pltpu.CompilerParams(vmem_limit_bytes=VMEM_LIMIT),
        cost_estimate=pl.CostEstimate(
            flops=16 * heads * tokens * tokens * HEAD_DIM,
            bytes_accessed=2 * heads * tokens * tokens,
            transcendentals=heads * tokens * tokens,
        ),
        name="attend_forward",
    )(clip_lengths, qkv, qkv, qkv)


def attend_back_kernel(
    e_ref,
    q_ref,
    k_ref,
    v_ref,
    out_ref,
    total_ref,
    left_ref,
    right_ref,
    cos_ref,
    sin_ref,
    half_ref,
    whole_ref,
    up_scr,
    up_low,
    score_grad,
):
    tokens = q_ref.shape[1]
    half = tokens // 2
    up_scr[:, :half] = left_ref[...].astype(f32)
    up_scr[:, half:] = right_ref[...].astype(f32)
    up_low[...] = (up_scr[...] / total_ref[0]).astype(bf16)
    centre = jnp.sum(up_low[...].astype(f32) * out_ref[...].astype(f32), axis=0, keepdims=True)
    for begin, end in query_tiles(tokens):
        prob_grad = dot(v_ref[...], up_low[:, begin:end], 0, 0)
        score_grad[:, begin:end] = (
            e_ref[0, :, begin:end].astype(f32) * (prob_grad - centre[:, begin:end])
        ).astype(bf16)
    cosine, sine = cos_ref[...], sin_ref[...]

    def store(part, low, high):
        for row, value in ((0, low), (HALF_DIM, high)):
            value = value.astype(bf16)
            whole_ref[part, row : row + HALF_DIM] = value
            half_ref[0, part, row : row + HALF_DIM] = value[:, :half]
            half_ref[1, part, row : row + HALF_DIM] = value[:, half:]

    def unrotated(part, grad):
        low, high = grad[:HALF_DIM] * SCALING, grad[HALF_DIM:] * SCALING
        store(part, low * cosine + high * sine, high * cosine - low * sine)

    value_grad = dot(up_low[...], e_ref[0], 1, 1)
    store(2, value_grad[:HALF_DIM], value_grad[HALF_DIM:])
    unrotated(1, dot(q_ref[...], score_grad[...], 1, 1))
    unrotated(0, dot(k_ref[...], score_grad[...], 1, 0))


def attend_backward(weights, qkv, attended, totals, left, right, cosine, sine, first, inner, heads):
    columns, tokens = qkv.shape
    local_heads = columns // 3 // HEAD_DIM
    half = tokens // 2
    block = lambda part: pl.BlockSpec(
        (HEAD_DIM, tokens), lambda i: (part * local_heads + first + i, 0)
    )
    whole = lambda i: (0, 0)
    return pl.pallas_call(
        attend_back_kernel,
        grid=(heads,),
        out_shape=(
            jax.ShapeDtypeStruct((2, 3, heads * HEAD_DIM, half), bf16),
            jax.ShapeDtypeStruct((3, heads * HEAD_DIM, tokens), bf16),
        ),
        in_specs=[
            pl.BlockSpec((1, tokens, tokens), lambda i: (inner + i, 0, 0)),
            block(0),
            block(1),
            block(2),
            pl.BlockSpec((HEAD_DIM, tokens), lambda i: (inner + i, 0)),
            pl.BlockSpec((1, 1, tokens), lambda i: (inner + i, 0, 0)),
            pl.BlockSpec((HEAD_DIM, half), lambda i: (first + i, 0)),
            pl.BlockSpec((HEAD_DIM, half), lambda i: (first + i, 0)),
            pl.BlockSpec(cosine.shape, whole),
            pl.BlockSpec(sine.shape, whole),
        ],
        out_specs=(
            pl.BlockSpec((2, 3, HEAD_DIM, half), lambda i: (0, 0, i, 0)),
            pl.BlockSpec((3, HEAD_DIM, tokens), lambda i: (0, i, 0)),
        ),
        scratch_shapes=[
            pltpu.VMEM((HEAD_DIM, tokens), f32),
            pltpu.VMEM((HEAD_DIM, tokens), bf16),
            pltpu.VMEM((tokens, tokens), bf16),
        ],
        compiler_params=pltpu.CompilerParams(vmem_limit_bytes=VMEM_LIMIT),
        cost_estimate=pl.CostEstimate(
            flops=32 * heads * tokens * tokens * HEAD_DIM,
            bytes_accessed=2 * heads * tokens * tokens,
            transcendentals=0,
        ),
        name="attend_backward",
    )(weights, qkv, qkv, qkv, attended, totals, left, right, cosine, sine)


def normal_parts(value):
    a = jnp.abs(value)
    t = 1.0 / (1.0 + (0.3275911 / math.sqrt(2.0)) * a)
    bell = jnp.exp2(value * value * (-0.5 * LOG2E))
    c = [0.5 * x for x in (0.254829592, -0.284496736, 1.421413741, -1.453152027, 1.061405429)]
    tail = ((((c[4] * t + c[3]) * t + c[2]) * t + c[1]) * t + c[0]) * t * bell
    return jnp.where(value >= 0, 1.0 - tail, tail), bell * (1.0 / math.sqrt(2.0 * math.pi))


def mlp_kernel(n_ref, c_ref, up_ref, bias_ref, down_ref, out_ref, ngrad_ref, w_ref, bgrad_ref):
    step = pl.program_id(0)
    upward = dot(n_ref[...], up_ref[...], 1, 0) + bias_ref[...]
    act_grad = dot(c_ref[...], down_ref[...], 1, 1)
    share, density = normal_parts(upward)
    activated = (upward * share).astype(bf16)
    upward_grad = (act_grad * (share + upward * density)).astype(bf16)
    bgrad_ref[...] = jnp.sum(upward_grad.astype(f32), axis=0, keepdims=True)
    out = dot(activated, down_ref[...], 1, 0)
    ngrad = dot(upward_grad, up_ref[...], 1, 1)

    @pl.when(step == 0)
    def _():
        out_ref[...] = out
        ngrad_ref[...] = ngrad

    @pl.when(step > 0)
    def _():
        out_ref[...] += out
        ngrad_ref[...] += ngrad

    w_ref[0] = dot(n_ref[...], upward_grad, 0, 0).astype(bf16)
    w_ref[1] = dot(c_ref[...], activated, 0, 0).astype(bf16)


def mlp(normed, cotangent, up_weight, up_bias, down_weight):
    tokens, width = normed.shape
    hidden = up_weight.shape[1]
    whole = lambda i: (0, 0)
    return pl.pallas_call(
        mlp_kernel,
        grid=(hidden // FF_TILE,),
        out_shape=(
            jax.ShapeDtypeStruct((tokens, width), f32),
            jax.ShapeDtypeStruct((tokens, width), f32),
            jax.ShapeDtypeStruct((2, width, hidden), bf16),
            jax.ShapeDtypeStruct((1, hidden), f32),
        ),
        in_specs=[
            pl.BlockSpec((tokens, width), whole),
            pl.BlockSpec((tokens, width), whole),
            pl.BlockSpec((width, FF_TILE), lambda i: (0, i)),
            pl.BlockSpec((1, FF_TILE), lambda i: (0, i)),
            pl.BlockSpec((FF_TILE, width), lambda i: (i, 0)),
        ],
        out_specs=(
            pl.BlockSpec((tokens, width), whole),
            pl.BlockSpec((tokens, width), whole),
            pl.BlockSpec((2, width, FF_TILE), lambda i: (0, 0, i)),
            pl.BlockSpec((1, FF_TILE), lambda i: (0, i)),
        ),
        compiler_params=pltpu.CompilerParams(vmem_limit_bytes=VMEM_LIMIT),
        cost_estimate=pl.CostEstimate(
            flops=12 * tokens * width * hidden,
            bytes_accessed=24_000_000,
            transcendentals=tokens * hidden,
        ),
        name="feed_forward",
    )(normed, cotangent, up_weight, up_bias[None, :], down_weight)


def over_tensor(value):
    return lax.ppermute(value, "tensor", [(0, 1), (1, 0)])


def over_bit(value, bit, count):
    return lax.ppermute(value, "dp", [(i, i ^ (1 << bit)) for i in range(count)])


def other_half(weight, place, count):
    rows = weight.shape[0] // 4
    mine = place % 4
    piece = lax.dynamic_slice_in_dim(weight, mine * rows, rows, 0)
    first = over_tensor(piece)
    second = over_bit(first, 1, count)
    third = over_bit(jnp.stack([first, second]), 0, count)
    whole = jnp.zeros_like(weight)
    for offset, part in ((0, first), (2, second), (1, third[0]), (3, third[1])):
        whole = lax.dynamic_update_slice_in_dim(whole, part, (mine ^ offset) * rows, 0)
    return whole


def scatter_sum(grads, place, count):
    groups, width, columns = grads.shape
    bits = count.bit_length() - 1
    for bit in range(bits):
        left = count >> (bit + 1)
        split = grads.reshape(groups, left, 2, width // count, columns)
        mine = (place >> bit) & 1
        keep = lax.dynamic_index_in_dim(split, mine, 2, keepdims=False)
        send = lax.dynamic_index_in_dim(split, 1 - mine, 2, keepdims=False)
        got = over_bit(send, bit, count)
        grads = keep.astype(f32) + got.astype(f32)
        if bit < bits - 1:
            grads = grads.astype(bf16)
    return grads.reshape(groups, width // count, columns)


def all_sum(vector, count):
    for bit in range(count.bit_length() - 1):
        vector = vector + over_bit(vector, bit, count)
    return vector


def norm_parts(values):
    centre = values - jnp.mean(values, axis=-1, keepdims=True)
    spread = jnp.mean(centre * centre, axis=-1, keepdims=True)
    scale = lax.rsqrt(spread + EPS)
    return centre * scale, scale


def norm_back(grad, unit, scale, gain):
    c = grad * gain
    mean = jnp.mean(c, axis=-1, keepdims=True)
    along = jnp.mean(c * unit, axis=-1, keepdims=True)
    return scale * (c - mean - unit * along)


def on_device(
    count,
    patches,
    cotangent,
    clip_lengths,
    attn_gain,
    attn_shift,
    qkv_weight,
    qkv_bias,
    proj_weight,
    proj_bias,
    mlp_gain,
    mlp_shift,
    up_weight,
    up_bias,
    down_weight,
    down_bias,
):
    tokens, width = patches.shape
    half = tokens // 2
    local_width = proj_weight.shape[0]
    local_heads = local_width // HEAD_DIM
    side = lax.axis_index("tensor")
    place = lax.axis_index("dp")
    first_side = side == 0

    def pick(pair):
        mine = lax.dynamic_index_in_dim(pair, side, 0, keepdims=False)
        return mine, lax.dynamic_index_in_dim(pair, 1 - side, 0, keepdims=False)

    def my_rows(value):
        return lax.dynamic_slice_in_dim(value, side * half, half, 0)

    def both_rows(mine):
        theirs = over_tensor(mine)
        return jnp.concatenate(
            [jnp.where(first_side, mine, theirs), jnp.where(first_side, theirs, mine)], axis=0
        )

    proj_other = other_half(proj_weight, place, count)
    up_other = other_half(up_weight, place, count)
    down_other = other_half(down_weight, place, count)
    qkv_flat = qkv_weight.reshape(width, 3 * local_width)
    qkv_other = other_half(qkv_flat, place, count)

    clip_len = clip_lengths[0, 0]
    cosine, sine = rotary_angles(jnp.arange(tokens, dtype=jnp.int32) % clip_len)
    normed, qkv = qkv_forward(
        patches, attn_gain, attn_shift, qkv_flat, qkv_bias.reshape(-1), cosine, sine
    )

    heads_call = local_heads // FWD_CALLS
    weights, attended, totals, att_mine, att_other = [], [], [], [], []
    for call in range(FWD_CALLS):
        e, halves, whole, total = attend_forward(qkv, clip_lengths, call * heads_call, heads_call)
        keep, send = pick(halves)
        weights.append(e)
        attended.append(whole)
        totals.append(total)
        att_mine.append(keep)
        att_other.append(over_tensor(send))
    att_mine = jnp.concatenate(att_mine, axis=0)
    att_other = jnp.concatenate(att_other, axis=0)

    patch_rows = my_rows(patches).astype(f32)
    cot_rows = my_rows(cotangent)
    attn_out = dot(att_mine, proj_weight, 0, 0).astype(bf16).astype(f32) + dot(
        att_other, proj_other, 0, 0
    ).astype(bf16).astype(f32)
    residual = patch_rows + (attn_out + proj_bias)
    unit_two, scale_two = norm_parts(residual)
    normed_two = (unit_two * mlp_gain + mlp_shift).astype(bf16)

    up_bias_other = over_tensor(up_bias)
    out_a, ngrad_a, wgrad_a, bgrad_a = mlp(normed_two, cot_rows, up_weight, up_bias, down_weight)
    out_b, ngrad_b, wgrad_b, bgrad_b = mlp(
        normed_two, cot_rows, up_other, up_bias_other, down_other
    )
    mlp_out = out_a.astype(bf16).astype(f32) + out_b.astype(bf16).astype(f32)
    block_out = both_rows((residual + (mlp_out + down_bias)).astype(bf16))

    normed_two_grad = ngrad_a + ngrad_b
    mlp_gain_grad = jnp.sum(normed_two_grad * unit_two, axis=0)
    mlp_shift_grad = jnp.sum(normed_two_grad, axis=0)
    cot_wide = cot_rows.astype(f32)
    residual_grad = cot_wide + norm_back(normed_two_grad, unit_two, scale_two, mlp_gain)
    branch_low = residual_grad.astype(bf16)
    proj_bias_grad = jnp.sum(branch_low.astype(f32), axis=0)
    down_bias_grad = jnp.sum(cot_wide, axis=0)

    att_grad_send = dot(proj_other, branch_low, 1, 1).astype(bf16)
    att_grad_got = over_tensor(att_grad_send)
    att_grad_mine = dot(proj_weight, branch_low, 1, 1).astype(bf16)
    left = jnp.where(first_side, att_grad_mine, att_grad_got)
    right = jnp.where(first_side, att_grad_got, att_grad_mine)

    proj_grad = jnp.stack(
        [dot(branch_low, att_mine, 0, 1).astype(bf16), dot(branch_low, att_other, 0, 1).astype(bf16)]
    )

    heads_call = local_heads // BWD_CALLS
    mixed_whole, mixed_mine, mixed_other = [], [], []
    for call in range(BWD_CALLS):
        first = call * heads_call
        index, inner = divmod(first, local_heads // FWD_CALLS)
        halves, whole = attend_backward(
            weights[index],
            qkv,
            attended[index],
            totals[index],
            left,
            right,
            cosine,
            sine,
            first,
            inner,
            heads_call,
        )
        keep, send = pick(halves)
        mixed_whole.append(whole)
        mixed_mine.append(keep)
        mixed_other.append(over_tensor(send))
    mixed_whole = jnp.concatenate(mixed_whole, axis=1).reshape(3 * local_width, tokens)
    mixed_mine = jnp.concatenate(mixed_mine, axis=1).reshape(3 * local_width, half)
    mixed_other = jnp.concatenate(mixed_other, axis=1).reshape(3 * local_width, half)

    qkv_bias_grad = jnp.sum(mixed_whole.astype(f32), axis=1)
    normed_grad = dot(mixed_mine, qkv_flat, 0, 1) + dot(mixed_other, qkv_other, 0, 1)
    unit_one, scale_one = norm_parts(patch_rows)
    attn_gain_grad = jnp.sum(normed_grad * unit_one, axis=0)
    attn_shift_grad = jnp.sum(normed_grad, axis=0)
    patch_grad = both_rows(
        (residual_grad + norm_back(normed_grad, unit_one, scale_one, attn_gain)).astype(bf16)
    )

    qkv_grad = dot(normed, mixed_whole, 0, 1).astype(bf16)

    mlp_a = scatter_sum(wgrad_a, place, count)
    mlp_b = scatter_sum(wgrad_b, place, count)
    mlp_sum = mlp_a + over_tensor(mlp_b.astype(bf16)).astype(f32)
    proj_pair = scatter_sum(proj_grad, place, count)
    proj_sum = proj_pair[0] + over_tensor(proj_pair[1].astype(bf16)).astype(f32)
    qkv_sum = scatter_sum(qkv_grad[None], place, count)[0]

    early = jnp.concatenate([mlp_gain_grad, mlp_shift_grad, proj_bias_grad, down_bias_grad])
    got = over_tensor(jnp.concatenate([early, bgrad_b[0]]))
    early = all_sum(
        jnp.concatenate([early + got[: 4 * width], bgrad_a[0] + got[4 * width :]]), count
    )
    late = jnp.concatenate([attn_gain_grad, attn_shift_grad])
    late = late + over_tensor(late)
    late = all_sum(jnp.concatenate([late, qkv_bias_grad]), count)
    return (
        block_out,
        patch_grad,
        late[:width],
        late[width : 2 * width],
        qkv_sum.reshape(width // count, 3, local_width),
        late[2 * width :].reshape(3, local_width),
        proj_sum.T,
        early[2 * width : 3 * width],
        early[:width],
        early[width : 2 * width],
        mlp_sum[0],
        early[4 * width :],
        mlp_sum[1].T,
        early[3 * width : 4 * width],
    )


def solution(mesh):
    return jax.shard_map(
        functools.partial(on_device, mesh.shape["dp"]),
        mesh=mesh,
        in_specs=(
            P("dp", None),
            P("dp", None),
            P("dp", None),
            P(),
            P(),
            P(None, None, "tensor"),
            P(None, "tensor"),
            P("tensor", None),
            P(),
            P(),
            P(),
            P(None, "tensor"),
            P("tensor"),
            P("tensor", None),
            P(),
        ),
        out_specs=(
            P("dp", None),
            P("dp", None),
            P(),
            P(),
            P("dp", None, "tensor"),
            P(None, "tensor"),
            P("tensor", "dp"),
            P(),
            P(),
            P(),
            P("dp", "tensor"),
            P("tensor"),
            P("tensor", "dp"),
            P(),
        ),
        check_vma=False,
    )
```

```python
import functools
import math

import jax
import jax.numpy as jnp
from jax import lax
from jax.experimental import pallas as pl
from jax.experimental.pallas import tpu as pltpu
from jax.sharding import PartitionSpec as P

HEAD_DIM = 64
HALF_DIM = HEAD_DIM // 2
GRID = 14
IMG = 196
EPS = 1e-06
SCALING = HEAD_DIM ** (-0.5)
LOG2E = math.log2(math.e)
CHUNKS = 7
MASK_ROWS = 16
ONES_ROWS = 16
FORBIDDEN = -1e30
QUARTERS = 4
VMEM_LIMIT = 60 * 1024 * 1024

MESH = pl.DeviceIdType.MESH

bf16 = jnp.bfloat16
f32 = jnp.float32


def dot(left, right, left_dim, right_dim):
    return lax.dot_general(
        left, right, (((left_dim,), (right_dim,)), ((), ())), preferred_element_type=f32
    )


def rotary_angles(offsets):
    pair_count = HALF_DIM
    side_pairs = pair_count * 11 // 32
    time_pairs = pair_count - 2 * side_pairs
    pair_index = jnp.arange(pair_count, dtype=jnp.int32)
    time_pair = pair_index < time_pairs
    height_pair = (pair_index >= time_pairs) & (pair_index < time_pairs + side_pairs)
    group_begin = jnp.where(
        time_pair, 0, jnp.where(height_pair, time_pairs, time_pairs + side_pairs)
    )
    group_size = jnp.where(time_pair, time_pairs, side_pairs)
    inverse = jnp.power(
        10000.0, -(pair_index - group_begin).astype(f32) / group_size.astype(f32)
    )
    frame_place = (offsets // IMG).astype(f32)
    row_place = (offsets % IMG // GRID).astype(f32)
    column_place = (offsets % GRID).astype(f32)
    position = jnp.where(
        time_pair[:, None],
        frame_place[None, :],
        jnp.where(height_pair[:, None], row_place[None, :], column_place[None, :]),
    )
    angles = position * inverse[:, None]
    return (jnp.cos(angles), jnp.sin(angles))


def params(collective_id=None):
    if collective_id is None:
        return pltpu.CompilerParams(vmem_limit_bytes=VMEM_LIMIT)
    return pltpu.CompilerParams(
        vmem_limit_bytes=VMEM_LIMIT, collective_id=collective_id, has_side_effects=True
    )


def greet(partners):
    barrier = pltpu.get_barrier_semaphore()
    for partner in partners:
        pl.semaphore_signal(barrier, inc=1, device_id=partner, device_id_type=MESH)
    pl.semaphore_wait(barrier, len(partners))


def remote(source, target, send_sem, recv_sem, partner):
    return pltpu.make_async_remote_copy(
        src_ref=source,
        dst_ref=target,
        send_sem=send_sem,
        recv_sem=recv_sem,
        device_id=partner,
        device_id_type=MESH,
    )


def whole_block(shape):
    return pl.BlockSpec(shape, lambda *_: (0,) * len(shape))


def norm_parts(values):
    centre = values - jnp.mean(values, axis=1, keepdims=True)
    spread = jnp.mean(centre * centre, axis=1, keepdims=True)
    scale = lax.rsqrt(spread + EPS)
    return centre * scale, scale


def norm_back(grad, unit, scale, gain):
    c = grad * gain
    mean = jnp.mean(c, axis=1, keepdims=True)
    along = jnp.mean(c * unit, axis=1, keepdims=True)
    return scale * (c - mean - unit * along)


def column_sum(values):
    return jnp.sum(values, axis=0, keepdims=True)


def qkv_kernel(x_ref, gain_ref, shift_ref, w_ref, b_ref, cos_ref, sin_ref, normed_ref, out_ref):
    part = pl.program_id(0)

    @pl.when(part == 0)
    def _():
        unit, _ = norm_parts(x_ref[...].astype(f32))
        width = x_ref.shape[1]
        normed_ref[:width] = (unit * gain_ref[...] + shift_ref[...]).astype(bf16).T
        normed_ref[width:] = jnp.ones((ONES_ROWS, x_ref.shape[0]), bf16)

    rows = out_ref.shape[1]
    bias = jnp.broadcast_to(b_ref[pl.ds(part, 1), :], (8, rows)).T[:, :1]
    mixed = dot(w_ref[0], normed_ref[: x_ref.shape[1]], 0, 0) + bias

    @pl.when(part < 2)
    def _():
        cosine, sine = cos_ref[...], sin_ref[...]
        for begin in range(0, rows, HEAD_DIM):
            middle, end = begin + HALF_DIM, begin + HEAD_DIM
            low, high = mixed[begin:middle], mixed[middle:end]
            out_ref[0, begin:middle, :] = (low * cosine - high * sine).astype(bf16)
            out_ref[0, middle:end, :] = (high * cosine + low * sine).astype(bf16)

    @pl.when(part == 2)
    def _():
        out_ref[0] = mixed.astype(bf16)


def qkv_forward(patches, gain, shift, weight, bias, cosine, sine):
    tokens, width = patches.shape
    columns = weight.shape[2]
    return pl.pallas_call(
        qkv_kernel,
        grid=(3,),
        out_shape=(
            jax.ShapeDtypeStruct((width + ONES_ROWS, tokens), bf16),
            jax.ShapeDtypeStruct((3, columns, tokens), bf16),
        ),
        in_specs=[
            whole_block((tokens, width)),
            whole_block((1, width)),
            whole_block((1, width)),
            pl.BlockSpec((1, width, columns), lambda i: (i, 0, 0)),
            whole_block((3, columns)),
            whole_block(cosine.shape),
            whole_block(sine.shape),
        ],
        out_specs=(
            whole_block((width + ONES_ROWS, tokens)),
            pl.BlockSpec((1, columns, tokens), lambda i: (i, 0, 0)),
        ),
        compiler_params=params(),
        cost_estimate=pl.CostEstimate(
            flops=6 * tokens * width * columns, bytes_accessed=14_000_000, transcendentals=0
        ),
        name="qkv_forward",
    )(patches, gain[None, :], shift[None, :], weight, bias, cosine, sine)


def clip_masks(clip_len, tokens):
    token = jnp.arange(tokens, dtype=jnp.int32)[None, :] // IMG
    row = jnp.arange(MASK_ROWS, dtype=jnp.int32)[:, None]
    same = token == row
    images = clip_len < tokens
    forbid = images & jnp.logical_not(same) & (row < tokens // IMG)
    return jnp.where(forbid, FORBIDDEN, 0.0).astype(bf16), same.astype(bf16)


def attend_kernel(
    q_ref, k_ref, v_ref, qm_ref, km_ref, e_ref, half_ref, whole_ref, total_ref, k_scr, s_scr
):
    tokens = q_ref.shape[2]
    half = tokens // 2
    rows = tokens // CHUNKS
    queries = jnp.concatenate([q_ref[0], qm_ref[...]], axis=0)
    k_scr[...] = jnp.concatenate([k_ref[0], km_ref[...]], axis=0).T
    values = jnp.concatenate([v_ref[0], jnp.ones((16, tokens), bf16)], axis=0)

    longest = jnp.max(column_sum(jnp.square(q_ref[0].astype(f32)))) * jnp.max(
        column_sum(jnp.square(k_ref[0].astype(f32)))
    )
    small = longest < (60.0 / (SCALING * LOG2E)) ** 2

    def finish(out):
        total = out[HEAD_DIM : HEAD_DIM + 1]
        total_ref[0] = total
        attended = (out[:HEAD_DIM] / total).astype(bf16)
        whole_ref[...] = attended
        half_ref[0] = attended[:, :half]
        half_ref[1] = attended[:, half:]

    @pl.when(small)
    def _():
        out = jnp.zeros((HEAD_DIM + 16, tokens), f32)
        for begin in range(0, tokens, rows):
            end = begin + rows
            scores = dot(k_scr[begin:end], queries, 1, 0)
            weights = jnp.exp2(scores * (SCALING * LOG2E)).astype(bf16)
            e_ref[0, begin:end] = weights
            out = out + dot(values[:, begin:end], weights, 1, 0)
        finish(out)

    @pl.when(jnp.logical_not(small))
    def _():
        s_scr[...] = dot(k_scr[...], queries, 1, 0)
        top = jnp.max(s_scr[...], axis=0, keepdims=True)
        e_ref[0] = jnp.exp2((s_scr[...] - top) * (SCALING * LOG2E)).astype(bf16)
        finish(dot(values, e_ref[0], 1, 0))


def attend_forward(qkv, query_mask, key_mask, first, heads):
    tokens = qkv.shape[2]
    half = tokens // 2
    block = lambda part: pl.BlockSpec((1, HEAD_DIM, tokens), lambda i: (part, first + i, 0))
    return pl.pallas_call(
        attend_kernel,
        grid=(heads,),
        out_shape=(
            jax.ShapeDtypeStruct((heads, tokens, tokens), bf16),
            jax.ShapeDtypeStruct((2, heads * HEAD_DIM, half), bf16),
            jax.ShapeDtypeStruct((heads * HEAD_DIM, tokens), bf16),
            jax.ShapeDtypeStruct((heads, 1, tokens), f32),
        ),
        in_specs=[
            block(0),
            block(1),
            block(2),
            whole_block((MASK_ROWS, tokens)),
            whole_block((MASK_ROWS, tokens)),
        ],
        out_specs=(
            pl.BlockSpec((1, tokens, tokens), lambda i: (i, 0, 0)),
            pl.BlockSpec((2, HEAD_DIM, half), lambda i: (0, i, 0)),
            pl.BlockSpec((HEAD_DIM, tokens), lambda i: (i, 0)),
            pl.BlockSpec((1, 1, tokens), lambda i: (i, 0, 0)),
        ),
        scratch_shapes=[
            pltpu.VMEM((tokens, HEAD_DIM + MASK_ROWS), bf16),
            pltpu.VMEM((tokens, tokens), f32),
        ],
        compiler_params=params(),
        cost_estimate=pl.CostEstimate(
            flops=16 * heads * tokens * tokens * HEAD_DIM,
            bytes_accessed=2 * heads * tokens * tokens,
            transcendentals=heads * tokens * tokens,
        ),
        name="attend_forward",
    )(qkv, qkv, qkv, query_mask, key_mask)


def attend_back_kernel(
    e_ref,
    q_ref,
    k_ref,
    v_ref,
    out_ref,
    total_ref,
    left_ref,
    right_ref,
    cos_ref,
    sin_ref,
    normed_ref,
    mine_ref,
    keep_ref,
    send_ref,
    sum_ref,
    other_ref,
    up_scr,
    up_low,
    v_scr,
    score_grad,
    turned,
    pair_scr,
    outgoing,
    grad,
    send_sem,
    recv_sem,
):
    head, heads = pl.program_id(0), pl.num_programs(0)
    tokens = q_ref.shape[2]
    half = tokens // 2
    side = lax.axis_index("tensor")
    core = lax.axis_index("dp") % 2
    peer = {"tensor": 1 - side}
    slot = head % 2

    def exchange(index):
        return remote(
            outgoing.at[index % 2],
            other_ref.at[index],
            send_sem.at[index % 2],
            recv_sem.at[index],
            peer,
        )

    @pl.when(head == 0)
    def _():
        greet([peer])

    up_scr[:, :half] = left_ref[...].astype(f32)
    up_scr[:, half:] = right_ref[...].astype(f32)
    up_low[...] = (up_scr[...] / total_ref[0]).astype(bf16)
    v_scr[...] = v_ref[0].T
    centre = column_sum(up_low[...].astype(f32) * out_ref[...].astype(f32))
    cosine, sine = cos_ref[...], sin_ref[...]

    @pl.when(head >= 2)
    def _():
        exchange(head - 2).wait_send()

    def store(part, low, high):
        for row, value in ((0, low), (HALF_DIM, high)):
            left, right = value[:, :half], value[:, half:]
            mine_ref[part, row : row + HALF_DIM] = jnp.where(side == 0, left, right).astype(bf16)
            outgoing[slot, part, row : row + HALF_DIM] = jnp.where(side == 0, right, left).astype(
                bf16
            )
            begin = pl.multiple_of(slot * HEAD_DIM + row, HALF_DIM)
            pair_scr[part, pl.ds(begin, HALF_DIM)] = value.astype(bf16)

    def unrotated(part, grad):
        low, high = grad[:HALF_DIM] * SCALING, grad[HALF_DIM:] * SCALING
        store(part, low * cosine + high * sine, high * cosine - low * sine)

    value_grad = dot(up_low[...], e_ref[0], 1, 1)
    store(2, value_grad[:HALF_DIM], value_grad[HALF_DIM:])
    prob_grad = dot(v_scr[...], up_low[...], 1, 0)
    score_grad[...] = (e_ref[0].astype(f32) * (prob_grad - centre)).astype(bf16)
    unrotated(0, dot(k_ref[0], score_grad[...], 1, 0))
    turned[...] = score_grad[...].T
    unrotated(1, dot(q_ref[0], turned[...], 1, 0))
    exchange(head).start()

    @pl.when(slot == 1)
    def _():
        width = grad.shape[0] - ONES_ROWS
        for part in range(3):
            grad[...] = dot(normed_ref[...], pair_scr[part], 1, 1)
            split_rows(grad, keep_ref.at[part], send_ref.at[part], core)
            sum_ref[part : part + 1] = grad[width : width + 1]

    @pl.when(head == heads - 1)
    def _():
        exchange(heads - 2).wait_send()
        exchange(heads - 1).wait_send()
        for index in range(other_ref.shape[0]):
            exchange(index).wait_recv()


def attend_backward(
    count, weights, qkv, attended, totals, left, right, cosine, sine, normed
):
    tokens = qkv.shape[2]
    half = tokens // 2
    heads = weights.shape[0]
    columns = heads * HEAD_DIM
    width = normed.shape[0] - ONES_ROWS
    split = (3, count // 2, width // count)
    block = lambda part: pl.BlockSpec((1, HEAD_DIM, tokens), lambda i: (part, i, 0))
    half_block = pl.BlockSpec((HEAD_DIM, half), lambda i: (i, 0))
    pair_block = pl.BlockSpec(split + (2 * HEAD_DIM,), lambda i: (0, 0, 0, i // 2))
    return pl.pallas_call(
        attend_back_kernel,
        grid=(heads,),
        out_shape=(
            jax.ShapeDtypeStruct((3, columns, half), bf16),
            jax.ShapeDtypeStruct(split + (columns,), bf16),
            jax.ShapeDtypeStruct(split + (columns,), bf16),
            jax.ShapeDtypeStruct((3, columns), f32),
            jax.ShapeDtypeStruct((heads, 3, HEAD_DIM, half), bf16),
        ),
        in_specs=[
            pl.BlockSpec((1, tokens, tokens), lambda i: (i, 0, 0)),
            block(0),
            block(1),
            block(2),
            pl.BlockSpec((HEAD_DIM, tokens), lambda i: (i, 0)),
            pl.BlockSpec((1, 1, tokens), lambda i: (i, 0, 0)),
            half_block,
            half_block,
            whole_block(cosine.shape),
            whole_block(sine.shape),
            whole_block(normed.shape),
        ],
        out_specs=(
            pl.BlockSpec((3, HEAD_DIM, half), lambda i: (0, i, 0)),
            pair_block,
            pair_block,
            pl.BlockSpec((3, 2 * HEAD_DIM), lambda i: (0, i // 2)),
            pl.BlockSpec(memory_space=pl.ANY),
        ),
        scratch_shapes=[
            pltpu.VMEM((HEAD_DIM, tokens), f32),
            pltpu.VMEM((HEAD_DIM, tokens), bf16),
            pltpu.VMEM((tokens, HEAD_DIM), bf16),
            pltpu.VMEM((tokens, tokens), bf16),
            pltpu.VMEM((tokens, tokens), bf16),
            pltpu.VMEM((3, 2 * HEAD_DIM, tokens), bf16),
            pltpu.VMEM((2, 3, HEAD_DIM, half), bf16),
            pltpu.VMEM((width + ONES_ROWS, 2 * HEAD_DIM), f32),
            pltpu.SemaphoreType.DMA((2,)),
            pltpu.SemaphoreType.DMA((heads,)),
        ],
        compiler_params=params(0),
        cost_estimate=pl.CostEstimate(
            flops=32 * heads * tokens * tokens * HEAD_DIM,
            bytes_accessed=2 * heads * tokens * tokens,
            transcendentals=0,
        ),
        name="attend_backward",
    )(weights, qkv, qkv, qkv, attended, totals, left, right, cosine, sine, normed)


def normal_parts(value):
    a = jnp.abs(value)
    t = 1.0 / (1.0 + (0.3275911 / math.sqrt(2.0)) * a)
    bell = jnp.exp2(value * value * (-0.5 * LOG2E))
    c = [0.5 * x for x in (0.254829592, -0.284496736, 1.421413741, -1.453152027, 1.061405429)]
    tail = ((((c[4] * t + c[3]) * t + c[2]) * t + c[1]) * t + c[0]) * t * bell
    return jnp.where(value >= 0, 1.0 - tail, tail), bell * (1.0 / math.sqrt(2.0 * math.pi))


def split_rows(grad, keep_ref, send_ref, core):
    count, rows = keep_ref.shape[:2]
    for pair in range(count):
        for ref, odd in ((keep_ref, core), (send_ref, 1 - core)):
            begin = pl.multiple_of((2 * pair + odd) * rows, rows)
            ref[pair] = grad[pl.ds(begin, rows), :].astype(bf16)


def accumulate(step, total, term):
    @pl.when(step == 0)
    def _():
        total[...] = term

    @pl.when(step > 0)
    def _():
        total[...] += term


def feed_up(step, core, n_ref, c_ref, up, bias, down, act_ref, slope_ref, total, grad, keep, send):
    upward = dot(n_ref[...], up, 1, 0) + bias
    share, density = normal_parts(upward)
    activated = (upward * share).astype(bf16)
    act_ref[...] = activated
    slope_ref[...] = (share + upward * density).astype(bf16)
    accumulate(step, total, dot(activated, down, 1, 0))
    grad[...] = dot(c_ref[...], activated, 0, 0)
    split_rows(grad, keep, send, core)


def first_kernel(pieces, place_ref, *refs):
    att_mine, refs = refs[:pieces], refs[pieces:]
    att_other, refs = refs[:pieces], refs[pieces:]
    (
        proj_ref,
        proj_other_ref,
        patch_ref,
        proj_bias_ref,
        gain_ref,
        shift_ref,
        cot_ref,
        up_ref,
        bias_ref,
        down_ref,
        residual_ref,
        n_ref,
        slope_ref,
        out_ref,
        keep_ref,
        send_ref,
        sum_ref,
        act_scr,
        total,
        grad,
    ) = refs
    step = pl.program_id(0)

    @pl.when(step == 0)
    def _():
        def branch(parts, weight_ref):
            value, row = None, 0
            for part in parts:
                rows = part.shape[0]
                term = dot(part[...], weight_ref[row : row + rows], 0, 0)
                value = term if value is None else value + term
                row += rows
            return value.astype(bf16).astype(f32)

        attn_out = branch(att_mine, proj_ref) + branch(att_other, proj_other_ref)
        residual = patch_ref[...].astype(f32) + (attn_out + proj_bias_ref[...])
        residual_ref[...] = residual
        unit, _ = norm_parts(residual)
        n_ref[...] = (unit * gain_ref[...] + shift_ref[...]).astype(bf16)
        sum_ref[...] = column_sum(cot_ref[...].astype(f32))

    feed_up(
        step,
        place_ref[1],
        n_ref,
        cot_ref,
        up_ref[...],
        bias_ref[...],
        down_ref[...],
        act_scr,
        slope_ref,
        total,
        grad,
        keep_ref,
        send_ref,
    )

    @pl.when(step == pl.num_programs(0) - 1)
    def _():
        out_ref[...] = total[...].astype(bf16)


def feed_first(
    place,
    count,
    att_mine,
    att_other,
    proj,
    proj_other,
    patches,
    proj_bias,
    gain,
    shift,
    cot,
    up,
    bias,
    down,
):
    tokens, width = patches.shape
    half = tokens // 2
    hidden = up.shape[1]
    tile = 1024
    mine = pl.BlockSpec((half, width), lambda i, place: (place[0], 0))
    row = whole_block((1, width))
    rows = whole_block((half, width))
    split = (count // 2, width // count)
    return pl.pallas_call(
        functools.partial(first_kernel, len(att_mine)),
        grid_spec=pltpu.PrefetchScalarGridSpec(
            num_scalar_prefetch=1,
            grid=(hidden // tile,),
            in_specs=[whole_block(x.shape) for x in att_mine]
            + [whole_block(x.shape) for x in att_other]
            + [
                whole_block(proj.shape),
                whole_block(proj.shape),
                mine,
                row,
                row,
                row,
                mine,
                pl.BlockSpec((width, tile), lambda i, place: (0, i)),
                pl.BlockSpec((1, tile), lambda i, place: (0, i)),
                pl.BlockSpec((tile, width), lambda i, place: (i, 0)),
            ],
            out_specs=(
                rows,
                rows,
                pl.BlockSpec((half, tile), lambda i, place: (0, i)),
                rows,
                pl.BlockSpec(split + (tile,), lambda i, place: (0, 0, i)),
                pl.BlockSpec(split + (tile,), lambda i, place: (0, 0, i)),
                row,
            ),
            scratch_shapes=[
                pltpu.VMEM((half, tile), bf16),
                pltpu.VMEM((half, width), f32),
                pltpu.VMEM((width, tile), f32),
            ],
        ),
        out_shape=(
            jax.ShapeDtypeStruct((half, width), f32),
            jax.ShapeDtypeStruct((half, width), bf16),
            jax.ShapeDtypeStruct((half, hidden), bf16),
            jax.ShapeDtypeStruct((half, width), bf16),
            jax.ShapeDtypeStruct(split + (hidden,), bf16),
            jax.ShapeDtypeStruct(split + (hidden,), bf16),
            jax.ShapeDtypeStruct((1, width), f32),
        ),
        compiler_params=params(),
        cost_estimate=pl.CostEstimate(
            flops=8 * half * width * hidden, bytes_accessed=24_000_000, transcendentals=half * hidden
        ),
        name="feed_first",
    )(
        place,
        *att_mine,
        *att_other,
        proj,
        proj_other,
        patches,
        proj_bias[None, :],
        gain[None, :],
        shift[None, :],
        cot,
        up,
        bias[None, :],
        down,
    )


def second_kernel(
    place_ref,
    n_ref,
    cot_ref,
    up_ref,
    bias_ref,
    down_ref,
    residual_ref,
    first_ref,
    down_bias_ref,
    slope_ref,
    out_ref,
    keep_ref,
    send_ref,
    act_scr,
    total,
    grad,
):
    step = pl.program_id(0)
    feed_up(
        step,
        place_ref[1],
        n_ref,
        cot_ref,
        up_ref[0],
        bias_ref[...],
        down_ref[0],
        act_scr,
        slope_ref,
        total,
        grad,
        keep_ref,
        send_ref,
    )

    @pl.when(step == pl.num_programs(0) - 1)
    def _():
        mlp_out = first_ref[...].astype(f32) + total[...].astype(bf16).astype(f32)
        out_ref[...] = (residual_ref[...] + (mlp_out + down_bias_ref[...])).astype(bf16)


def feed_second(place, count, normed, cot, up, bias, down, residual, first, down_bias):
    half, width = normed.shape
    quarters, _, tile = up.shape
    hidden = quarters * tile
    rows = whole_block((half, width))
    split = (count // 2, width // count)
    return pl.pallas_call(
        second_kernel,
        grid_spec=pltpu.PrefetchScalarGridSpec(
            num_scalar_prefetch=1,
            grid=(quarters,),
            in_specs=[
                rows,
                pl.BlockSpec((half, width), lambda i, place: (place[0], 0)),
                pl.BlockSpec((1, width, tile), lambda i, place: (i ^ place[2], 0, 0)),
                pl.BlockSpec((1, tile), lambda i, place: (0, i)),
                pl.BlockSpec((1, tile, width), lambda i, place: (i ^ place[2], 0, 0)),
                rows,
                rows,
                whole_block((1, width)),
            ],
            out_specs=(
                pl.BlockSpec((half, tile), lambda i, place: (0, i)),
                rows,
                pl.BlockSpec(split + (tile,), lambda i, place: (0, 0, i)),
                pl.BlockSpec(split + (tile,), lambda i, place: (0, 0, i)),
            ),
            scratch_shapes=[
                pltpu.VMEM((half, tile), bf16),
                pltpu.VMEM((half, width), f32),
                pltpu.VMEM((width, tile), f32),
            ],
        ),
        out_shape=(
            jax.ShapeDtypeStruct((half, hidden), bf16),
            jax.ShapeDtypeStruct((half, width), bf16),
            jax.ShapeDtypeStruct(split + (hidden,), bf16),
            jax.ShapeDtypeStruct(split + (hidden,), bf16),
        ),
        compiler_params=params(),
        cost_estimate=pl.CostEstimate(
            flops=6 * half * width * hidden, bytes_accessed=24_000_000, transcendentals=half * hidden
        ),
        name="feed_second",
    )(place, normed, cot, up, bias[None, :], down, residual, first, down_bias[None, :])


def feed_down(step, core, n_ref, c_ref, up, down, slope_ref, sum_ref, grad, keep, send):
    act_grad = dot(c_ref[...], down, 1, 1)
    upward_grad = (act_grad * slope_ref[...].astype(f32)).astype(bf16)
    sum_ref[...] = column_sum(upward_grad.astype(f32))
    grad[...] = dot(n_ref[...], upward_grad, 0, 0)
    split_rows(grad, keep, send, core)
    return dot(upward_grad, up, 1, 1)


def back_first_kernel(
    place_ref,
    n_ref,
    c_ref,
    up_ref,
    down_ref,
    slope_ref,
    total_ref,
    sum_ref,
    keep_ref,
    send_ref,
    grad,
):
    step = pl.program_id(0)
    term = feed_down(
        step,
        place_ref[1],
        n_ref,
        c_ref,
        up_ref[...],
        down_ref[...],
        slope_ref,
        sum_ref,
        grad,
        keep_ref,
        send_ref,
    )
    accumulate(step, total_ref, term)


def feed_back_first(place, count, normed, cot, up, down, slope):
    half, width = normed.shape
    hidden = up.shape[1]
    tile = 1024
    rows = whole_block((half, width))
    split = (count // 2, width // count)
    return pl.pallas_call(
        back_first_kernel,
        grid_spec=pltpu.PrefetchScalarGridSpec(
            num_scalar_prefetch=1,
            grid=(hidden // tile,),
            in_specs=[
                rows,
                pl.BlockSpec((half, width), lambda i, place: (place[0], 0)),
                pl.BlockSpec((width, tile), lambda i, place: (0, i)),
                pl.BlockSpec((tile, width), lambda i, place: (i, 0)),
                pl.BlockSpec((half, tile), lambda i, place: (0, i)),
            ],
            out_specs=(
                rows,
                pl.BlockSpec((1, tile), lambda i, place: (0, i)),
                pl.BlockSpec(split + (tile,), lambda i, place: (0, 0, i)),
                pl.BlockSpec(split + (tile,), lambda i, place: (0, 0, i)),
            ),
            scratch_shapes=[pltpu.VMEM((width, tile), f32)],
        ),
        out_shape=(
            jax.ShapeDtypeStruct((half, width), f32),
            jax.ShapeDtypeStruct((1, hidden), f32),
            jax.ShapeDtypeStruct(split + (hidden,), bf16),
            jax.ShapeDtypeStruct(split + (hidden,), bf16),
        ),
        compiler_params=params(),
        cost_estimate=pl.CostEstimate(
            flops=6 * half * width * hidden, bytes_accessed=24_000_000, transcendentals=0
        ),
        name="feed_back_first",
    )(place, normed, cot, up, down, slope)


def back_second_kernel(
    place_ref,
    n_ref,
    c_ref,
    up_ref,
    down_ref,
    slope_ref,
    first_ref,
    residual_ref,
    gain_ref,
    proj_ref,
    proj_other_ref,
    sum_ref,
    keep_ref,
    send_ref,
    grad_ref,
    low_ref,
    vector_ref,
    mine_ref,
    other_ref,
    grad,
    total,
):
    step = pl.program_id(0)

    @pl.when(step == 0)
    def _():
        total[...] = first_ref[...]

    total[...] += feed_down(
        step,
        place_ref[1],
        n_ref,
        c_ref,
        up_ref[0],
        down_ref[0],
        slope_ref,
        sum_ref,
        grad,
        keep_ref,
        send_ref,
    )

    @pl.when(step == pl.num_programs(0) - 1)
    def _():
        unit, scale = norm_parts(residual_ref[...])
        normed_grad = total[...]
        residual_grad = c_ref[...].astype(f32) + norm_back(normed_grad, unit, scale, gain_ref[...])
        low = residual_grad.astype(bf16)
        grad_ref[...] = residual_grad
        low_ref[...] = low
        vector_ref[0:1] = column_sum(normed_grad * unit)
        vector_ref[1:2] = column_sum(normed_grad)
        vector_ref[2:3] = column_sum(low.astype(f32))
        mine_ref[...] = dot(proj_ref[...], low, 1, 1).astype(bf16)
        other_ref[...] = dot(proj_other_ref[...], low, 1, 1).astype(bf16)


def feed_back_second(
    place, count, normed, cot, up, down, slope, first, residual, gain, proj, proj_other
):
    half, width = normed.shape
    quarters, _, tile = up.shape
    hidden = quarters * tile
    rows = whole_block((half, width))
    heads = whole_block((proj.shape[0], half))
    split = (count // 2, width // count)
    return pl.pallas_call(
        back_second_kernel,
        grid_spec=pltpu.PrefetchScalarGridSpec(
            num_scalar_prefetch=1,
            grid=(quarters,),
            in_specs=[
                rows,
                pl.BlockSpec((half, width), lambda i, place: (place[0], 0)),
                pl.BlockSpec((1, width, tile), lambda i, place: (i ^ place[2], 0, 0)),
                pl.BlockSpec((1, tile, width), lambda i, place: (i ^ place[2], 0, 0)),
                pl.BlockSpec((half, tile), lambda i, place: (0, i)),
                rows,
                rows,
                whole_block((1, width)),
                whole_block(proj.shape),
                whole_block(proj.shape),
            ],
            out_specs=(
                pl.BlockSpec((1, tile), lambda i, place: (0, i)),
                pl.BlockSpec(split + (tile,), lambda i, place: (0, 0, i)),
                pl.BlockSpec(split + (tile,), lambda i, place: (0, 0, i)),
                rows,
                rows,
                whole_block((3, width)),
                heads,
                heads,
            ),
            scratch_shapes=[pltpu.VMEM((width, tile), f32), pltpu.VMEM((half, width), f32)],
        ),
        out_shape=(
            jax.ShapeDtypeStruct((1, hidden), f32),
            jax.ShapeDtypeStruct(split + (hidden,), bf16),
            jax.ShapeDtypeStruct(split + (hidden,), bf16),
            jax.ShapeDtypeStruct((half, width), f32),
            jax.ShapeDtypeStruct((half, width), bf16),
            jax.ShapeDtypeStruct((3, width), f32),
            jax.ShapeDtypeStruct((proj.shape[0], half), bf16),
            jax.ShapeDtypeStruct((proj.shape[0], half), bf16),
        ),
        compiler_params=params(),
        cost_estimate=pl.CostEstimate(
            flops=8 * half * width * hidden, bytes_accessed=24_000_000, transcendentals=0
        ),
        name="feed_back_second",
    )(place, normed, cot, up, down, slope, first, residual, gain[None, :], proj, proj_other)


def input_back_kernel(
    mine_ref,
    other_ref,
    w_ref,
    w_other_ref,
    gain_ref,
    x_hbm,
    grad_hbm,
    sum_ref,
    out_hbm,
    total,
    x_scr,
    grad_scr,
    out_scr,
    load_sem,
    store_sem,
    send_sem,
    recv_sem,
):
    step = pl.program_id(0)
    half = total.shape[0]
    side = lax.axis_index("tensor")
    peer = {"tensor": 1 - side}
    quarter = lax.axis_index("dp") % QUARTERS
    mine = pl.ds(pl.multiple_of(side * half, 16), half)
    loads = [
        pltpu.make_async_copy(x_hbm.at[mine], x_scr, load_sem.at[0]),
        pltpu.make_async_copy(grad_hbm, grad_scr, load_sem.at[1]),
    ]

    @pl.when(step == 0)
    def _():
        for load in loads:
            load.start()
        greet([peer])

    heads = other_ref.shape[0]
    left = other_ref[...].reshape(heads * HEAD_DIM, half)
    weight = jnp.concatenate([w_other_ref[i ^ quarter, 0] for i in range(QUARTERS)], axis=1)
    term = dot(mine_ref[0], w_ref[0], 0, 1) + dot(left, weight, 0, 1)
    accumulate(step, total, term)

    @pl.when(step == pl.num_programs(0) - 1)
    def _():
        for load in loads:
            load.wait()
        gain = gain_ref[...]
        sums = [0.0, 0.0]
        copies = []
        begin = 0
        for block, rows in enumerate((half // 32 * 16, half - half // 32 * 16)):
            at = pl.ds(begin, rows)
            unit, scale = norm_parts(x_scr[at].astype(f32))
            normed_grad = total[at]
            out = grad_scr[at] + norm_back(normed_grad, unit, scale, gain)
            out_scr[at] = out.astype(bf16)
            sums = [sums[0] + column_sum(normed_grad * unit), sums[1] + column_sum(normed_grad)]
            target = out_hbm.at[pl.ds(pl.multiple_of(side * half + begin, 16), rows)]
            copies.append(
                (
                    remote(
                        out_scr.at[at], target, send_sem.at[block], recv_sem.at[block], peer
                    ),
                    pltpu.make_async_copy(out_scr.at[at], target, store_sem.at[block]),
                )
            )
            for copy in copies[-1]:
                copy.start()
            begin += rows
        sum_ref[0:1] = sums[0]
        sum_ref[1:2] = sums[1]
        for far, near in copies:
            near.wait()
            far.wait()


def input_backward(mine, other, weight, weight_other, patches, gain, residual_grad):
    tokens, width = patches.shape
    half = tokens // 2
    columns = mine.shape[1]
    heads = other.shape[0]
    hbm = pl.BlockSpec(memory_space=pl.ANY)
    return pl.pallas_call(
        input_back_kernel,
        grid=(3,),
        in_specs=[
            pl.BlockSpec((1, columns, half), lambda i: (i, 0, 0)),
            pl.BlockSpec((heads, None, HEAD_DIM, half), lambda i: (0, i, 0, 0)),
            pl.BlockSpec((1, width, columns), lambda i: (i, 0, 0)),
            pl.BlockSpec((QUARTERS, 1, width, columns // QUARTERS), lambda i: (0, i, 0, 0)),
            whole_block((1, width)),
            hbm,
            hbm,
        ],
        out_specs=(whole_block((2, width)), hbm),
        out_shape=(
            jax.ShapeDtypeStruct((2, width), f32),
            jax.ShapeDtypeStruct((tokens, width), bf16),
        ),
        scratch_shapes=[
            pltpu.VMEM((half, width), f32),
            pltpu.VMEM((half, width), bf16),
            pltpu.VMEM((half, width), f32),
            pltpu.VMEM((half, width), bf16),
            pltpu.SemaphoreType.DMA((2,)),
            pltpu.SemaphoreType.DMA((2,)),
            pltpu.SemaphoreType.DMA((2,)),
            pltpu.SemaphoreType.DMA((2,)),
        ],
        compiler_params=params(1),
        cost_estimate=pl.CostEstimate(
            flops=12 * half * width * columns, bytes_accessed=20_000_000, transcendentals=0
        ),
        name="input_backward",
    )(mine, other, weight, weight_other, gain[None, :], patches, residual_grad)


def over_tensor(value):
    return lax.ppermute(value, "tensor", [(0, 1), (1, 0)])


def over_bit(value, bit, count):
    return lax.ppermute(value, "dp", [(i, i ^ (1 << bit)) for i in range(count)])


def other_half(piece, count):
    first = over_tensor(piece)
    second = over_bit(first, 1, count)
    return jnp.stack([first, over_bit(first, 0, count), second, over_bit(second, 0, count)])


def halve(keep, got, bit, place):
    groups, left, rows, columns = keep.shape
    mine = (place >> bit) & 1

    def side(index):
        pick = lambda x: lax.dynamic_index_in_dim(
            x.reshape(groups, left // 2, 2, rows, columns), index, 2, keepdims=False
        ).astype(f32)
        return (pick(keep) + pick(got)).astype(bf16)

    return side(mine), side(1 - mine)


class Halving:
    def __init__(self, keep, send, place, count):
        self.keep, self.send, self.place, self.count = keep, send, place, count
        self.bit = 0

    def step(self):
        got = over_bit(self.send, self.bit, self.count)
        self.bit += 1
        if 1 << self.bit == self.count:
            self.keep = self.keep.astype(f32) + got.astype(f32)
            self.send = None
        else:
            self.keep, self.send = halve(self.keep, got, self.bit, self.place)

    def finish(self):
        while self.send is not None:
            self.step()
        return self.keep[:, 0]


def all_sum(vector, count):
    for bit in range(count.bit_length() - 1):
        vector = vector + over_bit(vector, bit, count)
    return vector


def after(values, *halvings):
    state = [(h.keep, h.send) for h in halvings]
    values, state = lax.optimization_barrier((values, state))
    for h, (keep, send) in zip(halvings, state):
        h.keep, h.send = keep, send
    return values


def on_device(
    count,
    patches,
    cotangent,
    clip_lengths,
    attn_gain,
    attn_shift,
    qkv_weight,
    qkv_bias,
    proj_weight,
    proj_bias,
    mlp_gain,
    mlp_shift,
    up_weight,
    up_bias,
    down_weight,
    down_bias,
):
    tokens, width = patches.shape
    half = tokens // 2
    local_width = proj_weight.shape[0]
    hidden = up_weight.shape[1]
    side = lax.axis_index("tensor")
    index = lax.axis_index("dp")
    first_side = side == 0
    place = jnp.stack([side, index % 2, index % QUARTERS]).astype(jnp.int32)

    def pick(pair):
        mine = lax.dynamic_index_in_dim(pair, side, 0, keepdims=False)
        return mine, lax.dynamic_index_in_dim(pair, 1 - side, 0, keepdims=False)

    def both_rows(mine):
        theirs = over_tensor(mine)
        return jnp.concatenate(
            [jnp.where(first_side, mine, theirs), jnp.where(first_side, theirs, mine)], axis=0
        )

    def quarter(weight, axis):
        size = weight.shape[axis] // QUARTERS
        return lax.dynamic_slice_in_dim(weight, index % QUARTERS * size, size, axis)

    def in_order(quarters):
        return jnp.stack(
            [
                lax.dynamic_index_in_dim(quarters, i ^ (index % QUARTERS), 0, keepdims=False)
                for i in range(QUARTERS)
            ]
        ).reshape(-1, quarters.shape[2])

    qkv_parts = jnp.transpose(qkv_weight, (1, 0, 2))
    proj_other = in_order(other_half(quarter(proj_weight, 0), count))
    up_other = other_half(quarter(up_weight, 1), count)
    down_other = other_half(quarter(down_weight, 0), count)
    qkv_other = other_half(quarter(qkv_parts, 2), count)
    up_bias_other = over_tensor(up_bias)

    clip_len = clip_lengths[0, 0]
    cosine, sine = rotary_angles(jnp.arange(tokens, dtype=jnp.int32) % clip_len)
    query_mask, key_mask = clip_masks(clip_len, tokens)
    normed, qkv = qkv_forward(
        patches, attn_gain, attn_shift, qkv_parts, qkv_bias, cosine, sine
    )

    heads = local_width // HEAD_DIM
    weights, halves, attended, totals = attend_forward(qkv, query_mask, key_mask, 0, heads)
    keep, send = pick(halves)
    att_mine, att_other = [keep], [over_tensor(send)]

    residual, normed_two, slope_a, out_a, keep, send, down_bias_grad = feed_first(
        place,
        count,
        att_mine,
        att_other,
        proj_weight,
        proj_other,
        patches,
        proj_bias,
        mlp_gain,
        mlp_shift,
        cotangent,
        up_weight,
        up_bias,
        down_weight,
    )
    sum_down_a = Halving(keep[None], send[None], index, count)
    slope_b, block_rows, keep, send = feed_second(
        place,
        count,
        normed_two,
        cotangent,
        up_other,
        up_bias_other,
        down_other,
        residual,
        out_a,
        down_bias,
    )
    sum_down_b = Halving(keep[None], send[None], index, count)
    block_out = both_rows(block_rows)

    sum_down_a.step()
    slope_a = after(slope_a, sum_down_a)
    normed_grad_a, bias_grad_a, keep, send = feed_back_first(
        place, count, normed_two, cotangent, up_weight, down_weight, slope_a
    )
    sum_up_a = Halving(keep[None], send[None], index, count)
    sum_down_b.step()
    slope_b = after(slope_b, sum_down_b)
    (
        bias_grad_b,
        keep,
        send,
        residual_grad,
        branch_low,
        vectors,
        att_grad_mine,
        att_grad_send,
    ) = feed_back_second(
        place,
        count,
        normed_two,
        cotangent,
        up_other,
        down_other,
        slope_b,
        normed_grad_a,
        residual,
        mlp_gain,
        proj_weight,
        proj_other,
    )
    sum_up_b = Halving(keep[None], send[None], index, count)
    att_grad_got = over_tensor(att_grad_send)

    early = jnp.concatenate([vectors.reshape(-1), down_bias_grad[0]])
    got = over_tensor(jnp.concatenate([early, bias_grad_b[0]]))
    early = jnp.concatenate([early + got[: 4 * width], bias_grad_a[0] + got[4 * width :]])
    sum_down_a.step()
    sum_up_a.step()
    att_rows = [jnp.concatenate(x, axis=0) for x in (att_mine, att_other)]
    proj_grad = jnp.stack([dot(branch_low, x, 0, 1).astype(bf16) for x in att_rows])
    split = proj_grad.reshape(2, count // 2, 2, width // count, local_width)
    sum_proj = Halving(
        lax.dynamic_index_in_dim(split, index % 2, 2, keepdims=False),
        lax.dynamic_index_in_dim(split, 1 - index % 2, 2, keepdims=False),
        index,
        count,
    )
    att_grad_mine = after(att_grad_mine, sum_down_a, sum_up_a, sum_proj)
    left = jnp.where(first_side, att_grad_mine, att_grad_got)
    right = jnp.where(first_side, att_grad_got, att_grad_mine)
    sum_up_b.step()
    sum_proj.step()
    left = after(left, sum_up_b, sum_proj)

    mixed_mine, keep, send, qkv_bias_grad, mixed_other = attend_backward(
        count, weights, qkv, attended, totals, left, right, cosine, sine, normed
    )
    sum_qkv = Halving(keep, send, index, count)
    last_vectors, patch_grad = input_backward(
        mixed_mine, mixed_other, qkv_parts, qkv_other, patches, attn_gain, residual_grad
    )

    def with_other_side(pair):
        return pair[0] + over_tensor(pair[1].astype(bf16)).astype(f32)

    down_sum = with_other_side([sum_down_a.finish()[0], sum_down_b.finish()[0]])
    up_sum = with_other_side([sum_up_a.finish()[0], sum_up_b.finish()[0]])
    proj_sum = with_other_side(sum_proj.finish())
    qkv_sum = sum_qkv.finish()

    early = all_sum(early, count)
    late = last_vectors.reshape(-1)
    late = late + over_tensor(late)
    late = all_sum(jnp.concatenate([late, qkv_bias_grad.reshape(-1)]), count)
    return (
        block_out,
        patch_grad,
        late[:width],
        late[width : 2 * width],
        jnp.transpose(qkv_sum, (1, 0, 2)),
        late[2 * width :].reshape(3, local_width),
        proj_sum.T,
        early[2 * width : 3 * width],
        early[:width],
        early[width : 2 * width],
        up_sum,
        early[4 * width :],
        down_sum.T,
        early[3 * width : 4 * width],
    )


def solution(mesh):
    return jax.shard_map(
        functools.partial(on_device, mesh.shape["dp"]),
        mesh=mesh,
        in_specs=(
            P("dp", None),
            P("dp", None),
            P("dp", None),
            P(),
            P(),
            P(None, None, "tensor"),
            P(None, "tensor"),
            P("tensor", None),
            P(),
            P(),
            P(),
            P(None, "tensor"),
            P("tensor"),
            P("tensor", None),
            P(),
        ),
        out_specs=(
            P("dp", None),
            P("dp", None),
            P(),
            P(),
            P("dp", None, "tensor"),
            P(None, "tensor"),
            P("tensor", "dp"),
            P(),
            P(),
            P(),
            P("dp", "tensor"),
            P("tensor"),
            P("tensor", "dp"),
            P(),
        ),
        check_vma=False,
    )
```

```python
import functools
import math

import jax
import jax.numpy as jnp
from jax import lax
from jax.experimental import pallas as pl
from jax.experimental.pallas import tpu as pltpu
from jax.sharding import PartitionSpec as P

HEAD_DIM = 64
HALF_DIM = HEAD_DIM // 2
GRID = 14
IMG = 196
EPS = 1e-06
SCALING = HEAD_DIM ** (-0.5)
LOG2E = math.log2(math.e)
KEY_CHUNKS = 2
MASK_ROWS = 16
ONES_ROWS = 16
FF_TILE = 512
FORBIDDEN = -1e30
VMEM_LIMIT = 60 * 1024 * 1024

MESH = pl.DeviceIdType.MESH

bf16 = jnp.bfloat16
f32 = jnp.float32


def dot(left, right, left_dim, right_dim):
    return lax.dot_general(
        left, right, (((left_dim,), (right_dim,)), ((), ())), preferred_element_type=f32
    )


def rotary_angles(offsets):
    pair_count = HALF_DIM
    side_pairs = pair_count * 11 // 32
    time_pairs = pair_count - 2 * side_pairs
    pair_index = jnp.arange(pair_count, dtype=jnp.int32)
    time_pair = pair_index < time_pairs
    height_pair = (pair_index >= time_pairs) & (pair_index < time_pairs + side_pairs)
    group_begin = jnp.where(
        time_pair, 0, jnp.where(height_pair, time_pairs, time_pairs + side_pairs)
    )
    group_size = jnp.where(time_pair, time_pairs, side_pairs)
    inverse = jnp.power(
        10000.0, -(pair_index - group_begin).astype(f32) / group_size.astype(f32)
    )
    frame_place = (offsets // IMG).astype(f32)
    row_place = (offsets % IMG // GRID).astype(f32)
    column_place = (offsets % GRID).astype(f32)
    position = jnp.where(
        time_pair[:, None],
        frame_place[None, :],
        jnp.where(height_pair[:, None], row_place[None, :], column_place[None, :]),
    )
    angles = position * inverse[:, None]
    return (jnp.cos(angles), jnp.sin(angles))


def params(collective_id=None):
    if collective_id is None:
        return pltpu.CompilerParams(vmem_limit_bytes=VMEM_LIMIT)
    return pltpu.CompilerParams(
        vmem_limit_bytes=VMEM_LIMIT, collective_id=collective_id, has_side_effects=True
    )


def greet(partners):
    barrier = pltpu.get_barrier_semaphore()
    for partner in partners:
        pl.semaphore_signal(barrier, inc=1, device_id=partner, device_id_type=MESH)
    pl.semaphore_wait(barrier, len(partners))


def partner_of(bit):
    index = lax.axis_index("dp")
    mine = (index // (1 << bit)) % 2
    return {"dp": index + (1 << bit) * (1 - 2 * mine)}, mine


def fold(keep, got, mine, next_keep, next_send):
    lead = (slice(None),) * (len(keep.shape) - 3)
    for pair in range(keep.shape[-3] // 2):
        for ref, odd in ((next_keep, mine), (next_send, 1 - mine)):
            at = lead + (2 * pair + odd,)
            ref[lead + (pair,)] = (keep[at].astype(f32) + got[at].astype(f32)).astype(bf16)


def remote(source, target, send_sem, recv_sem, partner):
    return pltpu.make_async_remote_copy(
        src_ref=source,
        dst_ref=target,
        send_sem=send_sem,
        recv_sem=recv_sem,
        device_id=partner,
        device_id_type=MESH,
    )


def whole_block(shape, **kwargs):
    return pl.BlockSpec(shape, lambda *_: (0,) * len(shape), **kwargs)


def once(shape):
    return whole_block(shape, pipeline_mode=pl.Buffered(1))


HBM = pl.BlockSpec(memory_space=pl.ANY)


def clamp(value, last):
    return jnp.minimum(jnp.maximum(value, 0), last)


def norm_parts(values):
    centre = values - jnp.mean(values, axis=1, keepdims=True)
    spread = jnp.mean(centre * centre, axis=1, keepdims=True)
    scale = lax.rsqrt(spread + EPS)
    return centre * scale, scale


def norm_back(grad, unit, scale, gain):
    c = grad * gain
    mean = jnp.mean(c, axis=1, keepdims=True)
    along = jnp.mean(c * unit, axis=1, keepdims=True)
    return scale * (c - mean - unit * along)


def column_sum(values):
    return jnp.sum(values, axis=0, keepdims=True)


def clip_masks(clip_len, tokens):
    token = jnp.arange(tokens, dtype=jnp.int32)[None, :] // IMG
    row = jnp.arange(MASK_ROWS, dtype=jnp.int32)[:, None]
    same = token == row
    images = clip_len < tokens
    forbid = images & jnp.logical_not(same) & (row < tokens // IMG)
    return jnp.where(forbid, FORBIDDEN, 0.0).astype(bf16), same.astype(bf16)


class Gather:
    COPIES = 11
    STAGES = ((0,), (1, 2), (3, 4, 5, 6), (7, 8, 9, 10))

    def __init__(self, weight, other, send_sem, recv_sem):
        self.weight, self.other = weight, other
        self.send_sem, self.recv_sem = send_sem, recv_sem

    def copy(self, number):
        bits = [partner_of(bit)[1] for bit in range(3)]
        partners = [partner_of(bit)[0] for bit in range(3)]
        size = self.other.shape[-2] // 8

        def piece(ref, half, x=0, z=0):
            index = bits[0] + 2 * (bits[1] + x * (1 - 2 * bits[1]))
            index = index + 4 * (bits[2] + z * (1 - 2 * bits[2]))
            begin, rows = index * size, size
            if half is not None:
                rows = size // 2
                begin = begin + half * rows
            lead = (slice(None),) * (len(ref.shape) - 2)
            return ref.at[lead + (pl.ds(pl.multiple_of(begin, rows), rows),)]

        half, x, z, partner = (
            (None, 0, 0, {"tensor": 1 - lax.axis_index("tensor")}),
            (0, 0, 0, partners[2]),
            (1, 0, 0, partners[1]),
            (0, 0, 0, partners[1]),
            (0, 0, 1, partners[1]),
            (1, 0, 0, partners[2]),
            (1, 1, 0, partners[2]),
            (None, 0, 0, partners[0]),
            (None, 1, 0, partners[0]),
            (None, 0, 1, partners[0]),
            (None, 1, 1, partners[0]),
        )[number]
        source = self.weight if number == 0 else self.other
        return remote(
            piece(source, half, x, z),
            piece(self.other, half, x, z),
            self.send_sem.at[number],
            self.recv_sem.at[number],
            partner,
        )

    def start(self, stage):
        for number in self.STAGES[stage]:
            self.copy(number).start()

    def wait(self, stage):
        for number in self.STAGES[stage]:
            self.copy(number).wait()

    def advance(self, stage):
        self.wait(stage - 1)
        self.start(stage)


def neighbours():
    return [{"tensor": 1 - lax.axis_index("tensor")}] + [partner_of(bit)[0] for bit in range(3)]


def attend_kernel(
    x_ref,
    gain_ref,
    shift_ref,
    w_ref,
    b_ref,
    cos_ref,
    sin_ref,
    qm_ref,
    km_ref,
    proj_hbm,
    up_hbm,
    down_hbm,
    normed_ref,
    qkv_ref,
    att_ref,
    mine_ref,
    factor_ref,
    e_hbm,
    other_hbm,
    proj_other,
    up_other,
    down_other,
    k_scr,
    s_scr,
    e_scr,
    outgoing,
    e_sem,
    send_sem,
    recv_sem,
    gather_send,
    gather_recv,
):
    step, last = pl.program_id(0), pl.num_programs(0) - 1
    tokens, width = x_ref.shape
    half = tokens // 2
    chunk = tokens // KEY_CHUNKS
    heads = e_hbm.shape[0]
    side = lax.axis_index("tensor")
    peer = {"tensor": 1 - side}
    proj, up, down = (
        Gather(weight, other, gather_send.at[number], gather_recv.at[number])
        for number, (weight, other) in enumerate(
            ((proj_hbm, proj_other), (up_hbm, up_other), (down_hbm, down_other))
        )
    )

    @pl.when(step == 0)
    def _():
        greet(neighbours())
        for weight in (proj, up, down):
            weight.start(0)
        unit, _ = norm_parts(x_ref[...].astype(f32))
        normed_ref[:width] = (unit * gain_ref[...] + shift_ref[...]).astype(bf16).T
        normed_ref[width:] = jnp.ones((ONES_ROWS, tokens), bf16)

    for at, weight, stage in (
        (1, proj, 1),
        (2, proj, 2),
        (4, proj, 3),
        (4, up, 1),
        (6, up, 2),
        (9, up, 3),
        (8, down, 1),
    ):

        @pl.when(step == at)
        def _():
            weight.advance(stage)

    @pl.when(step < 3)
    def _():
        rows = w_ref.shape[2]
        bias = jnp.broadcast_to(b_ref[pl.ds(step, 1), :], (8, rows)).T[:, :1]
        mixed = dot(w_ref[0], normed_ref[:width], 0, 0) + bias

        @pl.when(step < 2)
        def _():
            cosine, sine = cos_ref[...], sin_ref[...]
            for begin in range(0, rows, HEAD_DIM):
                middle, end = begin + HALF_DIM, begin + HEAD_DIM
                low, high = mixed[begin:middle], mixed[middle:end]
                qkv_ref[step, begin:middle, :] = (low * cosine - high * sine).astype(bf16)
                qkv_ref[step, middle:end, :] = (high * cosine + low * sine).astype(bf16)

        @pl.when(step == 2)
        def _():
            qkv_ref[step] = mixed.astype(bf16)

    head = step - 3
    slot = head % 2

    def store(index, part):
        at = pl.ds(part * chunk, chunk)
        return pltpu.make_async_copy(
            e_scr.at[index % 2, at], e_hbm.at[index, at], e_sem.at[index % 2, part]
        )

    def exchange(index):
        at = pl.ds(pl.multiple_of(index * HEAD_DIM, HEAD_DIM), HEAD_DIM)
        return remote(
            outgoing.at[index % 2],
            other_hbm.at[at],
            send_sem.at[index % 2],
            recv_sem.at[index],
            peer,
        )

    @pl.when(head >= 2)
    def _():
        for part in range(KEY_CHUNKS):
            store(head - 2, part).wait()
        exchange(head - 2).wait_send()

    @pl.when(head >= 0)
    def _():
        at = pl.ds(pl.multiple_of(clamp(head, heads - 1) * HEAD_DIM, HEAD_DIM), HEAD_DIM)
        queries = jnp.concatenate([qkv_ref[0, at], qm_ref[...]], axis=0)
        k_scr[...] = jnp.concatenate([qkv_ref[1, at], km_ref[...]], axis=0).T
        values = jnp.concatenate([qkv_ref[2, at], jnp.ones((16, tokens), bf16)], axis=0)
        top, out, tops = None, None, []
        s_scr[0] = dot(k_scr[:chunk], queries, 1, 0)
        for part in range(KEY_CHUNKS):
            begin, end = part * chunk, (part + 1) * chunk
            if part + 1 < KEY_CHUNKS:
                s_scr[(part + 1) % 2] = dot(k_scr[end : end + chunk], queries, 1, 0)
            scores = s_scr[part % 2]
            here = jnp.max(scores, axis=0, keepdims=True)
            new_top = here if top is None else jnp.maximum(top, here)
            weights = jnp.exp2((scores - new_top) * (SCALING * LOG2E)).astype(bf16)
            e_scr[slot, begin:end] = weights
            store(head, part).start()
            term = dot(values[:, begin:end], weights, 1, 0)
            if out is None:
                out = term
            else:
                out = out * jnp.exp2((top - new_top) * (SCALING * LOG2E)) + term
            top = new_top
            tops.append(top)
        scale = 1.0 / out[HEAD_DIM : HEAD_DIM + 1]
        for part in range(KEY_CHUNKS):
            factor_ref[0, part : part + 1] = scale * jnp.exp2(
                (tops[part] - top) * (SCALING * LOG2E)
            )
        attended = out[:HEAD_DIM] * scale
        att_ref[...] = attended.astype(bf16)
        left, right = attended[:, :half], attended[:, half:]
        mine_ref[...] = jnp.where(side == 0, left, right).astype(bf16)
        outgoing[slot] = jnp.where(side == 0, right, left).astype(bf16)
        exchange(head).start()

    @pl.when(step == last)
    def _():
        for back in (2, 1):
            for part in range(KEY_CHUNKS):
                store(heads - back, part).wait()
            exchange(heads - back).wait_send()
        for index in range(heads):
            exchange(index).wait_recv()
        for weight, stage in ((proj, 3), (up, 3), (down, 1)):
            weight.wait(stage)


def attend_forward(
    patches, gain, shift, weight, bias, cosine, sine, query_mask, key_mask, proj, up, down
):
    tokens, width = patches.shape
    columns = weight.shape[2]
    heads = columns // HEAD_DIM
    half = tokens // 2
    head = lambda i: clamp(i - 3, heads - 1)
    vmem = pltpu.VMEM
    dma = lambda *shape: pltpu.SemaphoreType.DMA(shape)
    return pl.pallas_call(
        attend_kernel,
        grid=(3 + heads,),
        out_shape=(
            jax.ShapeDtypeStruct((width + ONES_ROWS, tokens), bf16),
            jax.ShapeDtypeStruct((3, columns, tokens), bf16),
            jax.ShapeDtypeStruct((columns, tokens), bf16),
            jax.ShapeDtypeStruct((columns, half), bf16),
            jax.ShapeDtypeStruct((heads, KEY_CHUNKS, tokens), f32),
            jax.ShapeDtypeStruct((heads, tokens, tokens), bf16),
            jax.ShapeDtypeStruct((columns, half), bf16),
            jax.ShapeDtypeStruct(proj.shape, bf16),
            jax.ShapeDtypeStruct(up.shape, bf16),
            jax.ShapeDtypeStruct(down.shape, bf16),
        ),
        in_specs=[
            once((tokens, width)),
            once((1, width)),
            once((1, width)),
            pl.BlockSpec((1, width, columns), lambda i: (clamp(i, 2), 0, 0)),
            once((3, columns)),
            once(cosine.shape),
            once(sine.shape),
            once(query_mask.shape),
            once(key_mask.shape),
            HBM,
            HBM,
            HBM,
        ],
        out_specs=(
            once((width + ONES_ROWS, tokens)),
            once((3, columns, tokens)),
            pl.BlockSpec((HEAD_DIM, tokens), lambda i: (head(i), 0)),
            pl.BlockSpec((HEAD_DIM, half), lambda i: (head(i), 0)),
            pl.BlockSpec((1, KEY_CHUNKS, tokens), lambda i: (head(i), 0, 0)),
            HBM,
            HBM,
            HBM,
            HBM,
            HBM,
        ),
        scratch_shapes=[
            vmem((tokens, HEAD_DIM + MASK_ROWS), bf16),
            vmem((2, tokens // KEY_CHUNKS, tokens), f32),
            vmem((2, tokens, tokens), bf16),
            vmem((2, HEAD_DIM, half), bf16),
            dma(2, KEY_CHUNKS),
            dma(2),
            dma(heads),
            dma(3, Gather.COPIES),
            dma(3, Gather.COPIES),
        ],
        compiler_params=params(3),
        cost_estimate=pl.CostEstimate(
            flops=6 * tokens * width * columns + 16 * heads * tokens * tokens * HEAD_DIM,
            bytes_accessed=60_000_000,
            transcendentals=heads * tokens * tokens,
        ),
        name="attend_forward",
    )(
        patches,
        gain[None, :],
        shift[None, :],
        weight,
        bias,
        cosine,
        sine,
        query_mask,
        key_mask,
        proj,
        up,
        down,
    )


def attend_back_kernel(
    e_ref,
    q_ref,
    k_ref,
    v_ref,
    out_ref,
    total_ref,
    left_ref,
    right_ref,
    cos_ref,
    sin_ref,
    normed_ref,
    down_keep_ref,
    down_got_ref,
    up_keep_ref,
    up_got_ref,
    proj_keep_ref,
    proj_got_ref,
    mine_ref,
    keep_ref,
    sum_ref,
    down_next_ref,
    up_next_ref,
    proj_next_ref,
    other_ref,
    got_ref,
    down_next_got,
    up_next_got,
    up_scr,
    up_low,
    value_scr,
    v_scr,
    score_grad,
    turned,
    pair_scr,
    outgoing,
    grad,
    outgoing_core,
    outgoing_down,
    outgoing_up,
    outgoing_proj,
    send_sem,
    recv_sem,
    core_send,
    core_recv,
    down_send,
    down_recv,
    up_send,
    up_recv,
    proj_send,
):
    head, heads = pl.program_id(0), pl.num_programs(0)
    tokens = q_ref.shape[2]
    half = tokens // 2
    side = lax.axis_index("tensor")
    peer = {"tensor": 1 - side}
    core_partner, core = partner_of(0)
    x_partner, x_side = partner_of(1)
    z_partner, z_side = partner_of(2)
    slot = head % 2
    items = up_next_got.shape[0]

    def exchange(index):
        return remote(
            outgoing.at[index % 2],
            other_ref.at[index],
            send_sem.at[index % 2],
            recv_sem.at[index],
            peer,
        )

    def to_core(pair):
        at = pl.ds(pl.multiple_of(pair * 2 * HEAD_DIM, 2 * HEAD_DIM), 2 * HEAD_DIM)
        return remote(
            outgoing_core.at[pair % 2],
            got_ref.at[:, :, :, at],
            core_send.at[pair % 2],
            core_recv.at[pair],
            core_partner,
        )

    def to_z(index):
        return remote(
            outgoing_down.at[index % 2],
            down_next_got.at[index],
            down_send.at[index % 2],
            down_recv.at[index],
            z_partner,
        )

    def to_x(index):
        return remote(
            outgoing_up.at[index % 2],
            up_next_got.at[index],
            up_send.at[index % 2],
            up_recv.at[index],
            x_partner,
        )

    def proj_to_x(index):
        return remote(
            outgoing_proj.at[index],
            up_next_got.at[index + heads],
            proj_send.at[index],
            up_recv.at[index + heads],
            x_partner,
        )

    @pl.when(head == 0)
    def _():
        greet([peer, core_partner, x_partner, z_partner])

    @pl.when(head >= 2)
    def _():
        exchange(head - 2).wait_send()
        to_z(head - 2).wait_send()
        to_x(head - 2).wait_send()

    fold(down_keep_ref.at[0], down_got_ref.at[0], z_side, down_next_ref.at[0], outgoing_down.at[slot])
    to_z(head).start()
    fold(up_keep_ref.at[0], up_got_ref.at[0], x_side, up_next_ref.at[0], outgoing_up.at[slot])
    to_x(head).start()

    @pl.when(head < 2)
    def _():
        fold(
            proj_keep_ref.at[0],
            proj_got_ref.at[0],
            x_side,
            proj_next_ref.at[0],
            outgoing_proj.at[head],
        )
        proj_to_x(head).start()

    chunks = total_ref.shape[1]
    chunk = tokens // chunks
    up_scr[:, :half] = left_ref[...].astype(f32)
    up_scr[:, half:] = right_ref[...].astype(f32)
    attended = out_ref[...].astype(f32)
    centre = []
    for part in range(chunks):
        up_low[part] = (up_scr[...] * total_ref[0, part : part + 1]).astype(bf16)
        centre.append(column_sum(up_low[part].astype(f32) * attended))
    v_scr[...] = v_ref[0].T
    cosine, sine = cos_ref[...], sin_ref[...]

    def store(part, low, high):
        for row, value in ((0, low), (HALF_DIM, high)):
            left, right = value[:, :half], value[:, half:]
            mine_ref[part, row : row + HALF_DIM] = jnp.where(side == 0, left, right).astype(bf16)
            outgoing[slot, part, row : row + HALF_DIM] = jnp.where(side == 0, right, left).astype(
                bf16
            )
            begin = pl.multiple_of(part * 2 * HEAD_DIM + slot * HEAD_DIM + row, HALF_DIM)
            pair_scr[pl.ds(begin, HALF_DIM)] = value.astype(bf16)

    def unrotated(part, grad):
        low, high = grad[:HALF_DIM] * SCALING, grad[HALF_DIM:] * SCALING
        store(part, low * cosine + high * sine, high * cosine - low * sine)

    for part in range(chunks):
        at = slice(part * chunk, (part + 1) * chunk)
        value_scr[:, at] = dot(up_low[part], e_ref[0, at], 1, 1)
        prob_grad = dot(v_scr[at], up_low[part], 1, 0)
        score_grad[at] = (e_ref[0, at].astype(f32) * (prob_grad - centre[part])).astype(bf16)
    store(2, value_scr[:HALF_DIM], value_scr[HALF_DIM:])
    unrotated(0, dot(k_ref[0], score_grad[...], 1, 0))
    turned[...] = score_grad[...].T
    unrotated(1, dot(q_ref[0], turned[...], 1, 0))
    exchange(head).start()

    @pl.when(slot == 1)
    def _():
        pair = head // 2
        width = grad.shape[0] - ONES_ROWS
        grad[...] = dot(normed_ref[...], pair_scr[...], 1, 1)

        @pl.when(pair >= 2)
        def _():
            to_core(pair - 2).wait_send()

        for part in range(3):
            lanes = pl.ds(part * 2 * HEAD_DIM, 2 * HEAD_DIM)
            split_rows(
                grad.at[:, lanes], keep_ref.at[part], outgoing_core.at[pair % 2, part], core
            )
            sum_ref[part : part + 1] = grad[width : width + 1, lanes]
        to_core(pair).start()

    @pl.when(head == heads - 1)
    def _():
        for back in (2, 1):
            exchange(heads - back).wait_send()
            to_z(heads - back).wait_send()
            to_x(heads - back).wait_send()
            to_core(heads // 2 - back).wait_send()
            proj_to_x(2 - back).wait_send()
        for index in range(other_ref.shape[0]):
            exchange(index).wait_recv()
            to_z(index).wait_recv()
        for index in range(items):
            to_x(index).wait_recv()
        for index in range(other_ref.shape[0] // 2):
            to_core(index).wait_recv()


def attend_backward(
    count,
    weights,
    qkv,
    attended,
    totals,
    left,
    right,
    cosine,
    sine,
    normed,
    down_keep,
    down_got,
    up_keep,
    up_got,
):
    tokens = qkv.shape[2]
    half = tokens // 2
    heads = weights.shape[0]
    columns = heads * HEAD_DIM
    width = normed.shape[0] - ONES_ROWS
    rows = width // count
    split = (3, count // 2, rows)
    left_x, left_z = (count // 4, rows, FF_TILE), (count // 8, rows, FF_TILE)
    block = lambda part: pl.BlockSpec((1, HEAD_DIM, tokens), lambda i: (part, i, 0))
    half_block = pl.BlockSpec((HEAD_DIM, half), lambda i: (i, 0))
    pair_block = pl.BlockSpec(split + (2 * HEAD_DIM,), lambda i: (0, 0, 0, i // 2))
    tile = lambda lead, first=0, last=heads - 1: pl.BlockSpec(
        (1,) + lead, lambda i: (first + clamp(i, last), 0, 0, 0)
    )
    core_left = (count // 2, rows, FF_TILE)
    vmem = pltpu.VMEM
    dma = lambda size: pltpu.SemaphoreType.DMA((size,))
    return pl.pallas_call(
        attend_back_kernel,
        grid=(heads,),
        out_shape=(
            jax.ShapeDtypeStruct((3, columns, half), bf16),
            jax.ShapeDtypeStruct(split + (columns,), bf16),
            jax.ShapeDtypeStruct((3, columns), f32),
            jax.ShapeDtypeStruct((heads,) + left_z, bf16),
            jax.ShapeDtypeStruct((heads,) + left_x, bf16),
            jax.ShapeDtypeStruct((2,) + left_x, bf16),
            jax.ShapeDtypeStruct((heads, 3, HEAD_DIM, half), bf16),
            jax.ShapeDtypeStruct(split + (columns,), bf16),
            jax.ShapeDtypeStruct((heads,) + left_z, bf16),
            jax.ShapeDtypeStruct((heads + 2,) + left_x, bf16),
        ),
        in_specs=[
            pl.BlockSpec((1, tokens, tokens), lambda i: (i, 0, 0)),
            block(0),
            block(1),
            block(2),
            pl.BlockSpec((HEAD_DIM, tokens), lambda i: (i, 0)),
            pl.BlockSpec((1, totals.shape[1], tokens), lambda i: (i, 0, 0)),
            half_block,
            half_block,
            once(cosine.shape),
            once(sine.shape),
            once(normed.shape),
            tile(left_x),
            tile(left_x),
            tile(core_left),
            tile(core_left, heads),
            tile(core_left, heads, 1),
            tile(core_left, 2 * heads, 1),
        ],
        out_specs=(
            pl.BlockSpec((3, HEAD_DIM, half), lambda i: (0, i, 0)),
            pair_block,
            pl.BlockSpec((3, 2 * HEAD_DIM), lambda i: (0, i // 2)),
            tile(left_z),
            tile(left_x),
            tile(left_x, 0, 1),
            HBM,
            HBM,
            HBM,
            HBM,
        ),
        scratch_shapes=[
            vmem((HEAD_DIM, tokens), f32),
            vmem((totals.shape[1], HEAD_DIM, tokens), bf16),
            vmem((HEAD_DIM, tokens), f32),
            vmem((tokens, HEAD_DIM), bf16),
            vmem((tokens, tokens), bf16),
            vmem((tokens, tokens), bf16),
            vmem((6 * HEAD_DIM, tokens), bf16),
            vmem((2, 3, HEAD_DIM, half), bf16),
            vmem((width + ONES_ROWS, 6 * HEAD_DIM), f32),
            vmem((2,) + split + (2 * HEAD_DIM,), bf16),
            vmem((2,) + left_z, bf16),
            vmem((2,) + left_x, bf16),
            vmem((2,) + left_x, bf16),
            dma(2),
            dma(heads),
            dma(2),
            dma(heads // 2),
            dma(2),
            dma(heads),
            dma(2),
            dma(heads + 2),
            dma(2),
        ],
        compiler_params=params(0),
        cost_estimate=pl.CostEstimate(
            flops=32 * heads * tokens * tokens * HEAD_DIM,
            bytes_accessed=2 * heads * tokens * tokens,
            transcendentals=0,
        ),
        name="attend_backward",
    )(
        weights,
        qkv,
        qkv,
        qkv,
        attended,
        totals,
        left,
        right,
        cosine,
        sine,
        normed,
        down_keep,
        down_got,
        up_keep,
        up_got,
        up_keep,
        up_got,
    )


def normal_parts(value):
    a = jnp.abs(value)
    t = 1.0 / (1.0 + (0.3275911 / math.sqrt(2.0)) * a)
    bell = jnp.exp2(value * value * (-0.5 * LOG2E))
    c = [0.5 * x for x in (0.254829592, -0.284496736, 1.421413741, -1.453152027, 1.061405429)]
    tail = ((((c[4] * t + c[3]) * t + c[2]) * t + c[1]) * t + c[0]) * t * bell
    return jnp.where(value >= 0, 1.0 - tail, tail), bell * (1.0 / math.sqrt(2.0 * math.pi))


def split_rows(grad, keep_ref, send_ref, core):
    count, rows = keep_ref.shape[:2]
    for pair in range(count):
        for ref, odd in ((keep_ref, core), (send_ref, 1 - core)):
            begin = pl.multiple_of((2 * pair + odd) * rows, rows)
            ref[pair] = grad[pl.ds(begin, rows), :].astype(bf16)


def accumulate(step, total, term):
    @pl.when(step == 0)
    def _():
        total[...] = term

    @pl.when(step > 0)
    def _():
        total[...] += term


def feed_kernel(
    att_ref,
    att_other_ref,
    proj_ref,
    proj_other_ref,
    proj_bias_ref,
    gain_ref,
    shift_ref,
    down_bias_ref,
    up_bias_ref,
    patch_hbm,
    cot_hbm,
    up_hbm,
    up_other_hbm,
    down_hbm,
    down_part_hbm,
    qkv_hbm,
    grad_ref,
    att_grad_ref,
    vector_ref,
    up_bias_grad_ref,
    keep_x_ref,
    keep_ref,
    out_hbm,
    att_got_hbm,
    got_hbm,
    got_x_hbm,
    down_other_hbm,
    qkv_other_hbm,
    n_scr,
    cot_scr,
    out_scr,
    total,
    act_scr,
    slope_scr,
    up_scr,
    down_scr,
    low_scr,
    att_scr,
    grad_scr,
    keep_ring,
    outgoing,
    arrived,
    outgoing_x,
    load_sem,
    up_sem,
    down_sem,
    store_sem,
    row_sem,
    att_sem,
    send_sem,
    recv_sem,
    arrive_sem,
    send_x_sem,
    recv_x_sem,
    gather_send,
    gather_recv,
):
    step, last = pl.program_id(0), pl.num_programs(0) - 1
    tiles = act_scr.shape[0]
    half_tiles = tiles // 2
    half = n_scr.shape[0]
    side = lax.axis_index("tensor")
    peer = {"tensor": 1 - side}
    core_partner, core = partner_of(0)
    x_partner, x_side = partner_of(1)
    mine = pl.ds(pl.multiple_of(side * half, 16), half)
    gather_down = Gather(down_hbm, down_other_hbm, gather_send.at[0], gather_recv.at[0])
    gather_qkv = Gather(qkv_hbm, qkv_other_hbm, gather_send.at[1], gather_recv.at[1])
    patch_load = pltpu.make_async_copy(patch_hbm.at[mine], out_scr, load_sem.at[0])
    cot_load = pltpu.make_async_copy(cot_hbm.at[mine], cot_scr, load_sem.at[1])
    out_near = pltpu.make_async_copy(out_scr, out_hbm.at[mine], store_sem)
    out_far = remote(out_scr, out_hbm.at[mine], row_sem.at[0], row_sem.at[1], peer)
    att_far = remote(att_scr, att_got_hbm, att_sem.at[0], att_sem.at[1], peer)

    def weights(index, act):
        tile, slot = index % tiles, index % 2

        def both(up, down, at):
            at = pl.ds(pl.multiple_of(at * FF_TILE, FF_TILE), FF_TILE)
            for copy in (
                pltpu.make_async_copy(up.at[:, at], up_scr.at[slot], up_sem.at[slot]),
                pltpu.make_async_copy(down.at[at], down_scr.at[slot], down_sem.at[slot]),
            ):
                getattr(copy, act)()

        @pl.when(tile < half_tiles)
        def _():
            both(up_hbm, down_hbm, tile)

        @pl.when(tile >= half_tiles)
        def _():
            both(up_other_hbm, down_other_hbm, tile - half_tiles)

    def to_core(index):
        return remote(
            outgoing.at[index % 2],
            got_hbm.at[index],
            send_sem.at[index % 2],
            recv_sem.at[index],
            core_partner,
        )

    def to_x(index):
        return remote(
            outgoing_x.at[index % 2],
            got_x_hbm.at[index],
            send_x_sem.at[index % 2],
            recv_x_sem.at[index],
            x_partner,
        )

    def arrive(index):
        return pltpu.make_async_copy(
            got_hbm.at[index], arrived.at[index % 2], arrive_sem.at[index % 2]
        )

    @pl.when(step == 0)
    def _():
        patch_load.start()
        cot_load.start()
        weights(0, "start")
        greet(neighbours())
        gather_down.start(2)
        gather_qkv.start(0)
        branch = dot(att_ref[...], proj_ref[...], 0, 0).astype(bf16).astype(f32)
        other = dot(att_other_ref[...], proj_other_ref[...], 0, 0).astype(bf16).astype(f32)
        patch_load.wait()
        residual = out_scr[...].astype(f32) + (branch + other + proj_bias_ref[...])
        grad_ref[...] = residual
        unit, _ = norm_parts(residual)
        n_scr[...] = (unit * gain_ref[...] + shift_ref[...]).astype(bf16)
        cot_load.wait()
        vector_ref[3:4] = column_sum(cot_scr[...].astype(f32))

    slot = step % 2

    @pl.when(step == half_tiles - 1)
    def _():
        gather_down.wait(3)

    for at, weight, stage in (
        (half_tiles - 2, gather_down, 3),
        (half_tiles, gather_qkv, 1),
        (half_tiles + 2, gather_qkv, 2),
        (half_tiles + 6, gather_qkv, 3),
    ):

        @pl.when(step == at)
        def _():
            weight.advance(stage)

    @pl.when(step < 2 * tiles - 1)
    def _():
        weights(step + 1, "start")

    @pl.when(step < 2 * tiles)
    def _():
        weights(step, "wait")

    @pl.when(step < tiles)
    def _():
        upward = dot(n_scr[...], up_scr[slot], 1, 0) + up_bias_ref[step]
        share, density = normal_parts(upward)
        activated = (upward * share).astype(bf16)
        act_scr[step] = activated
        slope_scr[step] = (share + upward * density).astype(bf16)
        accumulate(step, total, dot(activated, down_scr[slot], 1, 0))

    @pl.when(step == tiles)
    def _():
        out_scr[...] = (grad_ref[...] + (total[...] + down_bias_ref[...])).astype(bf16)
        out_near.start()
        out_far.start()

    item = step - tiles

    @pl.when(item >= 2)
    def _():
        to_core(item - 2).wait_send()

    @pl.when((item >= 0) & (item < tiles))
    def _():
        grad_scr[...] = dot(cot_scr[...], act_scr[item], 0, 0)
        split_rows(grad_scr, keep_ring.at[item % 3], outgoing.at[slot], core)
        to_core(item).start()
        act_grad = dot(cot_scr[...], down_scr[slot], 1, 1)
        upward_grad = (act_grad * slope_scr[item].astype(f32)).astype(bf16)
        slope_scr[item] = upward_grad
        up_bias_grad_ref[0] = column_sum(upward_grad.astype(f32))
        accumulate(item, total, dot(upward_grad, up_scr[slot], 1, 1))

    @pl.when(item == tiles - 1)
    def _():
        unit, scale = norm_parts(grad_ref[...])
        normed_grad = total[...]
        residual_grad = cot_scr[...].astype(f32) + norm_back(
            normed_grad, unit, scale, gain_ref[...]
        )
        low = residual_grad.astype(bf16)
        grad_ref[...] = residual_grad
        low_scr[...] = low
        att_scr[...] = dot(proj_other_ref[...], low, 1, 1).astype(bf16)
        att_far.start()
        att_grad_ref[...] = dot(proj_ref[...], low, 1, 1).astype(bf16)
        vector_ref[0:1] = column_sum(normed_grad * unit)
        vector_ref[1:2] = column_sum(normed_grad)
        vector_ref[2:3] = column_sum(low.astype(f32))

    def send_gradient(value):
        grad_scr[...] = value
        split_rows(grad_scr, keep_ref.at[0], outgoing.at[slot], core)
        to_core(item).start()

    @pl.when((item >= tiles) & (item < 2 * tiles))
    def _():
        send_gradient(dot(n_scr[...], slope_scr[item - tiles], 0, 0))

    @pl.when(item == 2 * tiles)
    def _():
        send_gradient(dot(low_scr[...], att_ref[...], 0, 1))

    @pl.when(item == 2 * tiles + 1)
    def _():
        send_gradient(dot(low_scr[...], att_other_ref[...], 0, 1))

    early, late = item - 1, item - 2

    @pl.when((early >= 0) & (early < tiles))
    def _():
        to_core(early).wait_recv()
        arrive(early).start()

    @pl.when((late >= 2) & (late < tiles))
    def _():
        to_x(late - 2).wait_send()

    @pl.when((late >= 0) & (late < tiles))
    def _():
        arrive(late).wait()
        fold(
            keep_ring.at[late % 3],
            arrived.at[late % 2],
            x_side,
            keep_x_ref.at[0],
            outgoing_x.at[late % 2],
        )
        to_x(late).start()

    @pl.when(step == last)
    def _():
        gather_qkv.wait(3)
        items = got_hbm.shape[0]
        to_core(items - 2).wait_send()
        to_core(items - 1).wait_send()
        for index in range(tiles, items):
            to_core(index).wait_recv()
        to_x(tiles - 2).wait_send()
        to_x(tiles - 1).wait_send()
        for index in range(tiles):
            to_x(index).wait_recv()
        att_far.wait()
        out_near.wait()
        out_far.wait()


def feed_forward(
    count,
    att_mine,
    att_other,
    proj,
    proj_other,
    proj_bias,
    gain,
    shift,
    down_bias,
    up_bias,
    patches,
    cot,
    up,
    up_other,
    down,
    down_part,
    qkv,
):
    tokens, width = patches.shape
    half = tokens // 2
    columns = proj.shape[0]
    tiles = 2 * up.shape[1] // FF_TILE
    items = 2 * tiles + 2
    row = once((1, width))
    left = (width // count, FF_TILE)
    tile = lambda first, lead, size: pl.BlockSpec(
        (1,) + lead, lambda i: (clamp(i - first, size - 1),) + (0,) * len(lead)
    )
    vmem = pltpu.VMEM
    dma = lambda *shape: pltpu.SemaphoreType.DMA(shape)
    return pl.pallas_call(
        feed_kernel,
        grid=(tiles + items,),
        in_specs=[
            once((columns, half)),
            once((columns, half)),
            once(proj.shape),
            once(proj.shape),
            row,
            row,
            row,
            row,
            once(up_bias.shape),
            HBM,
            HBM,
            HBM,
            HBM,
            HBM,
            HBM,
            HBM,
        ],
        out_specs=(
            once((half, width)),
            once((columns, half)),
            once((4, width)),
            tile(tiles, (1, FF_TILE), tiles),
            tile(tiles + 2, (count // 4,) + left, tiles),
            tile(2 * tiles, (count // 2,) + left, tiles + 2),
            HBM,
            HBM,
            HBM,
            HBM,
            HBM,
            HBM,
        ),
        out_shape=(
            jax.ShapeDtypeStruct((half, width), f32),
            jax.ShapeDtypeStruct((columns, half), bf16),
            jax.ShapeDtypeStruct((4, width), f32),
            jax.ShapeDtypeStruct((tiles, 1, FF_TILE), f32),
            jax.ShapeDtypeStruct((tiles, count // 4) + left, bf16),
            jax.ShapeDtypeStruct((tiles + 2, count // 2) + left, bf16),
            jax.ShapeDtypeStruct((tokens, width), bf16),
            jax.ShapeDtypeStruct((columns, half), bf16),
            jax.ShapeDtypeStruct((items, count // 2) + left, bf16),
            jax.ShapeDtypeStruct((tiles, count // 4) + left, bf16),
            jax.ShapeDtypeStruct(down.shape, bf16),
            jax.ShapeDtypeStruct(qkv.shape, bf16),
        ),
        input_output_aliases={14: 10},
        scratch_shapes=[
            vmem((half, width), bf16),
            vmem((half, width), bf16),
            vmem((half, width), bf16),
            vmem((half, width), f32),
            vmem((tiles, half, FF_TILE), bf16),
            vmem((tiles, half, FF_TILE), bf16),
            vmem((2, width, FF_TILE), bf16),
            vmem((2, FF_TILE, width), bf16),
            vmem((half, width), bf16),
            vmem((columns, half), bf16),
            vmem((width, FF_TILE), f32),
            vmem((3, count // 2) + left, bf16),
            vmem((2, count // 2) + left, bf16),
            vmem((2, count // 2) + left, bf16),
            vmem((2, count // 4) + left, bf16),
            dma(2),
            dma(2),
            dma(2),
            pltpu.SemaphoreType.DMA,
            dma(2),
            dma(2),
            dma(2),
            dma(items),
            dma(2),
            dma(2),
            dma(tiles),
            dma(2, Gather.COPIES),
            dma(2, Gather.COPIES),
        ],
        compiler_params=params(2),
        cost_estimate=pl.CostEstimate(
            flops=12 * half * width * tiles * FF_TILE,
            bytes_accessed=60_000_000,
            transcendentals=half * tiles * FF_TILE,
        ),
        name="feed_forward",
    )(
        att_mine,
        att_other,
        proj,
        proj_other,
        proj_bias[None, :],
        gain[None, :],
        shift[None, :],
        down_bias[None, :],
        up_bias,
        patches,
        cot,
        up,
        up_other,
        down,
        down_part,
        qkv,
    )


class Chain:
    def __init__(self, keep, got, bits, scratch):
        self.keep, self.got, self.bits, self.scratch = keep, got, list(bits), list(scratch)
        self.last = None

    def step(self):
        if self.last is not None:
            self.copy(*self.last).wait()
            self.last = None
        if not self.bits:
            return
        bit = self.bits.pop(0)
        keep, send, got, sem = self.scratch.pop(0)
        fold(self.keep, self.got, partner_of(bit)[1], keep, send)
        self.last = (bit, send, got, sem)
        self.copy(*self.last).start()
        self.keep, self.got = keep, got

    def copy(self, bit, send, got, sem):
        return remote(send, got, sem.at[0], sem.at[1], partner_of(bit)[0])

    def result(self, tile):
        return self.keep[tile, 0].astype(f32) + self.got[tile, 0].astype(f32)


def input_back_kernel(
    bits,
    mine_ref,
    other_ref,
    w_ref,
    w_other_ref,
    gain_ref,
    vector_ref,
    down_keep,
    down_got,
    up_keep,
    up_got,
    qkv_keep,
    qkv_got,
    x_hbm,
    grad_hbm,
    total_ref,
    down_ref,
    up_ref,
    proj_ref,
    qkv_ref,
    out_hbm,
    total,
    x_scr,
    grad_scr,
    out_scr,
    vector_send,
    vector_got,
    vector_scr,
    vector_next,
    side_send,
    side_got,
    load_sem,
    store_sem,
    row_send,
    row_recv,
    vector_sem,
    side_sem,
    *scratch,
):
    step = pl.program_id(0)
    half, width = total.shape
    side = lax.axis_index("tensor")
    peer = {"tensor": 1 - side}
    mine = pl.ds(pl.multiple_of(side * half, 16), half)
    loads = [
        pltpu.make_async_copy(x_hbm.at[mine], x_scr, load_sem.at[0]),
        pltpu.make_async_copy(grad_hbm, grad_scr, load_sem.at[1]),
    ]
    stages, rest = [], list(scratch)
    for first in (3, 2, 1):
        stages.append([tuple(rest[4 * i : 4 * i + 4]) for i in range(bits - first)])
        rest = rest[4 * (bits - first) :]
    down = Chain(down_keep, down_got, range(3, bits), stages[0])
    up = Chain(up_keep, up_got, range(2, bits), stages[1])
    qkv = Chain(qkv_keep, qkv_got, range(1, bits), stages[2])

    @pl.when(step == 0)
    def _():
        for load in loads:
            load.start()
        greet([peer] + [partner_of(bit)[0] for bit in range(bits)])
        down.step()
        qkv.step()
        up.step()

    heads = other_ref.shape[0]
    left = other_ref[...].reshape(heads * HEAD_DIM, half)
    term = dot(mine_ref[0], w_ref[0], 0, 1) + dot(left, w_other_ref[0], 0, 1)
    accumulate(step, total, term)

    @pl.when(step == pl.num_programs(0) - 1)
    def _():
        for load in loads:
            load.wait()
        gain = gain_ref[...]
        sums = [0.0, 0.0]
        copies = []
        begin = 0
        for block, rows in enumerate((half // 32 * 16, half - half // 32 * 16)):
            at = pl.ds(begin, rows)
            unit, scale = norm_parts(x_scr[at].astype(f32))
            normed_grad = total[at]
            out = grad_scr[at] + norm_back(normed_grad, unit, scale, gain)
            out_scr[at] = out.astype(bf16)
            sums = [sums[0] + column_sum(normed_grad * unit), sums[1] + column_sum(normed_grad)]
            target = out_hbm.at[pl.ds(pl.multiple_of(side * half + begin, 16), rows)]
            copies.append(
                (
                    remote(out_scr.at[at], target, row_send.at[block], row_recv.at[block], peer),
                    pltpu.make_async_copy(out_scr.at[at], target, store_sem.at[block]),
                )
            )
            for copy in copies[-1]:
                copy.start()
            begin += rows

        both = vector_got.shape[1]
        vector_send[:, : 2 * width] = jnp.concatenate(sums, axis=1)
        vector_send[:, 2 * width :] = vector_ref[1:2, 2 * width : both]
        vector_copy = remote(vector_send, vector_got, vector_sem.at[0], vector_sem.at[1], peer)
        vector_copy.start()

        def other_side(parts, at):
            for number, part in enumerate(parts):
                side_send[at + number] = part.astype(bf16)
            size = len(parts)
            copy = remote(
                side_send.at[pl.ds(at, size)],
                side_got.at[pl.ds(at, size)],
                side_sem.at[2 * (at // size)],
                side_sem.at[2 * (at // size) + 1],
                peer,
            )
            copy.start()
            return copy

        tiles = down_ref.shape[1] // FF_TILE
        chains = [qkv, up, down]
        while down.bits:
            for chain in chains:
                chain.step()
        down.step()
        down_copy = other_side([down.result(tiles + i) for i in range(tiles)], 0)

        vector_copy.wait()
        vector_scr[:, :both] = vector_got[...] + jnp.concatenate(
            sums + [vector_ref[0:1, 2 * width : both]], axis=1
        )
        vector_scr[:, both:] = vector_ref[0:1, both:]

        def add_vectors(bit):
            copy = remote(
                vector_scr,
                vector_next.at[bit],
                vector_sem.at[2 * bit + 2],
                vector_sem.at[2 * bit + 3],
                partner_of(bit)[0],
            )
            copy.start()
            copy.wait()
            vector_scr[...] += vector_next[bit]

        vector_bits = list(range(bits))
        while up.bits or qkv.bits:
            if vector_bits:
                add_vectors(vector_bits.pop(0))
            qkv.step()
            up.step()
        for bit in vector_bits:
            add_vectors(bit)
        total_ref[...] = vector_scr[...]
        up.step()
        up_copy = other_side(
            [up.result(tiles + i) for i in range(tiles)] + [up.result(2 * tiles + 1)], tiles + 1
        )
        qkv.step()
        for part in range(3):
            qkv_ref[part] = qkv.result(part)
        down_copy.wait()
        up_copy.wait()
        for tile in range(tiles):
            at = pl.ds(tile * FF_TILE, FF_TILE)
            down_ref[:, at] = down.result(tile) + side_got[tile].astype(f32)
            up_ref[:, at] = up.result(tile) + side_got[tiles + 1 + tile].astype(f32)
        proj_ref[...] = up.result(2 * tiles) + side_got[2 * tiles + 1].astype(f32)
        for far, near in copies:
            near.wait()
            far.wait()


def input_backward(
    count,
    mine,
    other,
    weight,
    weight_other,
    gain,
    vectors,
    down_keep,
    down_got,
    up_keep,
    up_got,
    qkv_keep,
    qkv_got,
    patches,
    residual_grad,
):
    tokens, width = patches.shape
    half = tokens // 2
    columns = mine.shape[1]
    heads = other.shape[0]
    bits = count.bit_length() - 1
    rows = width // count
    tiles = heads // 2
    size = vectors.shape[1]
    both = size - FF_TILE * 3
    vmem = pltpu.VMEM
    dma = lambda *shape: pltpu.SemaphoreType.DMA(shape)
    scratch = []
    for first, lead in ((3, heads), (2, heads + 2), (1, 3)):
        for bit in range(first, bits):
            shape = (lead, count >> (bit + 1), rows, FF_TILE)
            scratch += [vmem(shape, bf16), vmem(shape, bf16), vmem(shape, bf16), dma(2)]
    return pl.pallas_call(
        functools.partial(input_back_kernel, bits),
        grid=(3,),
        in_specs=[
            pl.BlockSpec((1, columns, half), lambda i: (i, 0, 0)),
            pl.BlockSpec((heads, None, HEAD_DIM, half), lambda i: (0, i, 0, 0)),
            pl.BlockSpec((1, width, columns), lambda i: (i, 0, 0)),
            pl.BlockSpec((1, width, columns), lambda i: (i, 0, 0)),
            once((1, width)),
            once(vectors.shape),
            once(down_keep.shape),
            once(down_got.shape),
            once(up_keep.shape),
            once(up_got.shape),
            once(qkv_keep.shape),
            once(qkv_got.shape),
            HBM,
            HBM,
        ],
        out_specs=(
            once((1, size)),
            once((rows, tiles * FF_TILE)),
            once((rows, tiles * FF_TILE)),
            once((rows, columns)),
            once((3, rows, columns)),
            HBM,
        ),
        out_shape=(
            jax.ShapeDtypeStruct((1, size), f32),
            jax.ShapeDtypeStruct((rows, tiles * FF_TILE), f32),
            jax.ShapeDtypeStruct((rows, tiles * FF_TILE), f32),
            jax.ShapeDtypeStruct((rows, columns), f32),
            jax.ShapeDtypeStruct((3, rows, columns), f32),
            jax.ShapeDtypeStruct((tokens, width), bf16),
        ),
        scratch_shapes=[
            vmem((half, width), f32),
            vmem((half, width), bf16),
            vmem((half, width), f32),
            vmem((half, width), bf16),
            vmem((1, both), f32),
            vmem((1, both), f32),
            vmem((1, size), f32),
            vmem((bits, 1, size), f32),
            vmem((2 * tiles + 2, rows, FF_TILE), bf16),
            vmem((2 * tiles + 2, rows, FF_TILE), bf16),
            dma(2),
            dma(2),
            dma(2),
            dma(2),
            dma(2 * bits + 2),
            dma(4),
        ]
        + scratch,
        compiler_params=params(1),
        cost_estimate=pl.CostEstimate(
            flops=12 * half * width * columns, bytes_accessed=20_000_000, transcendentals=0
        ),
        name="input_backward",
    )(
        mine,
        other,
        weight,
        weight_other,
        gain[None, :],
        vectors,
        down_keep,
        down_got,
        up_keep,
        up_got,
        qkv_keep,
        qkv_got,
        patches,
        residual_grad,
    )


def over_tensor(value):
    return lax.ppermute(value, "tensor", [(0, 1), (1, 0)])


def on_device(
    count,
    patches,
    cotangent,
    clip_lengths,
    attn_gain,
    attn_shift,
    qkv_weight,
    qkv_bias,
    proj_weight,
    proj_bias,
    mlp_gain,
    mlp_shift,
    up_weight,
    up_bias,
    down_weight,
    down_bias,
):
    tokens, width = patches.shape
    local_width = proj_weight.shape[0]
    first_side = lax.axis_index("tensor") == 0

    qkv_parts = jnp.transpose(qkv_weight, (1, 0, 2))
    up_biases = jnp.concatenate([up_bias, over_tensor(up_bias)]).reshape(-1, 1, FF_TILE)

    clip_len = clip_lengths[0, 0]
    cosine, sine = rotary_angles(jnp.arange(tokens, dtype=jnp.int32) % clip_len)
    query_mask, key_mask = clip_masks(clip_len, tokens)
    (
        normed,
        qkv,
        attended,
        att_mine,
        totals,
        weights,
        att_other,
        proj_other,
        up_other,
        down_part,
    ) = attend_forward(
        patches,
        attn_gain,
        attn_shift,
        qkv_parts,
        qkv_bias,
        cosine,
        sine,
        query_mask,
        key_mask,
        proj_weight,
        up_weight,
        down_weight,
    )
    (
        residual_grad,
        att_grad_mine,
        vectors,
        up_bias_grad,
        down_keep,
        up_keep,
        block_out,
        att_grad_got,
        up_got,
        down_got,
        _,
        qkv_other,
    ) = feed_forward(
        count,
        att_mine,
        att_other,
        proj_weight,
        proj_other,
        proj_bias,
        mlp_gain,
        mlp_shift,
        down_bias,
        up_biases,
        patches,
        cotangent,
        up_weight,
        up_other,
        down_weight,
        down_part,
        qkv_parts,
    )
    left = jnp.where(first_side, att_grad_mine, att_grad_got)
    right = jnp.where(first_side, att_grad_got, att_grad_mine)
    (
        mixed_mine,
        qkv_keep,
        qkv_bias_grad,
        down_keep,
        up_keep,
        proj_keep,
        mixed_other,
        qkv_got,
        down_got,
        up_got,
    ) = attend_backward(
        count,
        weights,
        qkv,
        attended,
        totals,
        left,
        right,
        cosine,
        sine,
        normed,
        down_keep,
        down_got,
        up_keep,
        up_got,
    )

    hidden = up_bias.shape[0]
    vectors = vectors.reshape(1, -1)
    up_bias_grad = up_bias_grad.reshape(2, hidden)
    ends = jnp.zeros((2, 2 * width), f32)
    vectors = jnp.concatenate(
        [
            ends,
            jnp.concatenate([vectors, vectors]),
            up_bias_grad,
            jnp.concatenate([qkv_bias_grad.reshape(1, -1)] * 2),
        ],
        axis=1,
    )
    vectors, down_grad, up_grad, proj_grad, qkv_grad, patch_grad = input_backward(
        count,
        mixed_mine,
        mixed_other,
        qkv_parts,
        qkv_other,
        attn_gain,
        vectors,
        down_keep,
        down_got,
        jnp.concatenate([up_keep, proj_keep]),
        up_got,
        qkv_keep,
        qkv_got,
        patches,
        residual_grad,
    )
    part = lambda first, size=width: vectors[0, first : first + size]
    return (
        block_out,
        patch_grad,
        part(0),
        part(width),
        jnp.transpose(qkv_grad, (1, 0, 2)),
        part(6 * width + hidden, 3 * local_width).reshape(3, local_width),
        proj_grad.T,
        part(4 * width),
        part(2 * width),
        part(3 * width),
        up_grad,
        part(6 * width, hidden),
        down_grad.T,
        part(5 * width),
    )


def solution(mesh):
    return jax.shard_map(
        functools.partial(on_device, mesh.shape["dp"]),
        mesh=mesh,
        in_specs=(
            P("dp", None),
            P("dp", None),
            P("dp", None),
            P(),
            P(),
            P(None, None, "tensor"),
            P(None, "tensor"),
            P("tensor", None),
            P(),
            P(),
            P(),
            P(None, "tensor"),
            P("tensor"),
            P("tensor", None),
            P(),
        ),
        out_specs=(
            P("dp", None),
            P("dp", None),
            P(),
            P(),
            P("dp", None, "tensor"),
            P(None, "tensor"),
            P("tensor", "dp"),
            P(),
            P(),
            P(),
            P("dp", "tensor"),
            P("tensor"),
            P("tensor", "dp"),
            P(),
        ),
        check_vma=False,
    )
```

```python
import functools
import math

import jax
import jax.numpy as jnp
from jax import lax
from jax.experimental import pallas as pl
from jax.experimental.pallas import tpu as pltpu
from jax.sharding import PartitionSpec as P

HEAD_DIM = 64
HALF_DIM = HEAD_DIM // 2
GRID = 14
IMG = 196
EPS = 1e-06
SCALING = HEAD_DIM ** (-0.5)
LOG2E = math.log2(math.e)
KEY_CHUNKS = 2
MASK_ROWS = 16
ONES_ROWS = 16
FF_TILE = 512
FORBIDDEN = -1e30
VMEM_LIMIT = 62 * 1024 * 1024

MESH = pl.DeviceIdType.MESH

bf16 = jnp.bfloat16
f32 = jnp.float32


def dot(left, right, left_dim, right_dim):
    return lax.dot_general(
        left, right, (((left_dim,), (right_dim,)), ((), ())), preferred_element_type=f32
    )


def rotary_angles(offsets):
    pair_count = HALF_DIM
    side_pairs = pair_count * 11 // 32
    time_pairs = pair_count - 2 * side_pairs
    pair_index = jnp.arange(pair_count, dtype=jnp.int32)
    time_pair = pair_index < time_pairs
    height_pair = (pair_index >= time_pairs) & (pair_index < time_pairs + side_pairs)
    group_begin = jnp.where(
        time_pair, 0, jnp.where(height_pair, time_pairs, time_pairs + side_pairs)
    )
    group_size = jnp.where(time_pair, time_pairs, side_pairs)
    inverse = jnp.power(
        10000.0, -(pair_index - group_begin).astype(f32) / group_size.astype(f32)
    )
    frame_place = (offsets // IMG).astype(f32)
    row_place = (offsets % IMG // GRID).astype(f32)
    column_place = (offsets % GRID).astype(f32)
    position = jnp.where(
        time_pair[:, None],
        frame_place[None, :],
        jnp.where(height_pair[:, None], row_place[None, :], column_place[None, :]),
    )
    angles = position * inverse[:, None]
    return (jnp.cos(angles), jnp.sin(angles))


def params(collective_id=None):
    if collective_id is None:
        return pltpu.CompilerParams(vmem_limit_bytes=VMEM_LIMIT)
    return pltpu.CompilerParams(
        vmem_limit_bytes=VMEM_LIMIT, collective_id=collective_id, has_side_effects=True
    )


def greet(partners):
    barrier = pltpu.get_barrier_semaphore()
    for partner in partners:
        pl.semaphore_signal(barrier, inc=1, device_id=partner, device_id_type=MESH)
    pl.semaphore_wait(barrier, len(partners))


def partner_of(bit):
    index = lax.axis_index("dp")
    mine = (index // (1 << bit)) % 2
    return {"dp": index + (1 << bit) * (1 - 2 * mine)}, mine


def fold(keep, got, mine, next_keep, next_send):
    lead = (slice(None),) * (len(keep.shape) - 3)
    for pair in range(keep.shape[-3] // 2):
        for ref, odd in ((next_keep, mine), (next_send, 1 - mine)):
            at = lead + (2 * pair + odd,)
            value = keep[at]
            if got is not None:
                value = value.astype(f32) + got[at].astype(f32)
            ref[lead + (pair,)] = value.astype(bf16)


def remote(source, target, send_sem, recv_sem, partner):
    return pltpu.make_async_remote_copy(
        src_ref=source,
        dst_ref=target,
        send_sem=send_sem,
        recv_sem=recv_sem,
        device_id=partner,
        device_id_type=MESH,
    )


def whole_block(shape, **kwargs):
    return pl.BlockSpec(shape, lambda *_: (0,) * len(shape), **kwargs)


def once(shape):
    return whole_block(shape, pipeline_mode=pl.Buffered(1))


HBM = pl.BlockSpec(memory_space=pl.ANY)


def clamp(value, last):
    return jnp.minimum(jnp.maximum(value, 0), last)


def norm_parts(values):
    centre = values - jnp.mean(values, axis=1, keepdims=True)
    spread = jnp.mean(centre * centre, axis=1, keepdims=True)
    scale = lax.rsqrt(spread + EPS)
    return centre * scale, scale


def norm_back(grad, unit, scale, gain):
    c = grad * gain
    mean = jnp.mean(c, axis=1, keepdims=True)
    along = jnp.mean(c * unit, axis=1, keepdims=True)
    return scale * (c - mean - unit * along)


def column_sum(values):
    return jnp.sum(values, axis=0, keepdims=True)


def clip_masks(clip_len, tokens):
    token = jnp.arange(tokens, dtype=jnp.int32)[None, :] // IMG
    row = jnp.arange(MASK_ROWS, dtype=jnp.int32)[:, None]
    same = token == row
    images = clip_len < tokens
    forbid = images & jnp.logical_not(same) & (row < tokens // IMG)
    return jnp.where(forbid, FORBIDDEN, 0.0).astype(bf16), same.astype(bf16)


class Gather:
    STAGES = ((0,), (1, 2), (3, 4, 5, 6), (7, 8, 9, 10))
    COPIES = 11
    ROUTES = (
        (None, 0, 0, None),
        (0, 0, 0, 2),
        (1, 0, 0, 1),
        (0, 0, 0, 1),
        (0, 0, 1, 1),
        (1, 0, 0, 2),
        (1, 1, 0, 2),
        (None, 0, 0, 0),
        (None, 1, 0, 0),
        (None, 0, 1, 0),
        (None, 1, 1, 0),
    )

    def __init__(self, weight, other, send_sem, recv_sem):
        self.weight, self.other = weight, other
        self.send_sem, self.recv_sem = send_sem, recv_sem

    def place(self, x, z):
        core, mine_x, mine_z = (partner_of(bit)[1] for bit in range(3))
        x = mine_x + x * (1 - 2 * mine_x)
        return core + 2 * x + 4 * (mine_z + z * (1 - 2 * mine_z)), 8

    def copy(self, number):
        half, x, z, bit = self.ROUTES[number]
        index, parts = self.place(x, z)
        rows = self.other.shape[-2] // parts
        begin = index * rows
        if half is not None:
            rows //= 2
            begin = begin + half * rows
        at = (slice(None),) * (len(self.other.shape) - 2)
        at = at + (pl.ds(pl.multiple_of(begin, rows), rows),)
        source = self.weight if number == 0 else self.other
        return remote(
            source.at[at],
            self.other.at[at],
            self.send_sem.at[number],
            self.recv_sem.at[number],
            {"tensor": 1 - lax.axis_index("tensor")} if bit is None else partner_of(bit)[0],
        )

    def start(self, stage):
        for number in self.STAGES[stage]:
            self.copy(number).start()

    def wait(self, stage):
        for number in self.STAGES[stage]:
            self.copy(number).wait()

    def advance(self, stage):
        self.wait(stage - 1)
        self.start(stage)


class GatherZ(Gather):
    STAGES = ((0,), (1,), (2, 3))
    ROUTES = ((None, 0, 0, None), (None, 0, 0, 2), (None, 0, 0, 0), (None, 0, 1, 0))

    def place(self, x, z):
        core, mine_z = partner_of(0)[1], partner_of(2)[1]
        return core + 2 * (mine_z + z * (1 - 2 * mine_z)), 4


def neighbours():
    return [{"tensor": 1 - lax.axis_index("tensor")}] + [partner_of(bit)[0] for bit in range(3)]


def attend_kernel(
    x_ref,
    gain_ref,
    shift_ref,
    w_ref,
    b_ref,
    cos_ref,
    sin_ref,
    qm_ref,
    km_ref,
    proj_hbm,
    up_hbm,
    down_hbm,
    normed_ref,
    qkv_ref,
    att_ref,
    mine_ref,
    factor_ref,
    e_hbm,
    other_hbm,
    proj_other,
    up_other,
    down_other,
    k_scr,
    s_scr,
    e_scr,
    outgoing,
    e_sem,
    send_sem,
    recv_sem,
    gather_send,
    gather_recv,
):
    step, last = pl.program_id(0), pl.num_programs(0) - 1
    tokens, width = x_ref.shape
    half = tokens // 2
    chunk = tokens // KEY_CHUNKS
    heads = e_hbm.shape[0]
    side = lax.axis_index("tensor")
    peer = {"tensor": 1 - side}
    proj = Gather(proj_hbm, proj_other, gather_send.at[0], gather_recv.at[0])
    up = Gather(up_hbm, up_other, gather_send.at[1], gather_recv.at[1])
    down = Gather(down_hbm, down_other, gather_send.at[2], gather_recv.at[2])

    @pl.when(step == 0)
    def _():
        greet(neighbours())
        proj.start(0)
        up.start(0)
        unit, _ = norm_parts(x_ref[...].astype(f32))
        normed_ref[:width] = (unit * gain_ref[...] + shift_ref[...]).astype(bf16).T
        normed_ref[width:] = jnp.ones((ONES_ROWS, tokens), bf16)

    for at, weight, stage in (
        (2, proj, 1),
        (3, down, 0),
        (4, proj, 2),
        (4, up, 1),
        (6, proj, 3),
        (6, up, 2),
        (9, up, 3),
    ):

        @pl.when(step == at)
        def _():
            if stage:
                weight.advance(stage)
            else:
                weight.start(stage)

    @pl.when(step < 3)
    def _():
        rows = w_ref.shape[2]
        bias = jnp.broadcast_to(b_ref[pl.ds(step, 1), :], (8, rows)).T[:, :1]
        mixed = dot(w_ref[0], normed_ref[:width], 0, 0) + bias

        @pl.when(step < 2)
        def _():
            cosine, sine = cos_ref[...], sin_ref[...]
            for begin in range(0, rows, HEAD_DIM):
                middle, end = begin + HALF_DIM, begin + HEAD_DIM
                low, high = mixed[begin:middle], mixed[middle:end]
                qkv_ref[step, begin:middle, :] = (low * cosine - high * sine).astype(bf16)
                qkv_ref[step, middle:end, :] = (high * cosine + low * sine).astype(bf16)

        @pl.when(step == 2)
        def _():
            qkv_ref[step] = mixed.astype(bf16)

    head = step - 3
    slot = head % 2

    def store(index, part):
        at = pl.ds(part * chunk, chunk)
        return pltpu.make_async_copy(
            e_scr.at[index % 2, at], e_hbm.at[index, at], e_sem.at[index % 2, part]
        )

    def exchange(index):
        at = pl.ds(pl.multiple_of(index * HEAD_DIM, HEAD_DIM), HEAD_DIM)
        return remote(
            outgoing.at[index],
            other_hbm.at[at],
            send_sem.at[index],
            recv_sem.at[index],
            peer,
        )

    @pl.when(head >= 2)
    def _():
        for part in range(KEY_CHUNKS):
            store(head - 2, part).wait()

    @pl.when(head >= 0)
    def _():
        at = pl.ds(pl.multiple_of(clamp(head, heads - 1) * HEAD_DIM, HEAD_DIM), HEAD_DIM)
        queries = jnp.concatenate([qkv_ref[0, at], qm_ref[...]], axis=0)
        k_scr[...] = jnp.concatenate([qkv_ref[1, at], km_ref[...]], axis=0).T
        values = jnp.concatenate([qkv_ref[2, at], jnp.ones((16, tokens), bf16)], axis=0)
        top, out, tops = None, None, []
        s_scr[0] = dot(k_scr[:chunk], queries, 1, 0)
        for part in range(KEY_CHUNKS):
            begin, end = part * chunk, (part + 1) * chunk
            if part + 1 < KEY_CHUNKS:
                s_scr[(part + 1) % 2] = dot(k_scr[end : end + chunk], queries, 1, 0)
            scores = s_scr[part % 2]
            here = jnp.max(scores, axis=0, keepdims=True)
            new_top = here if top is None else jnp.maximum(top, here)
            weights = jnp.exp2((scores - new_top) * (SCALING * LOG2E)).astype(bf16)
            e_scr[slot, begin:end] = weights
            store(head, part).start()
            term = dot(values[:, begin:end], weights, 1, 0)
            if out is None:
                out = term
            else:
                out = out * jnp.exp2((top - new_top) * (SCALING * LOG2E)) + term
            top = new_top
            tops.append(top)
        scale = 1.0 / out[HEAD_DIM : HEAD_DIM + 1]
        for part in range(KEY_CHUNKS):
            factor_ref[0, part : part + 1] = scale * jnp.exp2(
                (tops[part] - top) * (SCALING * LOG2E)
            )
        attended = out[:HEAD_DIM] * scale
        att_ref[...] = attended.astype(bf16)
        left, right = attended[:, :half], attended[:, half:]
        mine_ref[...] = jnp.where(side == 0, left, right).astype(bf16)
        outgoing[clamp(head, heads - 1)] = jnp.where(side == 0, right, left).astype(bf16)
        exchange(head).start()

    @pl.when(step == last)
    def _():
        for back in (2, 1):
            for part in range(KEY_CHUNKS):
                store(heads - back, part).wait()
        for index in range(heads):
            exchange(index).wait()
        for weight, stage in ((proj, 3), (up, 3), (down, 0)):
            weight.wait(stage)


def attend_forward(
    patches, gain, shift, weight, bias, cosine, sine, query_mask, key_mask, proj, up, down
):
    tokens, width = patches.shape
    columns = weight.shape[2]
    heads = columns // HEAD_DIM
    half = tokens // 2
    head = lambda i: clamp(i - 3, heads - 1)
    vmem = pltpu.VMEM
    dma = lambda *shape: pltpu.SemaphoreType.DMA(shape)
    return pl.pallas_call(
        attend_kernel,
        grid=(3 + heads,),
        out_shape=(
            jax.ShapeDtypeStruct((width + ONES_ROWS, tokens), bf16),
            jax.ShapeDtypeStruct((3, columns, tokens), bf16),
            jax.ShapeDtypeStruct((columns, tokens), bf16),
            jax.ShapeDtypeStruct((columns, half), bf16),
            jax.ShapeDtypeStruct((heads, KEY_CHUNKS, tokens), f32),
            jax.ShapeDtypeStruct((heads, tokens, tokens), bf16),
            jax.ShapeDtypeStruct((columns, half), bf16),
            jax.ShapeDtypeStruct(proj.shape, bf16),
            jax.ShapeDtypeStruct(up.shape, bf16),
            jax.ShapeDtypeStruct(down.shape, bf16),
        ),
        in_specs=[
            once((tokens, width)),
            once((1, width)),
            once((1, width)),
            pl.BlockSpec((1, width, columns), lambda i: (clamp(i, 2), 0, 0)),
            once((3, columns)),
            once(cosine.shape),
            once(sine.shape),
            once(query_mask.shape),
            once(key_mask.shape),
            HBM,
            HBM,
            HBM,
        ],
        out_specs=(
            once((width + ONES_ROWS, tokens)),
            once((3, columns, tokens)),
            pl.BlockSpec((HEAD_DIM, tokens), lambda i: (head(i), 0)),
            pl.BlockSpec((HEAD_DIM, half), lambda i: (head(i), 0)),
            pl.BlockSpec((1, KEY_CHUNKS, tokens), lambda i: (head(i), 0, 0)),
            HBM,
            HBM,
            HBM,
            HBM,
            HBM,
        ),
        scratch_shapes=[
            vmem((tokens, HEAD_DIM + MASK_ROWS), bf16),
            vmem((2, tokens // KEY_CHUNKS, tokens), f32),
            vmem((2, tokens, tokens), bf16),
            vmem((heads, HEAD_DIM, half), bf16),
            dma(2, KEY_CHUNKS),
            dma(heads),
            dma(heads),
            dma(3, Gather.COPIES),
            dma(3, Gather.COPIES),
        ],
        compiler_params=params(3),
        cost_estimate=pl.CostEstimate(
            flops=6 * tokens * width * columns + 16 * heads * tokens * tokens * HEAD_DIM,
            bytes_accessed=60_000_000,
            transcendentals=heads * tokens * tokens,
        ),
        name="attend_forward",
    )(
        patches,
        gain[None, :],
        shift[None, :],
        weight,
        bias,
        cosine,
        sine,
        query_mask,
        key_mask,
        proj,
        up,
        down,
    )


def attend_back_kernel(
    e_ref,
    q_ref,
    k_ref,
    v_ref,
    out_ref,
    total_ref,
    att_grad_ref,
    cos_ref,
    sin_ref,
    normed_ref,
    down_keep_ref,
    down_got_ref,
    up_keep_ref,
    up_got_ref,
    att_send_hbm,
    _,
    mine_ref,
    keep_ref,
    sum_ref,
    down_sum_ref,
    up_sum_ref,
    other_ref,
    got_ref,
    att_got_hbm,
    att_scr,
    up_scr,
    up_low,
    value_scr,
    v_scr,
    score_grad,
    turned,
    pair_scr,
    outgoing,
    grad,
    outgoing_core,
    down_scr,
    down_last,
    up_first,
    up_last,
    send_sem,
    recv_sem,
    core_send,
    core_recv,
    down_sem,
    down_last_sem,
    up_sem,
    up_last_sem,
    att_sem,
    att_load_sem,
):
    head, heads = pl.program_id(0), pl.num_programs(0)
    tokens = q_ref.shape[2]
    half = tokens // 2
    side = lax.axis_index("tensor")
    peer = {"tensor": 1 - side}
    core_partner, core = partner_of(0)
    slot = head % 2
    def exchange(index):
        return remote(
            outgoing.at[index % 4],
            other_ref.at[index],
            send_sem.at[index % 4],
            recv_sem.at[index],
            peer,
        )

    def to_core(pair):
        at = pl.ds(pl.multiple_of(pair * 2 * HEAD_DIM, 2 * HEAD_DIM), 2 * HEAD_DIM)
        return remote(
            outgoing_core.at[pair % 2],
            got_ref.at[:, :, :, at],
            core_send.at[pair % 2],
            core_recv.at[pair],
            core_partner,
        )

    def hop(buffers, sems, pair, bit):
        at = pl.ds(2 * pair, 2)
        return remote(
            buffers.at[1, at],
            buffers.at[2, at],
            sems.at[0, pair],
            sems.at[1, pair],
            partner_of(bit)[0],
        )

    def start(keep, got, buffers, sems, pair, bit):
        at = pl.ds(2 * pair, 2)
        fold(keep, got, partner_of(bit)[1], buffers.at[0, at], buffers.at[1, at])
        hop(buffers, sems, pair, bit).start()

    def relay(source, source_sems, source_bit, buffers, sems, pair, bit):
        hop(source, source_sems, pair, source_bit).wait_recv()
        at = pl.ds(2 * pair, 2)
        start(source.at[0, at], source.at[2, at], buffers, sems, pair, bit)

    down_pairs, up_pairs = down_scr.shape[1] // 2, up_first.shape[1] // 2
    behind = heads - up_pairs

    late_heads = pl.ds(att_got_hbm.shape[0] // 2, att_got_hbm.shape[0] // 2)
    att_far = remote(
        att_send_hbm.at[late_heads], att_got_hbm.at[late_heads], att_sem.at[0], att_sem.at[1], peer
    )

    def att_load(index):
        at = pl.ds(pl.multiple_of(index * HEAD_DIM, HEAD_DIM), HEAD_DIM)
        return pltpu.make_async_copy(
            att_got_hbm.at[at], att_scr.at[index % 2], att_load_sem.at[index % 2]
        )

    @pl.when(head == 0)
    def _():
        att_load(0).start()
        greet(neighbours() + [partner_of(3)[0]])
        att_far.start()

    @pl.when(head >= 4)
    def _():
        exchange(head - 4).wait_send()

    @pl.when(head < up_pairs)
    def _():
        start(up_keep_ref, up_got_ref, up_first, up_sem, head, 1)

    @pl.when(head < down_pairs)
    def _():
        start(down_keep_ref, down_got_ref, down_scr, down_sem, head, 2)

    @pl.when(head >= heads - down_pairs)
    def _():
        relay(
            down_scr, down_sem, 2, down_last, down_last_sem, head - (heads - down_pairs), 3
        )

    @pl.when(head >= behind)
    def _():
        relay(up_first, up_sem, 1, up_last, up_last_sem, head - behind, 2)

    @pl.when(head + 1 == heads // 2)
    def _():
        att_far.wait_recv()

    @pl.when(head + 1 < heads)
    def _():
        att_load(head + 1).start()

    att_load(head).wait()
    chunks = total_ref.shape[1]
    chunk = tokens // chunks
    att_mine, att_other = att_grad_ref[...].astype(f32), att_scr[slot].astype(f32)
    up_scr[:, :half] = jnp.where(side == 0, att_mine, att_other)
    up_scr[:, half:] = jnp.where(side == 0, att_other, att_mine)
    attended = out_ref[...].astype(f32)
    centre = []
    for part in range(chunks):
        up_low[part] = (up_scr[...] * total_ref[0, part : part + 1]).astype(bf16)
        centre.append(column_sum(up_low[part].astype(f32) * attended))
    v_scr[...] = v_ref[0].T
    cosine, sine = cos_ref[...], sin_ref[...]

    def store(part, low, high):
        for row, value in ((0, low), (HALF_DIM, high)):
            left, right = value[:, :half], value[:, half:]
            mine_ref[part, row : row + HALF_DIM] = jnp.where(side == 0, left, right).astype(bf16)
            outgoing[head % 4, part, row : row + HALF_DIM] = jnp.where(
                side == 0, right, left
            ).astype(bf16)
            begin = pl.multiple_of(part * 2 * HEAD_DIM + slot * HEAD_DIM + row, HALF_DIM)
            pair_scr[pl.ds(begin, HALF_DIM)] = value.astype(bf16)

    def unrotated(part, grad):
        low, high = grad[:HALF_DIM] * SCALING, grad[HALF_DIM:] * SCALING
        store(part, low * cosine + high * sine, high * cosine - low * sine)

    for part in range(chunks):
        at = slice(part * chunk, (part + 1) * chunk)
        value_scr[:, at] = dot(up_low[part], e_ref[0, at], 1, 1)
        prob_grad = dot(v_scr[at], up_low[part], 1, 0)
        score_grad[at] = (e_ref[0, at].astype(f32) * (prob_grad - centre[part])).astype(bf16)
    store(2, value_scr[:HALF_DIM], value_scr[HALF_DIM:])
    unrotated(0, dot(k_ref[0], score_grad[...], 1, 0))
    turned[...] = score_grad[...].T
    unrotated(1, dot(q_ref[0], turned[...], 1, 0))
    exchange(head).start()

    @pl.when(slot == 1)
    def _():
        pair = head // 2
        width = grad.shape[0] - ONES_ROWS
        grad[...] = dot(normed_ref[...], pair_scr[...], 1, 1)

        @pl.when(pair >= 2)
        def _():
            to_core(pair - 2).wait_send()

        for part in range(3):
            lanes = pl.ds(part * 2 * HEAD_DIM, 2 * HEAD_DIM)
            split_rows(
                grad.at[:, lanes], keep_ref.at[part], outgoing_core.at[pair % 2, part], core
            )
            sum_ref[part : part + 1] = grad[width : width + 1, lanes]
        to_core(pair).start()

    @pl.when(head == heads - 1)
    def _():
        for back in range(4):
            exchange(heads - 1 - back).wait_send()
        for back in range(2):
            to_core(heads // 2 - 1 - back).wait_send()
        for index in range(other_ref.shape[0] // 2):
            to_core(index).wait_recv()
        for pair in range(down_pairs):
            hop(down_scr, down_sem, pair, 2).wait_send()
            hop(down_last, down_last_sem, pair, 3).wait()
        down_sum_ref[...] = down_last[0].astype(f32) + down_last[2].astype(f32)
        for pair in range(up_pairs):
            hop(up_first, up_sem, pair, 1).wait_send()
            hop(up_last, up_last_sem, pair, 2).wait()
        up_sum_ref[...] = (up_last[0].astype(f32) + up_last[2].astype(f32)).astype(bf16)
        att_far.wait_send()
        for index in range(other_ref.shape[0]):
            exchange(index).wait_recv()


def attend_backward(
    count,
    weights,
    qkv,
    attended,
    totals,
    att_grad,
    att_send,
    att_got,
    cosine,
    sine,
    normed,
    down_keep,
    down_got,
    up_keep,
    up_got,
):
    tokens = qkv.shape[2]
    half = tokens // 2
    heads = weights.shape[0]
    columns = heads * HEAD_DIM
    width = normed.shape[0] - ONES_ROWS
    rows = width // count
    split = (3, count // 2, rows)
    blocks = lambda bits: (count >> bits, rows, FF_TILE)
    pair = lambda lead, first, last: pl.BlockSpec(
        (2,) + lead, lambda i: (first + clamp(i, last), 0, 0, 0)
    )
    block = lambda part: pl.BlockSpec((1, HEAD_DIM, tokens), lambda i: (part, i, 0))
    half_block = pl.BlockSpec((HEAD_DIM, half), lambda i: (i, 0))
    pair_block = pl.BlockSpec(split + (2 * HEAD_DIM,), lambda i: (0, 0, 0, i // 2))
    vmem = pltpu.VMEM
    dma = lambda *shape: pltpu.SemaphoreType.DMA(shape)
    return pl.pallas_call(
        attend_back_kernel,
        grid=(heads,),
        out_shape=(
            jax.ShapeDtypeStruct((3, columns, half), bf16),
            jax.ShapeDtypeStruct(split + (columns,), bf16),
            jax.ShapeDtypeStruct((3, columns), f32),
            jax.ShapeDtypeStruct((heads,) + blocks(4), f32),
            jax.ShapeDtypeStruct((heads + 2,) + blocks(3), bf16),
            jax.ShapeDtypeStruct((heads, 3, HEAD_DIM, half), bf16),
            jax.ShapeDtypeStruct(split + (columns,), bf16),
            jax.ShapeDtypeStruct(att_got.shape, bf16),
        ),
        input_output_aliases={15: 7},
        in_specs=[
            pl.BlockSpec((1, tokens, tokens), lambda i: (i, 0, 0)),
            block(0),
            block(1),
            block(2),
            pl.BlockSpec((HEAD_DIM, tokens), lambda i: (i, 0)),
            pl.BlockSpec((1, totals.shape[1], tokens), lambda i: (i, 0, 0)),
            half_block,
            once(cosine.shape),
            once(sine.shape),
            once(normed.shape),
            pair(blocks(2), 0, heads // 2 - 1),
            pair(blocks(2), 0, heads // 2 - 1),
            pair(blocks(1), 0, heads // 2),
            pair(blocks(1), heads // 2, heads // 2),
            HBM,
            HBM,
        ],
        out_specs=(
            pl.BlockSpec((3, HEAD_DIM, half), lambda i: (0, i, 0)),
            pair_block,
            pl.BlockSpec((3, 2 * HEAD_DIM), lambda i: (0, i // 2)),
            once((heads,) + blocks(4)),
            once((heads + 2,) + blocks(3)),
            HBM,
            HBM,
            HBM,
        ),
        scratch_shapes=[
            vmem((2, HEAD_DIM, half), bf16),
            vmem((HEAD_DIM, tokens), f32),
            vmem((totals.shape[1], HEAD_DIM, tokens), bf16),
            vmem((HEAD_DIM, tokens), f32),
            vmem((tokens, HEAD_DIM), bf16),
            vmem((tokens, tokens), bf16),
            vmem((tokens, tokens), bf16),
            vmem((6 * HEAD_DIM, tokens), bf16),
            vmem((4, 3, HEAD_DIM, half), bf16),
            vmem((width + ONES_ROWS, 6 * HEAD_DIM), f32),
            vmem((2,) + split + (2 * HEAD_DIM,), bf16),
            vmem((3, heads) + blocks(3), bf16),
            vmem((3, heads) + blocks(4), bf16),
            vmem((3, heads + 2) + blocks(2), bf16),
            vmem((3, heads + 2) + blocks(3), bf16),
            dma(4),
            dma(heads),
            dma(2),
            dma(heads // 2),
            dma(2, heads // 2),
            dma(2, heads // 2),
            dma(2, heads // 2 + 1),
            dma(2, heads // 2 + 1),
            dma(2),
            dma(2),
        ],
        compiler_params=params(0),
        cost_estimate=pl.CostEstimate(
            flops=32 * heads * tokens * tokens * HEAD_DIM,
            bytes_accessed=2 * heads * tokens * tokens,
            transcendentals=0,
        ),
        name="attend_backward",
    )(
        weights,
        qkv,
        qkv,
        qkv,
        attended,
        totals,
        att_grad,
        cosine,
        sine,
        normed,
        down_keep,
        down_got,
        up_keep,
        up_got,
        att_send,
        att_got,
    )


def normal_parts(value):
    a = jnp.abs(value)
    t = 1.0 / (1.0 + (0.3275911 / math.sqrt(2.0)) * a)
    bell = jnp.exp2(value * value * (-0.5 * LOG2E))
    c = [0.5 * x for x in (0.254829592, -0.284496736, 1.421413741, -1.453152027, 1.061405429)]
    tail = ((((c[4] * t + c[3]) * t + c[2]) * t + c[1]) * t + c[0]) * t * bell
    return jnp.where(value >= 0, 1.0 - tail, tail), bell * (1.0 / math.sqrt(2.0 * math.pi))


def split_rows(grad, keep_ref, send_ref, core):
    count, rows = keep_ref.shape[:2]
    for pair in range(count):
        for ref, odd in ((keep_ref, core), (send_ref, 1 - core)):
            begin = pl.multiple_of((2 * pair + odd) * rows, rows)
            ref[pair] = grad[pl.ds(begin, rows), :].astype(bf16)


def accumulate(step, total, term):
    @pl.when(step == 0)
    def _():
        total[...] = term

    @pl.when(step > 0)
    def _():
        total[...] += term


def feed_kernel(
    att_ref,
    att_other_ref,
    proj_ref,
    proj_other_ref,
    proj_bias_ref,
    gain_ref,
    shift_ref,
    down_bias_ref,
    up_bias_ref,
    patch_hbm,
    cot_hbm,
    up_hbm,
    up_other_hbm,
    down_hbm,
    _,
    qkv_hbm,
    grad_ref,
    att_grad_ref,
    att_scr,
    vector_ref,
    up_bias_grad_ref,
    keep_x_ref,
    keep_ref,
    out_hbm,
    att_got_hbm,
    got_hbm,
    got_x_hbm,
    down_other_hbm,
    qkv_other_hbm,
    n_scr,
    cot_scr,
    out_scr,
    total,
    act_scr,
    slope_scr,
    up_scr,
    down_scr,
    low_scr,
    grad_scr,
    keep_ring,
    outgoing,
    arrived,
    outgoing_x,
    load_sem,
    up_sem,
    down_sem,
    store_sem,
    row_sem,
    att_sem,
    send_sem,
    recv_sem,
    arrive_sem,
    send_x_sem,
    recv_x_sem,
    gather_send,
    gather_recv,
):
    step, last = pl.program_id(0), pl.num_programs(0) - 1
    tiles = act_scr.shape[0]
    half_tiles = tiles // 2
    half = n_scr.shape[0]
    side = lax.axis_index("tensor")
    peer = {"tensor": 1 - side}
    core_partner, core = partner_of(0)
    x_partner, x_side = partner_of(1)
    mine = pl.ds(pl.multiple_of(side * half, 16), half)
    gather_down = Gather(down_hbm, down_other_hbm, gather_send.at[0], gather_recv.at[0])
    gather_qkv = GatherZ(qkv_hbm, qkv_other_hbm, gather_send.at[1], gather_recv.at[1])
    patch_load = pltpu.make_async_copy(patch_hbm.at[mine], out_scr, load_sem.at[0])
    cot_load = pltpu.make_async_copy(cot_hbm.at[mine], cot_scr, load_sem.at[1])
    out_near = pltpu.make_async_copy(out_scr, out_hbm.at[mine], store_sem)
    out_far = remote(out_scr, out_hbm.at[mine], row_sem.at[0], row_sem.at[1], peer)
    early_heads = pl.ds(0, att_scr.shape[0] // 2)
    att_far = remote(
        att_scr.at[early_heads], att_got_hbm.at[early_heads], att_sem.at[0], att_sem.at[1], peer
    )

    def load_up(tile, act):
        for begin, source in ((0, up_hbm), (half_tiles, up_other_hbm)):

            @pl.when((tile >= begin) & (tile < begin + half_tiles))
            def _():
                at = pl.ds(pl.multiple_of((tile - begin) * FF_TILE, FF_TILE), FF_TILE)
                copy = pltpu.make_async_copy(
                    source.at[:, at], up_scr.at[tile % 2], up_sem.at[tile % 2]
                )
                getattr(copy, act)()

    def load_down(tile, act):
        for begin, source in ((0, down_hbm), (half_tiles, down_other_hbm)):

            @pl.when((tile >= begin) & (tile < begin + half_tiles))
            def _():
                at = pl.ds(pl.multiple_of((tile - begin) * FF_TILE, FF_TILE), FF_TILE)
                copy = pltpu.make_async_copy(
                    source.at[at], down_scr.at[tile % 2], down_sem.at[tile % 2]
                )
                getattr(copy, act)()

    def to_core(index):
        return remote(
            outgoing.at[index % 2],
            got_hbm.at[index],
            send_sem.at[index % 2],
            recv_sem.at[index],
            core_partner,
        )

    def to_x(index):
        return remote(
            outgoing_x.at[index],
            got_x_hbm.at[index],
            send_x_sem.at[index],
            recv_x_sem.at[index],
            x_partner,
        )

    def arrive(index):
        return pltpu.make_async_copy(
            got_hbm.at[index], arrived.at[index % 2], arrive_sem.at[index % 2]
        )

    @pl.when(step == 0)
    def _():
        patch_load.start()
        cot_load.start()
        load_up(0, "start")
        greet(neighbours())
        gather_down.start(1)
        gather_qkv.start(0)
        branch = dot(att_ref[...], proj_ref[...], 0, 0).astype(bf16).astype(f32)
        other = dot(att_other_ref[...], proj_other_ref[...], 0, 0).astype(bf16).astype(f32)
        patch_load.wait()
        residual = out_scr[...].astype(f32) + (branch + other + proj_bias_ref[...])
        grad_ref[...] = residual
        unit, _ = norm_parts(residual)
        n_scr[...] = (unit * gain_ref[...] + shift_ref[...]).astype(bf16)
        cot_load.wait()
        vector_ref[3:4] = column_sum(cot_scr[...].astype(f32))

    slot = step % 2

    for at, weight, stage in (
        (half_tiles - 1, gather_down, 2),
        (tiles, gather_down, 3),
        (tiles + 4, gather_qkv, 1),
        (2 * tiles + 4, gather_qkv, 2),
    ):

        @pl.when(step == at)
        def _():
            weight.advance(stage)

    @pl.when(step == tiles + half_tiles - 1)
    def _():
        gather_down.wait(3)

    first, second, third = step, step - tiles, step - 2 * tiles

    @pl.when(first + 1 < tiles)
    def _():
        load_up(first + 1, "start")

    @pl.when(first < tiles)
    def _():
        load_up(first, "wait")

    @pl.when((second + 1 >= 0) & (second + 1 < tiles))
    def _():
        load_down(second + 1, "start")

    @pl.when((second >= 0) & (second < tiles))
    def _():
        load_down(second, "wait")

    @pl.when((third + 1 >= 0) & (third + 1 < tiles))
    def _():
        load_up(third + 1, "start")
        load_down(third + 1, "start")

    @pl.when((third >= 0) & (third < tiles))
    def _():
        load_up(third, "wait")
        load_down(third, "wait")

    item = jnp.where(step < tiles, step, step - 2 * tiles)
    sends = (step < tiles) | (step >= 3 * tiles)

    @pl.when(sends & (item >= 2))
    def _():
        to_core(item - 2).wait_send()

    def send_gradient(value, keep):
        grad_scr[...] = value
        split_rows(grad_scr, keep, outgoing.at[slot], core)
        to_core(item).start()

    @pl.when(first < tiles)
    def _():
        upward = dot(n_scr[...], up_scr[slot], 1, 0) + up_bias_ref[clamp(first, tiles - 1)]
        share, density = normal_parts(upward)
        activated = (upward * share).astype(bf16)
        act_scr[clamp(first, tiles - 1)] = activated
        slope_scr[clamp(first, tiles - 1)] = (share + upward * density).astype(bf16)
        send_gradient(dot(cot_scr[...], activated, 0, 0), keep_ring.at[clamp(first, tiles - 1)])

    @pl.when((second >= 0) & (second < tiles))
    def _():
        accumulate(second, total, dot(act_scr[clamp(second, tiles - 1)], down_scr[slot], 1, 0))

    @pl.when(second == tiles - 1)
    def _():
        out_scr[...] = (grad_ref[...] + (total[...] + down_bias_ref[...])).astype(bf16)
        out_near.start()
        out_far.start()

    @pl.when((third >= 0) & (third < tiles))
    def _():
        tile = clamp(third, tiles - 1)
        act_grad = dot(cot_scr[...], down_scr[slot], 1, 1)
        upward_grad = (act_grad * slope_scr[tile].astype(f32)).astype(bf16)
        slope_scr[tile] = upward_grad
        up_bias_grad_ref[0] = column_sum(upward_grad.astype(f32))
        accumulate(third, total, dot(upward_grad, up_scr[slot], 1, 1))

    @pl.when(third == tiles - 1)
    def _():
        unit, scale = norm_parts(grad_ref[...])
        normed_grad = total[...]
        residual_grad = cot_scr[...].astype(f32) + norm_back(
            normed_grad, unit, scale, gain_ref[...]
        )
        low = residual_grad.astype(bf16)
        grad_ref[...] = residual_grad
        low_scr[...] = low
        att_scr[...] = dot(proj_other_ref[...], low, 1, 1).astype(bf16)
        att_far.start()
        att_grad_ref[...] = dot(proj_ref[...], low, 1, 1).astype(bf16)
        vector_ref[0:1] = column_sum(normed_grad * unit)
        vector_ref[1:2] = column_sum(normed_grad)
        vector_ref[2:3] = column_sum(low.astype(f32))

    fourth = step - 3 * tiles

    @pl.when((fourth >= 0) & (fourth < tiles))
    def _():
        value = dot(n_scr[...], slope_scr[clamp(fourth, tiles - 1)], 0, 0)
        send_gradient(value, keep_ref.at[0])

    @pl.when(fourth == tiles)
    def _():
        send_gradient(dot(low_scr[...], att_ref[...], 0, 1), keep_ref.at[0])

    @pl.when(fourth == tiles + 1)
    def _():
        send_gradient(dot(low_scr[...], att_other_ref[...], 0, 1), keep_ref.at[0])

    @pl.when((second + 1 >= 0) & (second + 1 < tiles))
    def _():
        to_core(second + 1).wait_recv()
        arrive(second + 1).start()

    @pl.when((second >= 0) & (second < tiles))
    def _():
        arrive(second).wait()
        tile = clamp(second, tiles - 1)
        fold(
            keep_ring.at[tile],
            arrived.at[tile % 2],
            x_side,
            keep_x_ref.at[0],
            outgoing_x.at[tile],
        )
        to_x(tile).start()

    @pl.when(step == last)
    def _():
        gather_qkv.wait(2)
        items = got_hbm.shape[0]
        to_core(items - 2).wait_send()
        to_core(items - 1).wait_send()
        for index in range(tiles, items):
            to_core(index).wait_recv()
        for index in range(tiles):
            to_x(index).wait()
        att_far.wait()
        out_near.wait()
        out_far.wait()


def feed_forward(
    count,
    att_mine,
    att_other,
    proj,
    proj_other,
    proj_bias,
    gain,
    shift,
    down_bias,
    up_bias,
    patches,
    cot,
    up,
    up_other,
    down,
    down_part,
    qkv,
):
    tokens, width = patches.shape
    half = tokens // 2
    columns = proj.shape[0]
    tiles = 2 * up.shape[1] // FF_TILE
    items = 2 * tiles + 2
    row = once((1, width))
    left = (width // count, FF_TILE)
    tile = lambda first, lead, size: pl.BlockSpec(
        (1,) + lead, lambda i: (clamp(i - first, size - 1),) + (0,) * len(lead)
    )
    vmem = pltpu.VMEM
    dma = lambda *shape: pltpu.SemaphoreType.DMA(shape)
    return pl.pallas_call(
        feed_kernel,
        grid=(4 * tiles + 2,),
        in_specs=[
            once((columns, half)),
            once((columns, half)),
            once(proj.shape),
            once(proj.shape),
            row,
            row,
            row,
            row,
            once(up_bias.shape),
            HBM,
            HBM,
            HBM,
            HBM,
            HBM,
            HBM,
            HBM,
        ],
        out_specs=(
            once((half, width)),
            once((columns, half)),
            once((columns, half)),
            once((4, width)),
            tile(2 * tiles, (1, FF_TILE), tiles),
            tile(tiles, (count // 4,) + left, tiles),
            tile(3 * tiles, (count // 2,) + left, tiles + 2),
            HBM,
            HBM,
            HBM,
            HBM,
            HBM,
            HBM,
        ),
        out_shape=(
            jax.ShapeDtypeStruct((half, width), f32),
            jax.ShapeDtypeStruct((columns, half), bf16),
            jax.ShapeDtypeStruct((columns, half), bf16),
            jax.ShapeDtypeStruct((4, width), f32),
            jax.ShapeDtypeStruct((tiles, 1, FF_TILE), f32),
            jax.ShapeDtypeStruct((tiles, count // 4) + left, bf16),
            jax.ShapeDtypeStruct((tiles + 2, count // 2) + left, bf16),
            jax.ShapeDtypeStruct((tokens, width), bf16),
            jax.ShapeDtypeStruct((columns, half), bf16),
            jax.ShapeDtypeStruct((items, count // 2) + left, bf16),
            jax.ShapeDtypeStruct((tiles, count // 4) + left, bf16),
            jax.ShapeDtypeStruct(down.shape, bf16),
            jax.ShapeDtypeStruct(qkv.shape, bf16),
        ),
        input_output_aliases={14: 11},
        scratch_shapes=[
            vmem((half, width), bf16),
            vmem((half, width), bf16),
            vmem((half, width), bf16),
            vmem((half, width), f32),
            vmem((tiles, half, FF_TILE), bf16),
            vmem((tiles, half, FF_TILE), bf16),
            vmem((2, width, FF_TILE), bf16),
            vmem((2, FF_TILE, width), bf16),
            vmem((half, width), bf16),
            vmem((width, FF_TILE), f32),
            vmem((tiles, count // 2) + left, bf16),
            vmem((2, count // 2) + left, bf16),
            vmem((2, count // 2) + left, bf16),
            vmem((tiles, count // 4) + left, bf16),
            dma(2),
            dma(2),
            dma(2),
            pltpu.SemaphoreType.DMA,
            dma(2),
            dma(2),
            dma(2),
            dma(items),
            dma(2),
            dma(tiles),
            dma(tiles),
            dma(2, Gather.COPIES),
            dma(2, Gather.COPIES),
        ],
        compiler_params=params(2),
        cost_estimate=pl.CostEstimate(
            flops=12 * half * width * tiles * FF_TILE,
            bytes_accessed=60_000_000,
            transcendentals=half * tiles * FF_TILE,
        ),
        name="feed_forward",
    )(
        att_mine,
        att_other,
        proj,
        proj_other,
        proj_bias[None, :],
        gain[None, :],
        shift[None, :],
        down_bias[None, :],
        up_bias,
        patches,
        cot,
        up,
        up_other,
        down,
        down_part,
        qkv,
    )


class Chain:
    def __init__(self, keep, got, bits, scratch):
        self.keep, self.got, self.bits, self.scratch = keep, got, list(bits), list(scratch)
        self.last = None

    def step(self):
        if self.last is not None:
            self.copy(*self.last).wait()
            self.last = None
        if not self.bits:
            return
        bit = self.bits.pop(0)
        keep, send, got, sem = self.scratch.pop(0)
        fold(self.keep, self.got, partner_of(bit)[1], keep, send)
        self.last = (bit, send, got, sem)
        self.copy(*self.last).start()
        self.keep, self.got = keep, got

    def copy(self, bit, send, got, sem):
        return remote(send, got, sem.at[0], sem.at[1], partner_of(bit)[0])

    def result(self, tile):
        value = self.keep[tile, 0].astype(f32)
        return value if self.got is None else value + self.got[tile, 0].astype(f32)


def input_back_kernel(
    bits,
    mine_ref,
    other_ref,
    w_ref,
    w_other_ref,
    gain_ref,
    vector_ref,
    down_sum,
    up_sum,
    qkv_keep,
    qkv_got,
    x_hbm,
    grad_hbm,
    total_ref,
    down_ref,
    up_ref,
    proj_ref,
    qkv_ref,
    out_hbm,
    total,
    x_scr,
    grad_scr,
    out_scr,
    vector_send,
    vector_got,
    vector_scr,
    vector_next,
    side_send,
    side_got,
    load_sem,
    store_sem,
    row_send,
    row_recv,
    vector_sem,
    side_sem,
    *scratch,
):
    step = pl.program_id(0)
    half, width = total.shape
    side = lax.axis_index("tensor")
    peer = {"tensor": 1 - side}
    mine = pl.ds(pl.multiple_of(side * half, 16), half)
    loads = [
        pltpu.make_async_copy(x_hbm.at[mine], x_scr, load_sem.at[0]),
        pltpu.make_async_copy(grad_hbm, grad_scr, load_sem.at[1]),
    ]
    stages, rest = [], list(scratch)
    for first in (4, 3, 1):
        stages.append([tuple(rest[4 * i : 4 * i + 4]) for i in range(bits - first)])
        rest = rest[4 * (bits - first) :]
    down = Chain(down_sum, None, range(4, bits), stages[0])
    up = Chain(up_sum, None, range(3, bits), stages[1])
    qkv = Chain(qkv_keep, qkv_got, range(1, bits), stages[2])
    tiles = down_ref.shape[1] // FF_TILE
    early_down = not down.bits

    def side_copy(at, size):
        return remote(
            side_send.at[pl.ds(at, size)],
            side_got.at[pl.ds(at, size)],
            side_sem.at[2 * (at // tiles)],
            side_sem.at[2 * (at // tiles) + 1],
            peer,
        )

    def other_side(parts, at):
        for number, part in enumerate(parts):
            side_send[at + number] = part.astype(bf16)
        copy = side_copy(at, len(parts))
        copy.start()
        return copy

    @pl.when(step == 0)
    def _():
        for load in loads:
            load.start()
        greet([peer] + [partner_of(bit)[0] for bit in range(bits)])
        if early_down:
            other_side([down.result(tiles + i) for i in range(tiles)], 0)
        for chain in (up, qkv, down):
            chain.step()

    heads = other_ref.shape[0]
    left = other_ref[...].reshape(heads * HEAD_DIM, half)
    term = dot(mine_ref[0], w_ref[0], 0, 1) + dot(left, w_other_ref[0], 0, 1)
    accumulate(step, total, term)

    @pl.when(step == pl.num_programs(0) - 1)
    def _():
        for load in loads:
            load.wait()
        gain = gain_ref[...]
        sums = [0.0, 0.0]
        begin, blocks = 0, []
        for block, rows in enumerate((half // 32 * 16, half - half // 32 * 16)):
            at = pl.ds(begin, rows)
            unit, scale = norm_parts(x_scr[at].astype(f32))
            normed_grad = total[at]
            out = grad_scr[at] + norm_back(normed_grad, unit, scale, gain)
            out_scr[at] = out.astype(bf16)
            sums = [sums[0] + column_sum(normed_grad * unit), sums[1] + column_sum(normed_grad)]
            target = out_hbm.at[pl.ds(pl.multiple_of(side * half + begin, 16), rows)]
            blocks.append(
                (
                    remote(out_scr.at[at], target, row_send.at[block], row_recv.at[block], peer),
                    pltpu.make_async_copy(out_scr.at[at], target, store_sem.at[block]),
                )
            )
            begin += rows

        both = vector_got.shape[1]
        vector_send[:, : 2 * width] = jnp.concatenate(sums, axis=1)
        vector_send[:, 2 * width :] = vector_ref[1:2, 2 * width : both]
        vector_copy = remote(vector_send, vector_got, vector_sem.at[0], vector_sem.at[1], peer)
        vector_copy.start()
        for far, near in blocks:
            far.start()
            near.start()

        def add_vectors(bit):
            copy = remote(
                vector_scr,
                vector_next.at[bit],
                vector_sem.at[2 * bit + 2],
                vector_sem.at[2 * bit + 3],
                partner_of(bit)[0],
            )
            copy.start()
            copy.wait()
            vector_scr[...] += vector_next[bit]

        qkv.step()
        vector_copy.wait()
        vector_scr[:, :both] = vector_got[...] + jnp.concatenate(
            sums + [vector_ref[0:1, 2 * width : both]], axis=1
        )
        vector_scr[:, both:] = vector_ref[0:1, both:]
        vector_bits = list(range(bits))
        while down.bits or up.bits or qkv.bits:
            if vector_bits:
                add_vectors(vector_bits.pop(0))
            for chain in (qkv, up, down):
                chain.step()
        if early_down:
            down_copy = side_copy(0, tiles)
        else:
            down.step()
            down_copy = other_side([down.result(tiles + i) for i in range(tiles)], 0)
        up.step()
        up_copy = other_side(
            [up.result(tiles + i) for i in range(tiles)] + [up.result(2 * tiles + 1)], tiles
        )
        for bit in vector_bits:
            add_vectors(bit)
        total_ref[...] = vector_scr[...]
        qkv.step()
        for part in range(3):
            qkv_ref[part] = qkv.result(part)
        down_copy.wait()
        for tile in range(tiles):
            at = pl.ds(tile * FF_TILE, FF_TILE)
            down_ref[:, at] = down.result(tile) + side_got[tile].astype(f32)
        up_copy.wait()
        for tile in range(tiles):
            at = pl.ds(tile * FF_TILE, FF_TILE)
            up_ref[:, at] = up.result(tile) + side_got[tiles + tile].astype(f32)
        proj_ref[...] = up.result(2 * tiles) + side_got[2 * tiles].astype(f32)
        for far, near in blocks:
            near.wait()
            far.wait()


def input_backward(
    count,
    mine,
    other,
    weight,
    weight_other,
    gain,
    vectors,
    down_sum,
    up_sum,
    qkv_keep,
    qkv_got,
    patches,
    residual_grad,
):
    tokens, width = patches.shape
    half = tokens // 2
    columns = mine.shape[1]
    heads = other.shape[0]
    bits = count.bit_length() - 1
    rows = width // count
    tiles = heads // 2
    size = vectors.shape[1]
    both = size - FF_TILE * 3
    vmem = pltpu.VMEM
    dma = lambda *shape: pltpu.SemaphoreType.DMA(shape)
    scratch = []
    for first, lead in ((4, heads), (3, heads + 2), (1, 3)):
        for bit in range(first, bits):
            shape = (lead, count >> (bit + 1), rows, FF_TILE)
            scratch += [vmem(shape, bf16), vmem(shape, bf16), vmem(shape, bf16), dma(2)]
    return pl.pallas_call(
        functools.partial(input_back_kernel, bits),
        grid=(3,),
        in_specs=[
            pl.BlockSpec((1, columns, half), lambda i: (i, 0, 0)),
            pl.BlockSpec((heads, None, HEAD_DIM, half), lambda i: (0, i, 0, 0)),
            pl.BlockSpec((1, width, columns), lambda i: (i, 0, 0)),
            pl.BlockSpec((1, width, columns), lambda i: (i, 0, 0)),
            once((1, width)),
            once(vectors.shape),
            once(down_sum.shape),
            once(up_sum.shape),
            once(qkv_keep.shape),
            once(qkv_got.shape),
            HBM,
            HBM,
        ],
        out_specs=(
            once((1, size)),
            once((rows, tiles * FF_TILE)),
            once((rows, tiles * FF_TILE)),
            once((rows, columns)),
            once((3, rows, columns)),
            HBM,
        ),
        out_shape=(
            jax.ShapeDtypeStruct((1, size), f32),
            jax.ShapeDtypeStruct((rows, tiles * FF_TILE), f32),
            jax.ShapeDtypeStruct((rows, tiles * FF_TILE), f32),
            jax.ShapeDtypeStruct((rows, columns), f32),
            jax.ShapeDtypeStruct((3, rows, columns), f32),
            jax.ShapeDtypeStruct((tokens, width), bf16),
        ),
        scratch_shapes=[
            vmem((half, width), f32),
            vmem((half, width), bf16),
            vmem((half, width), f32),
            vmem((half, width), bf16),
            vmem((1, both), f32),
            vmem((1, both), f32),
            vmem((1, size), f32),
            vmem((bits, 1, size), f32),
            vmem((2 * tiles + 1, rows, FF_TILE), bf16),
            vmem((2 * tiles + 1, rows, FF_TILE), bf16),
            dma(2),
            dma(2),
            dma(2),
            dma(2),
            dma(2 * bits + 2),
            dma(4),
        ]
        + scratch,
        compiler_params=params(1),
        cost_estimate=pl.CostEstimate(
            flops=12 * half * width * columns, bytes_accessed=20_000_000, transcendentals=0
        ),
        name="input_backward",
    )(
        mine,
        other,
        weight,
        weight_other,
        gain[None, :],
        vectors,
        down_sum,
        up_sum,
        qkv_keep,
        qkv_got,
        patches,
        residual_grad,
    )


def over_tensor(value):
    return lax.ppermute(value, "tensor", [(0, 1), (1, 0)])


def on_device(
    count,
    patches,
    cotangent,
    clip_lengths,
    attn_gain,
    attn_shift,
    qkv_weight,
    qkv_bias,
    proj_weight,
    proj_bias,
    mlp_gain,
    mlp_shift,
    up_weight,
    up_bias,
    down_weight,
    down_bias,
):
    tokens, width = patches.shape
    local_width = proj_weight.shape[0]

    qkv_parts = jnp.transpose(qkv_weight, (1, 0, 2))
    up_biases = jnp.concatenate([up_bias, over_tensor(up_bias)]).reshape(-1, 1, FF_TILE)

    clip_len = clip_lengths[0, 0]
    cosine, sine = rotary_angles(jnp.arange(tokens, dtype=jnp.int32) % clip_len)
    query_mask, key_mask = clip_masks(clip_len, tokens)
    (
        normed,
        qkv,
        attended,
        att_mine,
        totals,
        weights,
        att_other,
        proj_other,
        up_other,
        down_part,
    ) = attend_forward(
        patches,
        attn_gain,
        attn_shift,
        qkv_parts,
        qkv_bias,
        cosine,
        sine,
        query_mask,
        key_mask,
        proj_weight,
        up_weight,
        down_weight,
    )
    (
        residual_grad,
        att_grad_mine,
        att_grad_send,
        vectors,
        up_bias_grad,
        down_keep,
        up_keep,
        block_out,
        att_grad_got,
        up_got,
        down_got,
        _,
        qkv_other,
    ) = feed_forward(
        count,
        att_mine,
        att_other,
        proj_weight,
        proj_other,
        proj_bias,
        mlp_gain,
        mlp_shift,
        down_bias,
        up_biases,
        patches,
        cotangent,
        up_weight,
        up_other,
        down_weight,
        down_part,
        qkv_parts,
    )
    (
        mixed_mine,
        qkv_keep,
        qkv_bias_grad,
        down_sum,
        up_sum,
        mixed_other,
        qkv_got,
        _,
    ) = attend_backward(
        count,
        weights,
        qkv,
        attended,
        totals,
        att_grad_mine,
        att_grad_send,
        att_grad_got,
        cosine,
        sine,
        normed,
        down_keep,
        down_got,
        up_keep,
        up_got,
    )

    hidden = up_bias.shape[0]
    vectors = vectors.reshape(1, -1)
    up_bias_grad = up_bias_grad.reshape(2, hidden)
    ends = jnp.zeros((2, 2 * width), f32)
    vectors = jnp.concatenate(
        [
            ends,
            jnp.concatenate([vectors, vectors]),
            up_bias_grad,
            jnp.concatenate([qkv_bias_grad.reshape(1, -1)] * 2),
        ],
        axis=1,
    )
    vectors, down_grad, up_grad, proj_grad, qkv_grad, patch_grad = input_backward(
        count,
        mixed_mine,
        mixed_other,
        qkv_parts,
        qkv_other,
        attn_gain,
        vectors,
        down_sum,
        up_sum,
        qkv_keep,
        qkv_got,
        patches,
        residual_grad,
    )
    part = lambda first, size=width: vectors[0, first : first + size]
    return (
        block_out,
        patch_grad,
        part(0),
        part(width),
        jnp.transpose(qkv_grad, (1, 0, 2)),
        part(6 * width + hidden, 3 * local_width).reshape(3, local_width),
        proj_grad.T,
        part(4 * width),
        part(2 * width),
        part(3 * width),
        up_grad,
        part(6 * width, hidden),
        down_grad.T,
        part(5 * width),
    )


def solution(mesh):
    return jax.shard_map(
        functools.partial(on_device, mesh.shape["dp"]),
        mesh=mesh,
        in_specs=(
            P("dp", None),
            P("dp", None),
            P("dp", None),
            P(),
            P(),
            P(None, None, "tensor"),
            P(None, "tensor"),
            P("tensor", None),
            P(),
            P(),
            P(),
            P(None, "tensor"),
            P("tensor"),
            P("tensor", None),
            P(),
        ),
        out_specs=(
            P("dp", None),
            P("dp", None),
            P(),
            P(),
            P("dp", None, "tensor"),
            P(None, "tensor"),
            P("tensor", "dp"),
            P(),
            P(),
            P(),
            P("dp", "tensor"),
            P("tensor"),
            P("tensor", "dp"),
            P(),
        ),
        check_vma=False,
    )
```

```python
import functools
import math

import jax
import jax.numpy as jnp
from jax import lax
from jax.experimental import pallas as pl
from jax.experimental.pallas import tpu as pltpu
from jax.sharding import PartitionSpec as P

HEAD_DIM = 64
HALF_DIM = HEAD_DIM // 2
GRID = 14
IMG = 196
EPS = 1e-06
SCALING = HEAD_DIM ** (-0.5)
LOG2E = math.log2(math.e)
KEY_CHUNKS = 2
MASK_ROWS = 16
END_WIDTH = 256
RESULT_STEPS = 7
ONES_ROWS = 16
FF_TILE = 512
FORBIDDEN = -1e30
VMEM_LIMIT = 62 * 1024 * 1024

MESH = pl.DeviceIdType.MESH

bf16 = jnp.bfloat16
f32 = jnp.float32


def dot(left, right, left_dim, right_dim):
    return lax.dot_general(
        left, right, (((left_dim,), (right_dim,)), ((), ())), preferred_element_type=f32
    )


def rotary_angles(offsets):
    pair_count = HALF_DIM
    side_pairs = pair_count * 11 // 32
    time_pairs = pair_count - 2 * side_pairs
    pair_index = jnp.arange(pair_count, dtype=jnp.int32)
    time_pair = pair_index < time_pairs
    height_pair = (pair_index >= time_pairs) & (pair_index < time_pairs + side_pairs)
    group_begin = jnp.where(
        time_pair, 0, jnp.where(height_pair, time_pairs, time_pairs + side_pairs)
    )
    group_size = jnp.where(time_pair, time_pairs, side_pairs)
    inverse = jnp.power(
        10000.0, -(pair_index - group_begin).astype(f32) / group_size.astype(f32)
    )
    frame_place = (offsets // IMG).astype(f32)
    row_place = (offsets % IMG // GRID).astype(f32)
    column_place = (offsets % GRID).astype(f32)
    position = jnp.where(
        time_pair[:, None],
        frame_place[None, :],
        jnp.where(height_pair[:, None], row_place[None, :], column_place[None, :]),
    )
    angles = position * inverse[:, None]
    return (jnp.cos(angles), jnp.sin(angles))


def params(collective_id=None):
    if collective_id is None:
        return pltpu.CompilerParams(vmem_limit_bytes=VMEM_LIMIT)
    return pltpu.CompilerParams(
        vmem_limit_bytes=VMEM_LIMIT, collective_id=collective_id, has_side_effects=True
    )


def greet(partners):
    barrier = pltpu.get_barrier_semaphore()
    for partner in partners:
        pl.semaphore_signal(barrier, inc=1, device_id=partner, device_id_type=MESH)
    pl.semaphore_wait(barrier, len(partners))


def partner_of(bit):
    index = lax.axis_index("dp")
    mine = (index // (1 << bit)) % 2
    return {"dp": index + (1 << bit) * (1 - 2 * mine)}, mine


def fold(keep, got, mine, next_keep, next_send):
    lead = (slice(None),) * (len(keep.shape) - 3)
    for pair in range(keep.shape[-3] // 2):
        for ref, odd in ((next_keep, mine), (next_send, 1 - mine)):
            at = lead + (2 * pair + odd,)
            value = keep[at]
            if got is not None:
                value = value.astype(f32) + got[at].astype(f32)
            ref[lead + (pair,)] = value.astype(bf16)


def remote(source, target, send_sem, recv_sem, partner):
    return pltpu.make_async_remote_copy(
        src_ref=source,
        dst_ref=target,
        send_sem=send_sem,
        recv_sem=recv_sem,
        device_id=partner,
        device_id_type=MESH,
    )


def whole_block(shape, **kwargs):
    return pl.BlockSpec(shape, lambda *_: (0,) * len(shape), **kwargs)


def once(shape):
    return whole_block(shape, pipeline_mode=pl.Buffered(1))


HBM = pl.BlockSpec(memory_space=pl.ANY)


def clamp(value, last):
    return jnp.minimum(jnp.maximum(value, 0), last)


def norm_parts(values):
    centre = values - jnp.mean(values, axis=1, keepdims=True)
    spread = jnp.mean(centre * centre, axis=1, keepdims=True)
    scale = lax.rsqrt(spread + EPS)
    return centre * scale, scale


def norm_back(grad, unit, scale, gain):
    c = grad * gain
    mean = jnp.mean(c, axis=1, keepdims=True)
    along = jnp.mean(c * unit, axis=1, keepdims=True)
    return scale * (c - mean - unit * along)


def column_sum(values):
    return jnp.sum(values, axis=0, keepdims=True)


def clip_masks(clip_len, tokens):
    token = jnp.arange(tokens, dtype=jnp.int32)[None, :] // IMG
    row = jnp.arange(MASK_ROWS, dtype=jnp.int32)[:, None]
    same = token == row
    images = clip_len < tokens
    forbid = images & jnp.logical_not(same) & (row < tokens // IMG)
    return jnp.where(forbid, FORBIDDEN, 0.0).astype(bf16), same.astype(bf16)


class Gather:
    STAGES = ((0,), (1, 2), (3, 4, 5, 6), (7, 8, 9, 10))
    COPIES = 11
    ROUTES = (
        (None, 0, 0, None),
        (0, 0, 0, 2),
        (1, 0, 0, 1),
        (0, 0, 0, 1),
        (0, 0, 1, 1),
        (1, 0, 0, 2),
        (1, 1, 0, 2),
        (None, 0, 0, 0),
        (None, 1, 0, 0),
        (None, 0, 1, 0),
        (None, 1, 1, 0),
    )

    def __init__(self, weight, other, send_sem, recv_sem):
        self.weight, self.other = weight, other
        self.send_sem, self.recv_sem = send_sem, recv_sem

    def place(self, x, z):
        core, mine_x, mine_z = (partner_of(bit)[1] for bit in range(3))
        x = mine_x + x * (1 - 2 * mine_x)
        return core + 2 * x + 4 * (mine_z + z * (1 - 2 * mine_z)), 8

    def copy(self, number):
        half, x, z, bit = self.ROUTES[number]
        index, parts = self.place(x, z)
        rows = self.other.shape[-2] // parts
        begin = index * rows
        if half is not None:
            rows //= 2
            begin = begin + half * rows
        at = (slice(None),) * (len(self.other.shape) - 2)
        at = at + (pl.ds(pl.multiple_of(begin, rows), rows),)
        source = self.weight if number == 0 else self.other
        return remote(
            source.at[at],
            self.other.at[at],
            self.send_sem.at[number],
            self.recv_sem.at[number],
            {"tensor": 1 - lax.axis_index("tensor")} if bit is None else partner_of(bit)[0],
        )

    def start(self, stage):
        for number in self.STAGES[stage]:
            self.copy(number).start()

    def wait(self, stage):
        for number in self.STAGES[stage]:
            self.copy(number).wait()

    def advance(self, stage):
        self.wait(stage - 1)
        self.start(stage)


class GatherZ(Gather):
    STAGES = ((0,), (1,), (2, 3))
    ROUTES = ((None, 0, 0, None), (None, 0, 0, 2), (None, 0, 0, 0), (None, 0, 1, 0))

    def place(self, x, z):
        core, mine_z = partner_of(0)[1], partner_of(2)[1]
        return core + 2 * (mine_z + z * (1 - 2 * mine_z)), 4


def neighbours():
    return [{"tensor": 1 - lax.axis_index("tensor")}] + [partner_of(bit)[0] for bit in range(3)]


def attend_kernel(
    x_ref,
    gain_ref,
    shift_ref,
    w_ref,
    b_ref,
    cos_ref,
    sin_ref,
    qm_ref,
    km_ref,
    up_bias_ref,
    proj_hbm,
    up_hbm,
    down_hbm,
    normed_ref,
    qkv_ref,
    att_ref,
    mine_ref,
    factor_ref,
    biases_ref,
    e_hbm,
    other_hbm,
    proj_other,
    up_other,
    down_other,
    k_scr,
    s_scr,
    e_scr,
    outgoing,
    bias_got,
    e_sem,
    bias_sem,
    send_sem,
    recv_sem,
    gather_send,
    gather_recv,
):
    step, last = pl.program_id(0), pl.num_programs(0) - 1
    tokens, width = x_ref.shape
    half = tokens // 2
    chunk = tokens // KEY_CHUNKS
    heads = e_hbm.shape[0]
    side = lax.axis_index("tensor")
    peer = {"tensor": 1 - side}
    proj = Gather(proj_hbm, proj_other, gather_send.at[0], gather_recv.at[0])
    up = Gather(up_hbm, up_other, gather_send.at[1], gather_recv.at[1])
    down = Gather(down_hbm, down_other, gather_send.at[2], gather_recv.at[2])

    bias_far = remote(up_bias_ref, bias_got, bias_sem.at[0], bias_sem.at[1], peer)

    @pl.when(step == 0)
    def _():
        greet(neighbours())
        bias_far.start()
        proj.start(0)
        up.start(0)
        unit, _ = norm_parts(x_ref[...].astype(f32))
        normed_ref[:width] = (unit * gain_ref[...] + shift_ref[...]).astype(bf16).T
        normed_ref[width:] = jnp.ones((ONES_ROWS, tokens), bf16)

    for at, weight, stage in (
        (2, proj, 1),
        (3, down, 0),
        (4, proj, 2),
        (4, up, 1),
        (6, proj, 3),
        (6, up, 2),
        (9, up, 3),
    ):

        @pl.when(step == at)
        def _():
            if stage:
                weight.advance(stage)
            else:
                weight.start(stage)

    @pl.when(step < 3)
    def _():
        rows = w_ref.shape[2]
        bias = jnp.broadcast_to(b_ref[pl.ds(step, 1), :], (8, rows)).T[:, :1]
        mixed = dot(w_ref[0], normed_ref[:width], 0, 0) + bias

        @pl.when(step < 2)
        def _():
            cosine, sine = cos_ref[...], sin_ref[...]
            for begin in range(0, rows, HEAD_DIM):
                middle, end = begin + HALF_DIM, begin + HEAD_DIM
                low, high = mixed[begin:middle], mixed[middle:end]
                qkv_ref[step, begin:middle, :] = (low * cosine - high * sine).astype(bf16)
                qkv_ref[step, middle:end, :] = (high * cosine + low * sine).astype(bf16)

        @pl.when(step == 2)
        def _():
            qkv_ref[step] = mixed.astype(bf16)

    head = step - 3
    slot = head % 2

    def store(index, part):
        at = pl.ds(part * chunk, chunk)
        return pltpu.make_async_copy(
            e_scr.at[index % 2, at], e_hbm.at[index, at], e_sem.at[index % 2, part]
        )

    def exchange(index):
        at = pl.ds(pl.multiple_of(index * HEAD_DIM, HEAD_DIM), HEAD_DIM)
        return remote(
            outgoing.at[index],
            other_hbm.at[at],
            send_sem.at[index],
            recv_sem.at[index],
            peer,
        )

    @pl.when(head >= 2)
    def _():
        for part in range(KEY_CHUNKS):
            store(head - 2, part).wait()

    @pl.when(head >= 0)
    def _():
        at = pl.ds(pl.multiple_of(clamp(head, heads - 1) * HEAD_DIM, HEAD_DIM), HEAD_DIM)
        queries = jnp.concatenate([qkv_ref[0, at], qm_ref[...]], axis=0)
        k_scr[...] = jnp.concatenate([qkv_ref[1, at], km_ref[...]], axis=0).T
        values = jnp.concatenate([qkv_ref[2, at], jnp.ones((16, tokens), bf16)], axis=0)
        top, out, tops = None, None, []
        s_scr[0] = dot(k_scr[:chunk], queries, 1, 0)
        for part in range(KEY_CHUNKS):
            begin, end = part * chunk, (part + 1) * chunk
            if part + 1 < KEY_CHUNKS:
                s_scr[(part + 1) % 2] = dot(k_scr[end : end + chunk], queries, 1, 0)
            scores = s_scr[part % 2]
            here = jnp.max(scores, axis=0, keepdims=True)
            new_top = here if top is None else jnp.maximum(top, here)
            weights = jnp.exp2((scores - new_top) * (SCALING * LOG2E)).astype(bf16)
            e_scr[slot, begin:end] = weights
            store(head, part).start()
            term = dot(values[:, begin:end], weights, 1, 0)
            if out is None:
                out = term
            else:
                out = out * jnp.exp2((top - new_top) * (SCALING * LOG2E)) + term
            top = new_top
            tops.append(top)
        scale = 1.0 / out[HEAD_DIM : HEAD_DIM + 1]
        for part in range(KEY_CHUNKS):
            factor_ref[0, part : part + 1] = scale * jnp.exp2(
                (tops[part] - top) * (SCALING * LOG2E)
            )
        attended = out[:HEAD_DIM] * scale
        att_ref[...] = attended.astype(bf16)
        left, right = attended[:, :half], attended[:, half:]
        mine_ref[...] = jnp.where(side == 0, left, right).astype(bf16)
        outgoing[clamp(head, heads - 1)] = jnp.where(side == 0, right, left).astype(bf16)
        exchange(head).start()

    @pl.when(step == last)
    def _():
        for back in (2, 1):
            for part in range(KEY_CHUNKS):
                store(heads - back, part).wait()
        for index in range(heads):
            exchange(index).wait()
        bias_far.wait()
        biases_ref[: bias_got.shape[0]] = up_bias_ref[...]
        biases_ref[bias_got.shape[0] :] = bias_got[...]
        for weight, stage in ((proj, 3), (up, 3), (down, 0)):
            weight.wait(stage)


def attend_forward(
    patches,
    gain,
    shift,
    weight,
    bias,
    cosine,
    sine,
    query_mask,
    key_mask,
    up_bias,
    proj,
    up,
    down,
):
    tokens, width = patches.shape
    columns = weight.shape[2]
    heads = columns // HEAD_DIM
    half = tokens // 2
    head = lambda i: clamp(i - 3, heads - 1)
    tiles = up_bias.shape[0] // FF_TILE
    vmem = pltpu.VMEM
    dma = lambda *shape: pltpu.SemaphoreType.DMA(shape)
    return pl.pallas_call(
        attend_kernel,
        grid=(3 + heads,),
        out_shape=(
            jax.ShapeDtypeStruct((width + ONES_ROWS, tokens), bf16),
            jax.ShapeDtypeStruct((3, columns, tokens), bf16),
            jax.ShapeDtypeStruct((columns, tokens), bf16),
            jax.ShapeDtypeStruct((columns, half), bf16),
            jax.ShapeDtypeStruct((heads, KEY_CHUNKS, tokens), f32),
            jax.ShapeDtypeStruct((2 * tiles, 1, FF_TILE), f32),
            jax.ShapeDtypeStruct((heads, tokens, tokens), bf16),
            jax.ShapeDtypeStruct((columns, half), bf16),
            jax.ShapeDtypeStruct(proj.shape, bf16),
            jax.ShapeDtypeStruct(up.shape, bf16),
            jax.ShapeDtypeStruct(down.shape, bf16),
        ),
        in_specs=[
            once((tokens, width)),
            once((1, width)),
            once((1, width)),
            pl.BlockSpec((1, width, columns), lambda i: (clamp(i, 2), 0, 0)),
            once((3, columns)),
            once(cosine.shape),
            once(sine.shape),
            once(query_mask.shape),
            once(key_mask.shape),
            once((tiles, 1, FF_TILE)),
            HBM,
            HBM,
            HBM,
        ],
        out_specs=(
            once((width + ONES_ROWS, tokens)),
            once((3, columns, tokens)),
            pl.BlockSpec((HEAD_DIM, tokens), lambda i: (head(i), 0)),
            pl.BlockSpec((HEAD_DIM, half), lambda i: (head(i), 0)),
            pl.BlockSpec((1, KEY_CHUNKS, tokens), lambda i: (head(i), 0, 0)),
            once((2 * tiles, 1, FF_TILE)),
            HBM,
            HBM,
            HBM,
            HBM,
            HBM,
        ),
        scratch_shapes=[
            vmem((tokens, HEAD_DIM + MASK_ROWS), bf16),
            vmem((2, tokens // KEY_CHUNKS, tokens), f32),
            vmem((2, tokens, tokens), bf16),
            vmem((heads, HEAD_DIM, half), bf16),
            vmem((tiles, 1, FF_TILE), f32),
            dma(2, KEY_CHUNKS),
            dma(2),
            dma(heads),
            dma(heads),
            dma(3, Gather.COPIES),
            dma(3, Gather.COPIES),
        ],
        compiler_params=params(3),
        cost_estimate=pl.CostEstimate(
            flops=6 * tokens * width * columns + 16 * heads * tokens * tokens * HEAD_DIM,
            bytes_accessed=60_000_000,
            transcendentals=heads * tokens * tokens,
        ),
        name="attend_forward",
    )(
        patches,
        gain[None, :],
        shift[None, :],
        weight,
        bias,
        cosine,
        sine,
        query_mask,
        key_mask,
        up_bias.reshape(tiles, 1, FF_TILE),
        proj,
        up,
        down,
    )


def attend_back_kernel(
    e_ref,
    q_ref,
    k_ref,
    v_ref,
    out_ref,
    total_ref,
    att_grad_ref,
    cos_ref,
    sin_ref,
    normed_ref,
    down_keep_ref,
    down_got_ref,
    up_keep_ref,
    up_got_ref,
    att_send_hbm,
    _,
    mine_ref,
    keep_ref,
    sum_ref,
    down_sum_ref,
    up_sum_ref,
    proj_sum_ref,
    other_ref,
    other_end_ref,
    got_ref,
    att_got_hbm,
    att_scr,
    up_scr,
    up_low,
    value_scr,
    v_scr,
    score_grad,
    turned,
    pair_scr,
    outgoing,
    outgoing_end,
    grad,
    outgoing_core,
    down_scr,
    down_last,
    up_first,
    up_last,
    send_sem,
    recv_sem,
    end_sem,
    core_send,
    core_recv,
    down_sem,
    down_last_sem,
    up_sem,
    up_last_sem,
    att_sem,
    att_load_sem,
):
    head, heads = pl.program_id(0), pl.num_programs(0)
    tokens = q_ref.shape[2]
    half = tokens // 2
    side = lax.axis_index("tensor")
    peer = {"tensor": 1 - side}
    core_partner, core = partner_of(0)
    slot = head % 2
    def exchange(index):
        return remote(
            outgoing.at[index % 4],
            other_ref.at[index],
            send_sem.at[index % 4],
            recv_sem.at[index],
            peer,
        )

    end_far = remote(outgoing_end, other_end_ref, end_sem.at[0], end_sem.at[1], peer)
    lanes = half // 128 * 128
    end_width = outgoing_end.shape[1] // heads

    def to_core(pair):
        at = pl.ds(pl.multiple_of(pair * 2 * HEAD_DIM, 2 * HEAD_DIM), 2 * HEAD_DIM)
        return remote(
            outgoing_core.at[pair % 2],
            got_ref.at[:, :, :, at],
            core_send.at[pair % 2],
            core_recv.at[pair],
            core_partner,
        )

    def hop(buffers, sems, pair, bit):
        at = pl.ds(2 * pair, 2)
        return remote(
            buffers.at[1, at],
            buffers.at[2, at],
            sems.at[0, pair],
            sems.at[1, pair],
            partner_of(bit)[0],
        )

    def start(keep, got, buffers, sems, pair, bit):
        at = pl.ds(2 * pair, 2)
        fold(keep, got, partner_of(bit)[1], buffers.at[0, at], buffers.at[1, at])
        hop(buffers, sems, pair, bit).start()

    def relay(source, source_sems, source_bit, buffers, sems, pair, bit):
        hop(source, source_sems, pair, source_bit).wait_recv()
        at = pl.ds(2 * pair, 2)
        start(source.at[0, at], source.at[2, at], buffers, sems, pair, bit)

    down_pairs, up_pairs = down_scr.shape[1] // 2, up_last.shape[1] // 2
    behind = heads - up_pairs

    late_heads = pl.ds(att_got_hbm.shape[0] // 2, att_got_hbm.shape[0] // 2)
    att_far = remote(
        att_send_hbm.at[late_heads], att_got_hbm.at[late_heads], att_sem.at[0], att_sem.at[1], peer
    )

    def att_load(index):
        at = pl.ds(pl.multiple_of(index * HEAD_DIM, HEAD_DIM), HEAD_DIM)
        return pltpu.make_async_copy(
            att_got_hbm.at[at], att_scr.at[index % 2], att_load_sem.at[index % 2]
        )

    @pl.when(head == 0)
    def _():
        att_load(0).start()
        greet(neighbours() + [partner_of(3)[0]])
        att_far.start()

    @pl.when(head >= 4)
    def _():
        exchange(head - 4).wait_send()

    @pl.when(head <= up_pairs)
    def _():
        start(up_keep_ref, up_got_ref, up_first, up_sem, head, 1)

    @pl.when(head < down_pairs)
    def _():
        start(down_keep_ref, down_got_ref, down_scr, down_sem, head, 2)

    @pl.when(head >= heads - down_pairs)
    def _():
        relay(
            down_scr, down_sem, 2, down_last, down_last_sem, head - (heads - down_pairs), 3
        )

    @pl.when(head >= behind)
    def _():
        relay(up_first, up_sem, 1, up_last, up_last_sem, head - behind, 2)

    @pl.when(head + 1 == heads // 2)
    def _():
        att_far.wait_recv()

    @pl.when(head + 1 < heads)
    def _():
        att_load(head + 1).start()

    att_load(head).wait()
    chunks = total_ref.shape[1]
    chunk = tokens // chunks
    att_mine, att_other = att_grad_ref[...].astype(f32), att_scr[slot].astype(f32)
    up_scr[:, :half] = jnp.where(side == 0, att_mine, att_other)
    up_scr[:, half:] = jnp.where(side == 0, att_other, att_mine)
    attended = out_ref[...].astype(f32)
    centre = []
    for part in range(chunks):
        up_low[part] = (up_scr[...] * total_ref[0, part : part + 1]).astype(bf16)
        centre.append(column_sum(up_low[part].astype(f32) * attended))
    v_scr[...] = v_ref[0].T
    cosine, sine = cos_ref[...], sin_ref[...]

    ends = {}

    def store(part, low, high):
        for row, value in ((0, low), (HALF_DIM, high)):
            left, right = value[:, :half], value[:, half:]
            mine_ref[part, row : row + HALF_DIM] = jnp.where(side == 0, left, right).astype(bf16)
            theirs = jnp.where(side == 0, right, left)
            outgoing[head % 4, part, row : row + HALF_DIM] = theirs[:, :lanes].astype(bf16)
            ends[part, row // HALF_DIM] = theirs[:, lanes:]
            begin = pl.multiple_of(part * 2 * HEAD_DIM + slot * HEAD_DIM + row, HALF_DIM)
            pair_scr[pl.ds(begin, HALF_DIM)] = value.astype(bf16)

    def unrotated(part, grad):
        low, high = grad[:HALF_DIM] * SCALING, grad[HALF_DIM:] * SCALING
        store(part, low * cosine + high * sine, high * cosine - low * sine)

    for part in range(chunks):
        at = slice(part * chunk, (part + 1) * chunk)
        value_scr[:, at] = dot(up_low[part], e_ref[0, at], 1, 1)
        prob_grad = dot(v_scr[at], up_low[part], 1, 0)
        score_grad[at] = (e_ref[0, at].astype(f32) * (prob_grad - centre[part])).astype(bf16)
    store(2, value_scr[:HALF_DIM], value_scr[HALF_DIM:])
    unrotated(0, dot(k_ref[0], score_grad[...], 1, 0))
    turned[...] = score_grad[...].T
    unrotated(1, dot(q_ref[0], turned[...], 1, 0))
    exchange(head).start()
    end = jnp.concatenate([ends[part, row] for part in range(3) for row in range(2)], axis=0)
    end = jnp.concatenate([end, jnp.zeros((end_width - end.shape[0], end.shape[1]), f32)], axis=0)
    begin = pl.multiple_of(head * end_width, end_width)
    outgoing_end[:, pl.ds(begin, end_width)] = end.T.astype(bf16)

    @pl.when(slot == 1)
    def _():
        pair = head // 2
        width = grad.shape[0] - ONES_ROWS
        grad[...] = dot(normed_ref[...], pair_scr[...], 1, 1)

        @pl.when(pair >= 2)
        def _():
            to_core(pair - 2).wait_send()

        for part in range(3):
            lanes = pl.ds(part * 2 * HEAD_DIM, 2 * HEAD_DIM)
            split_rows(
                grad.at[:, lanes], keep_ref.at[part], outgoing_core.at[pair % 2, part], core
            )
            sum_ref[part : part + 1] = grad[width : width + 1, lanes]
        to_core(pair).start()

    @pl.when(head == heads - 1)
    def _():
        end_far.start()
        for back in range(4):
            exchange(heads - 1 - back).wait_send()
        for back in range(2):
            to_core(heads // 2 - 1 - back).wait_send()
        for index in range(other_ref.shape[0] // 2):
            to_core(index).wait_recv()
        for pair in range(down_pairs):
            hop(down_scr, down_sem, pair, 2).wait_send()
            hop(down_last, down_last_sem, pair, 3).wait()
        down_sum_ref[...] = down_last[0].astype(f32) + down_last[2].astype(f32)
        for pair in range(up_pairs):
            hop(up_first, up_sem, pair, 1).wait_send()
            hop(up_last, up_last_sem, pair, 2).wait()
        up_sum_ref[...] = (up_last[0].astype(f32) + up_last[2].astype(f32)).astype(bf16)
        hop(up_first, up_sem, up_pairs, 1).wait()
        at = pl.ds(2 * up_pairs, 2)
        proj_sum_ref[...] = (up_first[0, at].astype(f32) + up_first[2, at].astype(f32)).astype(bf16)
        att_far.wait_send()
        end_far.wait()
        for index in range(other_ref.shape[0]):
            exchange(index).wait_recv()


def attend_backward(
    count,
    weights,
    qkv,
    attended,
    totals,
    att_grad,
    att_send,
    att_got,
    cosine,
    sine,
    normed,
    down_keep,
    down_got,
    up_keep,
    up_got,
):
    tokens = qkv.shape[2]
    half = tokens // 2
    heads = weights.shape[0]
    columns = heads * HEAD_DIM
    width = normed.shape[0] - ONES_ROWS
    rows = width // count
    split = (3, count // 2, rows)
    blocks = lambda bits: (count >> bits, rows, FF_TILE)
    pair = lambda lead, first, last: pl.BlockSpec(
        (2,) + lead, lambda i: (first + clamp(i, last), 0, 0, 0)
    )
    block = lambda part: pl.BlockSpec((1, HEAD_DIM, tokens), lambda i: (part, i, 0))
    half_block = pl.BlockSpec((HEAD_DIM, half), lambda i: (i, 0))
    lanes = half // 128 * 128
    pair_block = pl.BlockSpec(split + (2 * HEAD_DIM,), lambda i: (0, 0, 0, i // 2))
    vmem = pltpu.VMEM
    dma = lambda *shape: pltpu.SemaphoreType.DMA(shape)
    return pl.pallas_call(
        attend_back_kernel,
        grid=(heads,),
        out_shape=(
            jax.ShapeDtypeStruct((3, columns, half), bf16),
            jax.ShapeDtypeStruct(split + (columns,), bf16),
            jax.ShapeDtypeStruct((3, columns), f32),
            jax.ShapeDtypeStruct((heads,) + blocks(4), f32),
            jax.ShapeDtypeStruct((heads,) + blocks(3), bf16),
            jax.ShapeDtypeStruct((2,) + blocks(2), bf16),
            jax.ShapeDtypeStruct((heads, 3, HEAD_DIM, lanes), bf16),
            jax.ShapeDtypeStruct((half - lanes, heads * END_WIDTH), bf16),
            jax.ShapeDtypeStruct(split + (columns,), bf16),
            jax.ShapeDtypeStruct(att_got.shape, bf16),
        ),
        input_output_aliases={15: 9},
        in_specs=[
            pl.BlockSpec((1, tokens, tokens), lambda i: (i, 0, 0)),
            block(0),
            block(1),
            block(2),
            pl.BlockSpec((HEAD_DIM, tokens), lambda i: (i, 0)),
            pl.BlockSpec((1, totals.shape[1], tokens), lambda i: (i, 0, 0)),
            half_block,
            once(cosine.shape),
            once(sine.shape),
            once(normed.shape),
            pair(blocks(2), 0, heads // 2 - 1),
            pair(blocks(2), 0, heads // 2 - 1),
            pair(blocks(1), 0, heads // 2),
            pair(blocks(1), heads // 2, heads // 2),
            HBM,
            HBM,
        ],
        out_specs=(
            pl.BlockSpec((3, HEAD_DIM, half), lambda i: (0, i, 0)),
            pair_block,
            pl.BlockSpec((3, 2 * HEAD_DIM), lambda i: (0, i // 2)),
            once((heads,) + blocks(4)),
            once((heads,) + blocks(3)),
            once((2,) + blocks(2)),
            HBM,
            HBM,
            HBM,
            HBM,
        ),
        scratch_shapes=[
            vmem((2, HEAD_DIM, half), bf16),
            vmem((HEAD_DIM, tokens), f32),
            vmem((totals.shape[1], HEAD_DIM, tokens), bf16),
            vmem((HEAD_DIM, tokens), f32),
            vmem((tokens, HEAD_DIM), bf16),
            vmem((tokens, tokens), bf16),
            vmem((tokens, tokens), bf16),
            vmem((6 * HEAD_DIM, tokens), bf16),
            vmem((4, 3, HEAD_DIM, lanes), bf16),
            vmem((half - lanes, heads * END_WIDTH), bf16),
            vmem((width + ONES_ROWS, 6 * HEAD_DIM), f32),
            vmem((2,) + split + (2 * HEAD_DIM,), bf16),
            vmem((3, heads) + blocks(3), bf16),
            vmem((3, heads) + blocks(4), bf16),
            vmem((3, heads + 2) + blocks(2), bf16),
            vmem((3, heads) + blocks(3), bf16),
            dma(4),
            dma(heads),
            dma(2),
            dma(2),
            dma(heads // 2),
            dma(2, heads // 2),
            dma(2, heads // 2),
            dma(2, heads // 2 + 1),
            dma(2, heads // 2),
            dma(2),
            dma(2),
        ],
        compiler_params=params(0),
        cost_estimate=pl.CostEstimate(
            flops=32 * heads * tokens * tokens * HEAD_DIM,
            bytes_accessed=2 * heads * tokens * tokens,
            transcendentals=0,
        ),
        name="attend_backward",
    )(
        weights,
        qkv,
        qkv,
        qkv,
        attended,
        totals,
        att_grad,
        cosine,
        sine,
        normed,
        down_keep,
        down_got,
        up_keep,
        up_got,
        att_send,
        att_got,
    )


def normal_parts(value):
    a = jnp.abs(value)
    t = 1.0 / (1.0 + (0.3275911 / math.sqrt(2.0)) * a)
    bell = jnp.exp2(value * value * (-0.5 * LOG2E))
    c = [0.5 * x for x in (0.254829592, -0.284496736, 1.421413741, -1.453152027, 1.061405429)]
    tail = ((((c[4] * t + c[3]) * t + c[2]) * t + c[1]) * t + c[0]) * t * bell
    return jnp.where(value >= 0, 1.0 - tail, tail), bell * (1.0 / math.sqrt(2.0 * math.pi))


def split_rows(grad, keep_ref, send_ref, core):
    count, rows = keep_ref.shape[:2]
    for pair in range(count):
        for ref, odd in ((keep_ref, core), (send_ref, 1 - core)):
            begin = pl.multiple_of((2 * pair + odd) * rows, rows)
            ref[pair] = grad[pl.ds(begin, rows), :].astype(bf16)


def accumulate(step, total, term):
    @pl.when(step == 0)
    def _():
        total[...] = term

    @pl.when(step > 0)
    def _():
        total[...] += term


def feed_kernel(
    att_ref,
    att_other_ref,
    proj_ref,
    proj_other_ref,
    proj_bias_ref,
    gain_ref,
    shift_ref,
    down_bias_ref,
    up_bias_ref,
    patch_hbm,
    cot_hbm,
    up_hbm,
    up_other_hbm,
    down_hbm,
    _,
    qkv_hbm,
    grad_ref,
    att_grad_ref,
    att_scr,
    vector_ref,
    up_bias_grad_ref,
    keep_x_ref,
    keep_ref,
    out_hbm,
    att_got_hbm,
    got_hbm,
    got_x_hbm,
    down_other_hbm,
    qkv_other_hbm,
    n_scr,
    cot_scr,
    out_scr,
    total,
    act_scr,
    slope_scr,
    up_scr,
    down_scr,
    low_scr,
    grad_scr,
    keep_ring,
    outgoing,
    arrived,
    outgoing_x,
    load_sem,
    up_sem,
    down_sem,
    store_sem,
    row_sem,
    att_sem,
    send_sem,
    recv_sem,
    arrive_sem,
    send_x_sem,
    recv_x_sem,
    gather_send,
    gather_recv,
):
    step, last = pl.program_id(0), pl.num_programs(0) - 1
    tiles = act_scr.shape[0]
    half_tiles = tiles // 2
    half = n_scr.shape[0]
    side = lax.axis_index("tensor")
    peer = {"tensor": 1 - side}
    core_partner, core = partner_of(0)
    x_partner, x_side = partner_of(1)
    mine = pl.ds(pl.multiple_of(side * half, 16), half)
    gather_down = Gather(down_hbm, down_other_hbm, gather_send.at[0], gather_recv.at[0])
    gather_qkv = GatherZ(qkv_hbm, qkv_other_hbm, gather_send.at[1], gather_recv.at[1])
    patch_load = pltpu.make_async_copy(patch_hbm.at[mine], out_scr, load_sem.at[0])
    cot_load = pltpu.make_async_copy(cot_hbm.at[mine], cot_scr, load_sem.at[1])
    out_near = pltpu.make_async_copy(out_scr, out_hbm.at[mine], store_sem)
    out_far = remote(out_scr, out_hbm.at[mine], row_sem.at[0], row_sem.at[1], peer)
    early_heads = pl.ds(0, att_scr.shape[0] // 2)
    att_far = remote(
        att_scr.at[early_heads], att_got_hbm.at[early_heads], att_sem.at[0], att_sem.at[1], peer
    )

    def load_up(tile, act):
        for begin, source in ((0, up_hbm), (half_tiles, up_other_hbm)):

            @pl.when((tile >= begin) & (tile < begin + half_tiles))
            def _():
                at = pl.ds(pl.multiple_of((tile - begin) * FF_TILE, FF_TILE), FF_TILE)
                copy = pltpu.make_async_copy(
                    source.at[:, at], up_scr.at[tile % 2], up_sem.at[tile % 2]
                )
                getattr(copy, act)()

    def load_down(tile, act):
        for begin, source in ((0, down_hbm), (half_tiles, down_other_hbm)):

            @pl.when((tile >= begin) & (tile < begin + half_tiles))
            def _():
                at = pl.ds(pl.multiple_of((tile - begin) * FF_TILE, FF_TILE), FF_TILE)
                copy = pltpu.make_async_copy(
                    source.at[at], down_scr.at[tile % 2], down_sem.at[tile % 2]
                )
                getattr(copy, act)()

    def to_core(index):
        return remote(
            outgoing.at[index % 2],
            got_hbm.at[index],
            send_sem.at[index % 2],
            recv_sem.at[index],
            core_partner,
        )

    def to_x(index):
        return remote(
            outgoing_x.at[index],
            got_x_hbm.at[index],
            send_x_sem.at[index],
            recv_x_sem.at[index],
            x_partner,
        )

    def arrive(index):
        return pltpu.make_async_copy(
            got_hbm.at[index], arrived.at[index % 2], arrive_sem.at[index % 2]
        )

    @pl.when(step == 0)
    def _():
        patch_load.start()
        cot_load.start()
        load_up(0, "start")
        greet(neighbours())
        gather_down.start(1)
        gather_qkv.start(0)
        branch = dot(att_ref[...], proj_ref[...], 0, 0).astype(bf16).astype(f32)
        other = dot(att_other_ref[...], proj_other_ref[...], 0, 0).astype(bf16).astype(f32)
        patch_load.wait()
        residual = out_scr[...].astype(f32) + (branch + other + proj_bias_ref[...])
        grad_ref[...] = residual
        unit, _ = norm_parts(residual)
        n_scr[...] = (unit * gain_ref[...] + shift_ref[...]).astype(bf16)
        cot_load.wait()
        vector_ref[3:4] = column_sum(cot_scr[...].astype(f32))

    slot = step % 2

    for at, weight, stage in (
        (half_tiles - 1, gather_down, 2),
        (tiles, gather_down, 3),
        (tiles + 4, gather_qkv, 1),
        (2 * tiles + 4, gather_qkv, 2),
    ):

        @pl.when(step == at)
        def _():
            weight.advance(stage)

    @pl.when(step == tiles + half_tiles - 1)
    def _():
        gather_down.wait(3)

    first, second, third = step, step - tiles, step - 2 * tiles

    @pl.when(first + 1 < tiles)
    def _():
        load_up(first + 1, "start")

    @pl.when(first < tiles)
    def _():
        load_up(first, "wait")

    @pl.when((second + 1 >= 0) & (second + 1 < tiles))
    def _():
        load_down(second + 1, "start")

    @pl.when((second >= 0) & (second < tiles))
    def _():
        load_down(second, "wait")

    @pl.when((third + 1 >= 0) & (third + 1 < tiles))
    def _():
        load_up(third + 1, "start")
        load_down(third + 1, "start")

    @pl.when((third >= 0) & (third < tiles))
    def _():
        load_up(third, "wait")
        load_down(third, "wait")

    item = jnp.where(step < tiles, step, step - 2 * tiles)
    sends = (step < tiles) | (step >= 3 * tiles)

    @pl.when(sends & (item >= 2))
    def _():
        to_core(item - 2).wait_send()

    def send_gradient(value, keep):
        grad_scr[...] = value
        split_rows(grad_scr, keep, outgoing.at[slot], core)
        to_core(item).start()

    @pl.when(first < tiles)
    def _():
        upward = dot(n_scr[...], up_scr[slot], 1, 0) + up_bias_ref[clamp(first, tiles - 1)]
        share, density = normal_parts(upward)
        activated = (upward * share).astype(bf16)
        act_scr[clamp(first, tiles - 1)] = activated
        slope_scr[clamp(first, tiles - 1)] = (share + upward * density).astype(bf16)
        send_gradient(dot(cot_scr[...], activated, 0, 0), keep_ring.at[clamp(first, tiles - 1)])

    @pl.when((second >= 0) & (second < tiles))
    def _():
        accumulate(second, total, dot(act_scr[clamp(second, tiles - 1)], down_scr[slot], 1, 0))

    @pl.when(second == tiles - 1)
    def _():
        out_scr[...] = (grad_ref[...] + (total[...] + down_bias_ref[...])).astype(bf16)
        out_near.start()
        out_far.start()

    @pl.when((third >= 0) & (third < tiles))
    def _():
        tile = clamp(third, tiles - 1)
        act_grad = dot(cot_scr[...], down_scr[slot], 1, 1)
        upward_grad = (act_grad * slope_scr[tile].astype(f32)).astype(bf16)
        slope_scr[tile] = upward_grad
        up_bias_grad_ref[0] = column_sum(upward_grad.astype(f32))
        accumulate(third, total, dot(upward_grad, up_scr[slot], 1, 1))

    @pl.when(third == tiles - 1)
    def _():
        unit, scale = norm_parts(grad_ref[...])
        normed_grad = total[...]
        residual_grad = cot_scr[...].astype(f32) + norm_back(
            normed_grad, unit, scale, gain_ref[...]
        )
        low = residual_grad.astype(bf16)
        grad_ref[...] = residual_grad
        low_scr[...] = low
        att_scr[...] = dot(proj_other_ref[...], low, 1, 1).astype(bf16)
        att_far.start()
        att_grad_ref[...] = dot(proj_ref[...], low, 1, 1).astype(bf16)
        vector_ref[0:1] = column_sum(normed_grad * unit)
        vector_ref[1:2] = column_sum(normed_grad)
        vector_ref[2:3] = column_sum(low.astype(f32))

    fourth = step - 3 * tiles

    @pl.when((fourth >= 0) & (fourth < tiles))
    def _():
        value = dot(n_scr[...], slope_scr[clamp(fourth, tiles - 1)], 0, 0)
        send_gradient(value, keep_ref.at[0])

    @pl.when(fourth == tiles)
    def _():
        send_gradient(dot(low_scr[...], att_ref[...], 0, 1), keep_ref.at[0])

    @pl.when(fourth == tiles + 1)
    def _():
        send_gradient(dot(low_scr[...], att_other_ref[...], 0, 1), keep_ref.at[0])

    @pl.when((second + 1 >= 0) & (second + 1 < tiles))
    def _():
        to_core(second + 1).wait_recv()
        arrive(second + 1).start()

    @pl.when((second >= 0) & (second < tiles))
    def _():
        arrive(second).wait()
        tile = clamp(second, tiles - 1)
        fold(
            keep_ring.at[tile],
            arrived.at[tile % 2],
            x_side,
            keep_x_ref.at[0],
            outgoing_x.at[tile],
        )
        to_x(tile).start()

    @pl.when(step == last)
    def _():
        gather_qkv.wait(2)
        items = got_hbm.shape[0] - 1
        to_core(items - 2).wait_send()
        to_core(items - 1).wait_send()
        for index in range(tiles, items):
            to_core(index).wait_recv()
        for index in range(tiles):
            to_x(index).wait()
        att_far.wait()
        out_near.wait()
        out_far.wait()


def feed_forward(
    count,
    att_mine,
    att_other,
    proj,
    proj_other,
    proj_bias,
    gain,
    shift,
    down_bias,
    up_bias,
    patches,
    cot,
    up,
    up_other,
    down,
    down_part,
    qkv,
):
    tokens, width = patches.shape
    half = tokens // 2
    columns = proj.shape[0]
    tiles = 2 * up.shape[1] // FF_TILE
    items = 2 * tiles + 2
    row = once((1, width))
    left = (width // count, FF_TILE)
    tile = lambda first, lead, size: pl.BlockSpec(
        (1,) + lead, lambda i: (clamp(i - first, size - 1),) + (0,) * len(lead)
    )
    vmem = pltpu.VMEM
    dma = lambda *shape: pltpu.SemaphoreType.DMA(shape)
    return pl.pallas_call(
        feed_kernel,
        grid=(4 * tiles + 2,),
        in_specs=[
            once((columns, half)),
            once((columns, half)),
            once(proj.shape),
            once(proj.shape),
            row,
            row,
            row,
            row,
            once(up_bias.shape),
            HBM,
            HBM,
            HBM,
            HBM,
            HBM,
            HBM,
            HBM,
        ],
        out_specs=(
            once((half, width)),
            once((columns, half)),
            once((columns, half)),
            once((4, width)),
            tile(2 * tiles, (1, FF_TILE), tiles),
            tile(tiles, (count // 4,) + left, tiles),
            tile(3 * tiles, (count // 2,) + left, tiles + 2),
            HBM,
            HBM,
            HBM,
            HBM,
            HBM,
            HBM,
        ),
        out_shape=(
            jax.ShapeDtypeStruct((half, width), f32),
            jax.ShapeDtypeStruct((columns, half), bf16),
            jax.ShapeDtypeStruct((columns, half), bf16),
            jax.ShapeDtypeStruct((4, width), f32),
            jax.ShapeDtypeStruct((tiles, 1, FF_TILE), f32),
            jax.ShapeDtypeStruct((tiles, count // 4) + left, bf16),
            jax.ShapeDtypeStruct((tiles + 2, count // 2) + left, bf16),
            jax.ShapeDtypeStruct((tokens, width), bf16),
            jax.ShapeDtypeStruct((columns, half), bf16),
            jax.ShapeDtypeStruct((items + 1, count // 2) + left, bf16),
            jax.ShapeDtypeStruct((tiles, count // 4) + left, bf16),
            jax.ShapeDtypeStruct(down.shape, bf16),
            jax.ShapeDtypeStruct(qkv.shape, bf16),
        ),
        input_output_aliases={14: 11},
        scratch_shapes=[
            vmem((half, width), bf16),
            vmem((half, width), bf16),
            vmem((half, width), bf16),
            vmem((half, width), f32),
            vmem((tiles, half, FF_TILE), bf16),
            vmem((tiles, half, FF_TILE), bf16),
            vmem((2, width, FF_TILE), bf16),
            vmem((2, FF_TILE, width), bf16),
            vmem((half, width), bf16),
            vmem((width, FF_TILE), f32),
            vmem((tiles, count // 2) + left, bf16),
            vmem((2, count // 2) + left, bf16),
            vmem((2, count // 2) + left, bf16),
            vmem((tiles, count // 4) + left, bf16),
            dma(2),
            dma(2),
            dma(2),
            pltpu.SemaphoreType.DMA,
            dma(2),
            dma(2),
            dma(2),
            dma(items),
            dma(2),
            dma(tiles),
            dma(tiles),
            dma(2, Gather.COPIES),
            dma(2, Gather.COPIES),
        ],
        compiler_params=params(2),
        cost_estimate=pl.CostEstimate(
            flops=12 * half * width * tiles * FF_TILE,
            bytes_accessed=60_000_000,
            transcendentals=half * tiles * FF_TILE,
        ),
        name="feed_forward",
    )(
        att_mine,
        att_other,
        proj,
        proj_other,
        proj_bias[None, :],
        gain[None, :],
        shift[None, :],
        down_bias[None, :],
        up_bias,
        patches,
        cot,
        up,
        up_other,
        down,
        down_part,
        qkv,
    )


class Chain:
    def __init__(self, keep, got, bits, scratch):
        self.keep, self.got, self.bits, self.scratch = keep, got, list(bits), list(scratch)
        self.last = None

    def step(self):
        if self.last is not None:
            self.copy(*self.last).wait()
            self.last = None
        if not self.bits:
            return
        bit = self.bits.pop(0)
        keep, send, got, sem = self.scratch.pop(0)
        fold(self.keep, self.got, partner_of(bit)[1], keep, send)
        self.last = (bit, send, got, sem)
        self.copy(*self.last).start()
        self.keep, self.got = keep, got

    def finish(self):
        while self.bits:
            self.step()
        self.step()

    def copy(self, bit, send, got, sem):
        return remote(send, got, sem.at[0], sem.at[1], partner_of(bit)[0])

    def result(self, tile):
        value = self.keep[tile, 0].astype(f32)
        return value if self.got is None else value + self.got[tile, 0].astype(f32)


def input_back_kernel(
    bits,
    mine_ref,
    other_ref,
    other_end_ref,
    w_ref,
    w_other_ref,
    gain_ref,
    vector_ref,
    down_sum,
    up_sum,
    proj_sum,
    qkv_keep,
    qkv_got,
    x_hbm,
    grad_hbm,
    total_ref,
    down_ref,
    up_ref,
    proj_ref,
    qkv_ref,
    out_hbm,
    total,
    x_scr,
    grad_scr,
    out_scr,
    vector_send,
    vector_got,
    vector_scr,
    vector_next,
    side_send,
    side_got,
    load_sem,
    store_sem,
    row_send,
    row_recv,
    vector_sem,
    side_sem,
    *scratch,
):
    step = pl.program_id(0)
    half, width = grad_scr.shape
    side = lax.axis_index("tensor")
    peer = {"tensor": 1 - side}
    mine = pl.ds(pl.multiple_of(side * half, 16), half)
    loads = [
        pltpu.make_async_copy(x_hbm.at[mine], x_scr, load_sem.at[0]),
        pltpu.make_async_copy(grad_hbm, grad_scr, load_sem.at[1]),
    ]
    stages, rest = [], list(scratch)
    for first in (4, 3, 2, 1):
        stages.append([tuple(rest[4 * i : 4 * i + 4]) for i in range(bits - first)])
        rest = rest[4 * (bits - first) :]
    down = Chain(down_sum, None, range(4, bits), stages[0])
    up = Chain(up_sum, None, range(3, bits), stages[1])
    proj = Chain(proj_sum, None, range(2, bits), stages[2])
    qkv = Chain(qkv_keep, qkv_got, range(1, bits), stages[3])
    tiles = down_ref.shape[1] // FF_TILE
    early_down = not down.bits

    def side_copy(at, size):
        return remote(
            side_send.at[pl.ds(at, size)],
            side_got.at[pl.ds(at, size)],
            side_sem.at[2 * (at // tiles)],
            side_sem.at[2 * (at // tiles) + 1],
            peer,
        )

    def other_side(parts, at):
        for number, part in enumerate(parts):
            side_send[at + number] = part.astype(bf16)
        side_copy(at, len(parts)).start()

    @pl.when(step == 0)
    def _():
        for load in loads:
            load.start()
        greet([peer] + [partner_of(bit)[0] for bit in range(bits)])
        if early_down:
            other_side([down.result(tiles + i) for i in range(tiles)], 0)
        for chain in (qkv, up, proj, down):
            chain.step()

    heads = other_ref.shape[0]
    lanes = other_ref.shape[3]
    gain = gain_ref[...]
    first_rows = lanes // 256 * 128
    blocks = ((0, first_rows), (first_rows, half))

    def rows_copies(block):
        begin, end = blocks[block]
        at = pl.ds(begin, end - begin)
        target = out_hbm.at[pl.ds(pl.multiple_of(side * half + begin, 16), end - begin)]
        return (
            remote(out_scr.at[at], target, row_send.at[block], row_recv.at[block], peer),
            pltpu.make_async_copy(out_scr.at[at], target, store_sem.at[block]),
        )

    def input_rows(block):
        begin, end = blocks[block]
        whole_end = min(end, lanes)
        near, far = 0.0, 0.0
        for part in range(3):
            near = near + dot(mine_ref[part, :, begin:end], w_ref[part], 0, 1)
            left = other_ref[:, part, :, begin:whole_end].reshape(
                heads * HEAD_DIM, whole_end - begin
            )
            far = far + dot(left, w_other_ref[part], 0, 1)
        if end > lanes:
            rest = 0.0
            for part in range(3):
                ends = [
                    other_end_ref[:, pl.ds(head * END_WIDTH, 3 * HEAD_DIM)][
                        :, part * HEAD_DIM : (part + 1) * HEAD_DIM
                    ]
                    for head in range(heads)
                ]
                rest = rest + dot(jnp.concatenate(ends, axis=1), w_other_ref[part], 1, 1)
            far = jnp.concatenate([far, rest], axis=0)
        normed_grad = near + far
        unit, scale = norm_parts(x_scr[begin:end].astype(f32))
        out = grad_scr[begin:end] + norm_back(normed_grad, unit, scale, gain)
        out_scr[begin:end] = out.astype(bf16)
        return column_sum(normed_grad * unit), column_sum(normed_grad)

    @pl.when(step == 0)
    def _():
        for load in loads:
            load.wait()
        sums = input_rows(0)
        for copy in rows_copies(0):
            copy.start()
        total[0:1], total[1:2] = sums

    @pl.when(step == 1)
    def _():
        sums = input_rows(1)
        sums = [total[number : number + 1] + sums[number] for number in range(2)]

        both = vector_got.shape[1]
        vector_send[:, : 2 * width] = jnp.concatenate(sums, axis=1)
        vector_send[:, 2 * width :] = vector_ref[1:2, 2 * width : both]
        vector_copy = remote(vector_send, vector_got, vector_sem.at[0], vector_sem.at[1], peer)
        vector_copy.start()
        for copy in rows_copies(1):
            copy.start()

        vector_bits = list(range(bits))

        def add_vectors():
            if not vector_bits:
                return
            bit = vector_bits.pop(0)
            copy = remote(
                vector_scr,
                vector_next.at[bit],
                vector_sem.at[2 * bit + 2],
                vector_sem.at[2 * bit + 3],
                partner_of(bit)[0],
            )
            copy.start()
            copy.wait()
            vector_scr[...] += vector_next[bit]

        qkv.step()
        while proj.bits:
            proj.step()
        vector_copy.wait()
        vector_scr[:, :both] = vector_got[...] + jnp.concatenate(
            sums + [vector_ref[0:1, 2 * width : both]], axis=1
        )
        vector_scr[:, both:] = vector_ref[0:1, both:]
        add_vectors()
        if not early_down:
            down.finish()
            other_side([down.result(tiles + i) for i in range(tiles)], 0)
        up.finish()
        other_side([up.result(tiles + i) for i in range(tiles)], tiles)
        add_vectors()
        qkv.step()
        proj.step()
        other_side([proj.result(1)], 2 * tiles)
        add_vectors()
        side_copy(0, tiles).wait()
        for tile in range(tiles):
            at = pl.ds(tile * FF_TILE, FF_TILE)
            down_ref[:, at] = down.result(tile) + side_got[tile].astype(f32)
        qkv.finish()
        for part in range(3):
            qkv_ref[part] = qkv.result(part)
        while vector_bits:
            add_vectors()
        total_ref[...] = vector_scr[...]
        side_copy(tiles, tiles).wait()
        for tile in range(tiles):
            at = pl.ds(tile * FF_TILE, FF_TILE)
            up_ref[:, at] = up.result(tile) + side_got[tiles + tile].astype(f32)
        side_copy(2 * tiles, 1).wait()
        proj_ref[...] = proj.result(0) + side_got[2 * tiles].astype(f32)
        for block in range(2):
            far, near = rows_copies(block)
            near.wait()
            far.wait()


def input_backward(
    count,
    mine,
    other,
    other_end,
    weight,
    weight_other,
    gain,
    vectors,
    down_sum,
    up_sum,
    proj_sum,
    qkv_keep,
    qkv_got,
    patches,
    residual_grad,
):
    tokens, width = patches.shape
    half = tokens // 2
    columns = mine.shape[1]
    heads = other.shape[0]
    bits = count.bit_length() - 1
    rows = width // count
    tiles = heads // 2
    size = vectors.shape[1]
    both = size - FF_TILE * 3
    vmem = pltpu.VMEM
    dma = lambda *shape: pltpu.SemaphoreType.DMA(shape)
    scratch = []
    for first, lead in ((4, heads), (3, heads), (2, 2), (1, 3)):
        for bit in range(first, bits):
            shape = (lead, count >> (bit + 1), rows, FF_TILE)
            scratch += [vmem(shape, bf16), vmem(shape, bf16), vmem(shape, bf16), dma(2)]
    return pl.pallas_call(
        functools.partial(input_back_kernel, bits),
        grid=(2,),
        in_specs=[
            once(mine.shape),
            once(other.shape),
            once(other_end.shape),
            once(weight.shape),
            once(weight_other.shape),
            once((1, width)),
            once(vectors.shape),
            once(down_sum.shape),
            once(up_sum.shape),
            once(proj_sum.shape),
            once(qkv_keep.shape),
            once(qkv_got.shape),
            HBM,
            HBM,
        ],
        out_specs=(
            once((1, size)),
            once((rows, tiles * FF_TILE)),
            once((rows, tiles * FF_TILE)),
            once((rows, columns)),
            once((3, rows, columns)),
            HBM,
        ),
        out_shape=(
            jax.ShapeDtypeStruct((1, size), f32),
            jax.ShapeDtypeStruct((rows, tiles * FF_TILE), f32),
            jax.ShapeDtypeStruct((rows, tiles * FF_TILE), f32),
            jax.ShapeDtypeStruct((rows, columns), f32),
            jax.ShapeDtypeStruct((3, rows, columns), f32),
            jax.ShapeDtypeStruct((tokens, width), bf16),
        ),
        scratch_shapes=[
            vmem((2, width), f32),
            vmem((half, width), bf16),
            vmem((half, width), f32),
            vmem((half, width), bf16),
            vmem((1, both), f32),
            vmem((1, both), f32),
            vmem((1, size), f32),
            vmem((bits, 1, size), f32),
            vmem((2 * tiles + 1, rows, FF_TILE), bf16),
            vmem((2 * tiles + 1, rows, FF_TILE), bf16),
            dma(2),
            dma(2),
            dma(2),
            dma(2),
            dma(2 * bits + 2),
            dma(6),
        ]
        + scratch,
        compiler_params=params(1),
        cost_estimate=pl.CostEstimate(
            flops=12 * half * width * columns, bytes_accessed=20_000_000, transcendentals=0
        ),
        name="input_backward",
    )(
        mine,
        other,
        other_end,
        weight,
        weight_other,
        gain[None, :],
        vectors,
        down_sum,
        up_sum,
        proj_sum,
        qkv_keep,
        qkv_got,
        patches,
        residual_grad,
    )


def result_kernel(sizes, vector_ref, *refs):
    count = (len(refs) - len(sizes)) // 2
    sources, targets = refs[:count], refs[count : 2 * count]
    for source, target in zip(sources[-2:], targets[-2:]):
        target[...] = source[...]

    @pl.when(pl.program_id(0) == 0)
    def _():
        for source, target in zip(sources[:-2], targets[:-2]):
            target[...] = source[...]
        begin = 0
        for size, target in zip(sizes, refs[2 * count :]):
            for row in range(size // 128):
                at = pl.ds(begin + row * 128, 128)
                target[row : row + 1, :] = vector_ref[:, at]
            begin += size


def results(vectors, sizes, arrays, rows):
    step = rows[0].shape[0] // RESULT_STEPS
    long_block = pl.BlockSpec((step, rows[0].shape[1]), lambda i: (i, 0))
    specs = [once(x.shape) for x in arrays] + [long_block] * len(rows)
    shapes = [(size // 128, 128) for size in sizes]
    out = pl.pallas_call(
        functools.partial(result_kernel, sizes),
        grid=(RESULT_STEPS,),
        in_specs=[once(vectors.shape)] + specs,
        out_specs=specs + [once(x) for x in shapes],
        out_shape=[jax.ShapeDtypeStruct(x.shape, x.dtype) for x in list(arrays) + list(rows)]
        + [jax.ShapeDtypeStruct(x, f32) for x in shapes],
        compiler_params=params(),
        name="results",
    )(vectors, *arrays, *rows)
    count = len(arrays) + len(rows)
    return out[:count], [x.reshape(-1) for x in out[count:]]


def on_device(
    count,
    patches,
    cotangent,
    clip_lengths,
    attn_gain,
    attn_shift,
    qkv_weight,
    qkv_bias,
    proj_weight,
    proj_bias,
    mlp_gain,
    mlp_shift,
    up_weight,
    up_bias,
    down_weight,
    down_bias,
):
    tokens, width = patches.shape
    local_width = proj_weight.shape[0]

    qkv_parts = jnp.transpose(qkv_weight, (1, 0, 2))

    clip_len = clip_lengths[0, 0]
    cosine, sine = rotary_angles(jnp.arange(tokens, dtype=jnp.int32) % clip_len)
    query_mask, key_mask = clip_masks(clip_len, tokens)
    (
        normed,
        qkv,
        attended,
        att_mine,
        totals,
        up_biases,
        weights,
        att_other,
        proj_other,
        up_other,
        down_part,
    ) = attend_forward(
        patches,
        attn_gain,
        attn_shift,
        qkv_parts,
        qkv_bias,
        cosine,
        sine,
        query_mask,
        key_mask,
        up_bias,
        proj_weight,
        up_weight,
        down_weight,
    )
    (
        residual_grad,
        att_grad_mine,
        att_grad_send,
        vectors,
        up_bias_grad,
        down_keep,
        up_keep,
        block_out,
        att_grad_got,
        up_got,
        down_got,
        _,
        qkv_other,
    ) = feed_forward(
        count,
        att_mine,
        att_other,
        proj_weight,
        proj_other,
        proj_bias,
        mlp_gain,
        mlp_shift,
        down_bias,
        up_biases,
        patches,
        cotangent,
        up_weight,
        up_other,
        down_weight,
        down_part,
        qkv_parts,
    )
    (
        mixed_mine,
        qkv_keep,
        qkv_bias_grad,
        down_sum,
        up_sum,
        proj_sum,
        mixed_other,
        mixed_end,
        qkv_got,
        _,
    ) = attend_backward(
        count,
        weights,
        qkv,
        attended,
        totals,
        att_grad_mine,
        att_grad_send,
        att_grad_got,
        cosine,
        sine,
        normed,
        down_keep,
        down_got,
        up_keep,
        up_got,
    )

    hidden = up_bias.shape[0]
    vectors = vectors.reshape(1, -1)
    up_bias_grad = up_bias_grad.reshape(2, hidden)
    ends = jnp.zeros((2, 2 * width), f32)
    vectors = jnp.concatenate(
        [
            ends,
            jnp.concatenate([vectors, vectors]),
            up_bias_grad,
            jnp.concatenate([qkv_bias_grad.reshape(1, -1)] * 2),
        ],
        axis=1,
    )
    vectors, down_grad, up_grad, proj_grad, qkv_grad, patch_grad = input_backward(
        count,
        mixed_mine,
        mixed_other,
        mixed_end,
        qkv_parts,
        qkv_other,
        attn_gain,
        vectors,
        down_sum,
        up_sum,
        proj_sum,
        qkv_keep,
        qkv_got,
        patches,
        residual_grad,
    )
    sizes = [width] * 6 + [hidden, 3 * local_width]
    (down_grad, up_grad, proj_grad, qkv_grad, block_out, patch_grad), pieces = results(
        vectors, sizes, [down_grad, up_grad, proj_grad, qkv_grad], [block_out, patch_grad]
    )
    attn_gain_grad, attn_shift_grad, mlp_gain_grad, mlp_shift_grad = pieces[:4]
    proj_bias_grad, down_bias_grad, up_bias_grad, qkv_bias_grad = pieces[4:]
    return (
        block_out,
        patch_grad,
        attn_gain_grad,
        attn_shift_grad,
        jnp.transpose(qkv_grad, (1, 0, 2)),
        qkv_bias_grad.reshape(3, local_width),
        proj_grad.T,
        proj_bias_grad,
        mlp_gain_grad,
        mlp_shift_grad,
        up_grad,
        up_bias_grad,
        down_grad.T,
        down_bias_grad,
    )


def solution(mesh):
    return jax.shard_map(
        functools.partial(on_device, mesh.shape["dp"]),
        mesh=mesh,
        in_specs=(
            P("dp", None),
            P("dp", None),
            P("dp", None),
            P(),
            P(),
            P(None, None, "tensor"),
            P(None, "tensor"),
            P("tensor", None),
            P(),
            P(),
            P(),
            P(None, "tensor"),
            P("tensor"),
            P("tensor", None),
            P(),
        ),
        out_specs=(
            P("dp", None),
            P("dp", None),
            P(),
            P(),
            P("dp", None, "tensor"),
            P(None, "tensor"),
            P("tensor", "dp"),
            P(),
            P(),
            P(),
            P("dp", "tensor"),
            P("tensor"),
            P("tensor", "dp"),
            P(),
        ),
        check_vma=False,
    )
```

```python
import functools
import math

import jax
import jax.numpy as jnp
from jax import lax
from jax.experimental import pallas as pl
from jax.experimental.pallas import tpu as pltpu
from jax.sharding import PartitionSpec as P

HEAD_DIM = 64
HALF_DIM = HEAD_DIM // 2
GRID = 14
IMG = 196
EPS = 1e-06
SCALING = HEAD_DIM ** (-0.5)
LOG2E = math.log2(math.e)
KEY_CHUNKS = 2
MASK_ROWS = 16
END_WIDTH = 256
RESULT_STEPS = 2
ONES_ROWS = 16
FF_TILE = 512
FORBIDDEN = -1e30
VMEM_LIMIT = 62 * 1024 * 1024

MESH = pl.DeviceIdType.MESH

bf16 = jnp.bfloat16
f32 = jnp.float32


def dot(left, right, left_dim, right_dim):
    return lax.dot_general(
        left, right, (((left_dim,), (right_dim,)), ((), ())), preferred_element_type=f32
    )


def rotary_angles(offsets):
    pair_count = HALF_DIM
    side_pairs = pair_count * 11 // 32
    time_pairs = pair_count - 2 * side_pairs
    pair_index = jnp.arange(pair_count, dtype=jnp.int32)
    time_pair = pair_index < time_pairs
    height_pair = (pair_index >= time_pairs) & (pair_index < time_pairs + side_pairs)
    group_begin = jnp.where(
        time_pair, 0, jnp.where(height_pair, time_pairs, time_pairs + side_pairs)
    )
    group_size = jnp.where(time_pair, time_pairs, side_pairs)
    inverse = jnp.power(
        10000.0, -(pair_index - group_begin).astype(f32) / group_size.astype(f32)
    )
    frame_place = (offsets // IMG).astype(f32)
    row_place = (offsets % IMG // GRID).astype(f32)
    column_place = (offsets % GRID).astype(f32)
    position = jnp.where(
        time_pair[:, None],
        frame_place[None, :],
        jnp.where(height_pair[:, None], row_place[None, :], column_place[None, :]),
    )
    angles = position * inverse[:, None]
    return (jnp.cos(angles), jnp.sin(angles))


def params(collective_id=None):
    if collective_id is None:
        return pltpu.CompilerParams(vmem_limit_bytes=VMEM_LIMIT)
    return pltpu.CompilerParams(
        vmem_limit_bytes=VMEM_LIMIT, collective_id=collective_id, has_side_effects=True
    )


def greet(partners):
    barrier = pltpu.get_barrier_semaphore()
    for partner in partners:
        pl.semaphore_signal(barrier, inc=1, device_id=partner, device_id_type=MESH)
    pl.semaphore_wait(barrier, len(partners))


def partner_of(bit):
    index = lax.axis_index("dp")
    mine = (index // (1 << bit)) % 2
    return {"dp": index + (1 << bit) * (1 - 2 * mine)}, mine


def fold(keep, got, mine, next_keep, next_send):
    lead = (slice(None),) * (len(keep.shape) - 3)
    for pair in range(keep.shape[-3] // 2):
        for ref, odd in ((next_keep, mine), (next_send, 1 - mine)):
            at = lead + (2 * pair + odd,)
            value = keep[at]
            if got is not None:
                value = value.astype(f32) + got[at].astype(f32)
            ref[lead + (pair,)] = value.astype(bf16)


def remote(source, target, send_sem, recv_sem, partner):
    return pltpu.make_async_remote_copy(
        src_ref=source,
        dst_ref=target,
        send_sem=send_sem,
        recv_sem=recv_sem,
        device_id=partner,
        device_id_type=MESH,
    )


def whole_block(shape, **kwargs):
    return pl.BlockSpec(shape, lambda *_: (0,) * len(shape), **kwargs)


def once(shape):
    return whole_block(shape, pipeline_mode=pl.Buffered(1))


HBM = pl.BlockSpec(memory_space=pl.ANY)


def clamp(value, last):
    return jnp.minimum(jnp.maximum(value, 0), last)


def norm_parts(values):
    centre = values - jnp.mean(values, axis=1, keepdims=True)
    spread = jnp.mean(centre * centre, axis=1, keepdims=True)
    scale = lax.rsqrt(spread + EPS)
    return centre * scale, scale


def norm_back(grad, unit, scale, gain):
    c = grad * gain
    mean = jnp.mean(c, axis=1, keepdims=True)
    along = jnp.mean(c * unit, axis=1, keepdims=True)
    return scale * (c - mean - unit * along)


def column_sum(values):
    return jnp.sum(values, axis=0, keepdims=True)


def clip_masks(clip_len, tokens):
    token = jnp.arange(tokens, dtype=jnp.int32)[None, :] // IMG
    row = jnp.arange(MASK_ROWS, dtype=jnp.int32)[:, None]
    same = token == row
    images = clip_len < tokens
    forbid = images & jnp.logical_not(same) & (row < tokens // IMG)
    return jnp.where(forbid, FORBIDDEN, 0.0).astype(bf16), same.astype(bf16)


class Gather:
    STAGES = ((0,), (1, 2), (3, 4, 5, 6), (7, 8, 9, 10))
    COPIES = 11
    ROUTES = (
        (None, 0, 0, None),
        (0, 0, 0, 2),
        (1, 0, 0, 1),
        (0, 0, 0, 1),
        (0, 0, 1, 1),
        (1, 0, 0, 2),
        (1, 1, 0, 2),
        (None, 0, 0, 0),
        (None, 1, 0, 0),
        (None, 0, 1, 0),
        (None, 1, 1, 0),
    )

    def __init__(self, weight, other, send_sem, recv_sem):
        self.weight, self.other = weight, other
        self.send_sem, self.recv_sem = send_sem, recv_sem

    def place(self, x, z):
        core, mine_x, mine_z = (partner_of(bit)[1] for bit in range(3))
        x = mine_x + x * (1 - 2 * mine_x)
        return core + 2 * x + 4 * (mine_z + z * (1 - 2 * mine_z)), 8

    def copy(self, number):
        half, x, z, bit = self.ROUTES[number]
        index, parts = self.place(x, z)
        rows = self.other.shape[-2] // parts
        begin = index * rows
        if half is not None:
            rows //= 2
            begin = begin + half * rows
        at = (slice(None),) * (len(self.other.shape) - 2)
        at = at + (pl.ds(pl.multiple_of(begin, rows), rows),)
        source = self.weight if number == 0 else self.other
        return remote(
            source.at[at],
            self.other.at[at],
            self.send_sem.at[number],
            self.recv_sem.at[number],
            {"tensor": 1 - lax.axis_index("tensor")} if bit is None else partner_of(bit)[0],
        )

    def start(self, stage):
        for number in self.STAGES[stage]:
            self.copy(number).start()

    def wait(self, stage):
        for number in self.STAGES[stage]:
            self.copy(number).wait()

    def advance(self, stage):
        self.wait(stage - 1)
        self.start(stage)


class GatherZ(Gather):
    STAGES = ((0,), (1,), (2, 3))
    ROUTES = ((None, 0, 0, None), (None, 0, 0, 2), (None, 0, 0, 0), (None, 0, 1, 0))

    def place(self, x, z):
        core, mine_z = partner_of(0)[1], partner_of(2)[1]
        return core + 2 * (mine_z + z * (1 - 2 * mine_z)), 4


def neighbours():
    return [{"tensor": 1 - lax.axis_index("tensor")}] + [partner_of(bit)[0] for bit in range(3)]


def attend_kernel(
    x_ref,
    gain_ref,
    shift_ref,
    w_ref,
    b_ref,
    cos_ref,
    sin_ref,
    qm_ref,
    km_ref,
    up_bias_ref,
    proj_hbm,
    up_hbm,
    down_hbm,
    normed_ref,
    qkv_ref,
    att_ref,
    mine_ref,
    factor_ref,
    biases_ref,
    e_hbm,
    other_hbm,
    proj_other,
    up_other,
    down_other,
    k_scr,
    s_scr,
    e_scr,
    outgoing,
    bias_got,
    e_sem,
    bias_sem,
    send_sem,
    recv_sem,
    gather_send,
    gather_recv,
):
    step, last = pl.program_id(0), pl.num_programs(0) - 1
    tokens, width = x_ref.shape
    half = tokens // 2
    chunk = tokens // KEY_CHUNKS
    heads = e_hbm.shape[0]
    side = lax.axis_index("tensor")
    peer = {"tensor": 1 - side}
    proj = Gather(proj_hbm, proj_other, gather_send.at[0], gather_recv.at[0])
    up = Gather(up_hbm, up_other, gather_send.at[1], gather_recv.at[1])
    down = Gather(down_hbm, down_other, gather_send.at[2], gather_recv.at[2])

    bias_far = remote(up_bias_ref, bias_got, bias_sem.at[0], bias_sem.at[1], peer)

    @pl.when(step == 0)
    def _():
        greet(neighbours())
        bias_far.start()
        proj.start(0)
        up.start(0)
        unit, _ = norm_parts(x_ref[...].astype(f32))
        normed_ref[:width] = (unit * gain_ref[...] + shift_ref[...]).astype(bf16).T
        normed_ref[width:] = jnp.ones((ONES_ROWS, tokens), bf16)

    for at, weight, stage in (
        (2, proj, 1),
        (3, down, 0),
        (4, proj, 2),
        (4, up, 1),
        (6, proj, 3),
        (6, up, 2),
        (9, up, 3),
    ):

        @pl.when(step == at)
        def _():
            if stage:
                weight.advance(stage)
            else:
                weight.start(stage)

    @pl.when(step < 3)
    def _():
        rows = w_ref.shape[2]
        bias = jnp.broadcast_to(b_ref[pl.ds(step, 1), :], (8, rows)).T[:, :1]
        mixed = dot(w_ref[0], normed_ref[:width], 0, 0) + bias

        @pl.when(step < 2)
        def _():
            cosine, sine = cos_ref[...], sin_ref[...]
            for begin in range(0, rows, HEAD_DIM):
                middle, end = begin + HALF_DIM, begin + HEAD_DIM
                low, high = mixed[begin:middle], mixed[middle:end]
                qkv_ref[step, begin:middle, :] = (low * cosine - high * sine).astype(bf16)
                qkv_ref[step, middle:end, :] = (high * cosine + low * sine).astype(bf16)

        @pl.when(step == 2)
        def _():
            qkv_ref[step] = mixed.astype(bf16)

    head = step - 3
    slot = head % 2

    def store(index, part):
        at = pl.ds(part * chunk, chunk)
        return pltpu.make_async_copy(
            e_scr.at[index % 2, at], e_hbm.at[index, at], e_sem.at[index % 2, part]
        )

    def exchange(index):
        at = pl.ds(pl.multiple_of(index * HEAD_DIM, HEAD_DIM), HEAD_DIM)
        return remote(
            outgoing.at[index],
            other_hbm.at[at],
            send_sem.at[index],
            recv_sem.at[index],
            peer,
        )

    @pl.when(head >= 2)
    def _():
        for part in range(KEY_CHUNKS):
            store(head - 2, part).wait()

    @pl.when(head >= 0)
    def _():
        at = pl.ds(pl.multiple_of(clamp(head, heads - 1) * HEAD_DIM, HEAD_DIM), HEAD_DIM)
        queries = jnp.concatenate([qkv_ref[0, at], qm_ref[...]], axis=0)
        k_scr[...] = jnp.concatenate([qkv_ref[1, at], km_ref[...]], axis=0).T
        values = jnp.concatenate([qkv_ref[2, at], jnp.ones((16, tokens), bf16)], axis=0)
        top, out, tops = None, None, []
        s_scr[0] = dot(k_scr[:chunk], queries, 1, 0)
        for part in range(KEY_CHUNKS):
            begin, end = part * chunk, (part + 1) * chunk
            if part + 1 < KEY_CHUNKS:
                s_scr[(part + 1) % 2] = dot(k_scr[end : end + chunk], queries, 1, 0)
            scores = s_scr[part % 2]
            here = jnp.max(scores, axis=0, keepdims=True)
            new_top = here if top is None else jnp.maximum(top, here)
            weights = jnp.exp2((scores - new_top) * (SCALING * LOG2E)).astype(bf16)
            e_scr[slot, begin:end] = weights
            store(head, part).start()
            term = dot(values[:, begin:end], weights, 1, 0)
            if out is None:
                out = term
            else:
                out = out * jnp.exp2((top - new_top) * (SCALING * LOG2E)) + term
            top = new_top
            tops.append(top)
        scale = 1.0 / out[HEAD_DIM : HEAD_DIM + 1]
        for part in range(KEY_CHUNKS):
            factor_ref[0, part : part + 1] = scale * jnp.exp2(
                (tops[part] - top) * (SCALING * LOG2E)
            )
        attended = out[:HEAD_DIM] * scale
        att_ref[...] = attended.astype(bf16)
        left, right = attended[:, :half], attended[:, half:]
        mine_ref[...] = jnp.where(side == 0, left, right).astype(bf16)
        outgoing[clamp(head, heads - 1)] = jnp.where(side == 0, right, left).astype(bf16)
        exchange(head).start()

    @pl.when(step == last)
    def _():
        for back in (2, 1):
            for part in range(KEY_CHUNKS):
                store(heads - back, part).wait()
        for index in range(heads):
            exchange(index).wait()
        bias_far.wait()
        biases_ref[: bias_got.shape[0]] = up_bias_ref[...]
        biases_ref[bias_got.shape[0] :] = bias_got[...]
        for weight, stage in ((proj, 3), (up, 3), (down, 0)):
            weight.wait(stage)


def attend_forward(
    patches,
    gain,
    shift,
    weight,
    bias,
    cosine,
    sine,
    query_mask,
    key_mask,
    up_bias,
    proj,
    up,
    down,
):
    tokens, width = patches.shape
    columns = weight.shape[2]
    heads = columns // HEAD_DIM
    half = tokens // 2
    head = lambda i: clamp(i - 3, heads - 1)
    tiles = up_bias.shape[0] // FF_TILE
    vmem = pltpu.VMEM
    dma = lambda *shape: pltpu.SemaphoreType.DMA(shape)
    return pl.pallas_call(
        attend_kernel,
        grid=(3 + heads,),
        out_shape=(
            jax.ShapeDtypeStruct((width + ONES_ROWS, tokens), bf16),
            jax.ShapeDtypeStruct((3, columns, tokens), bf16),
            jax.ShapeDtypeStruct((columns, tokens), bf16),
            jax.ShapeDtypeStruct((columns, half), bf16),
            jax.ShapeDtypeStruct((heads, KEY_CHUNKS, tokens), f32),
            jax.ShapeDtypeStruct((2 * tiles, 1, FF_TILE), f32),
            jax.ShapeDtypeStruct((heads, tokens, tokens), bf16),
            jax.ShapeDtypeStruct((columns, half), bf16),
            jax.ShapeDtypeStruct(proj.shape, bf16),
            jax.ShapeDtypeStruct(up.shape, bf16),
            jax.ShapeDtypeStruct(down.shape, bf16),
        ),
        in_specs=[
            once((tokens, width)),
            once((1, width)),
            once((1, width)),
            pl.BlockSpec((1, width, columns), lambda i: (clamp(i, 2), 0, 0)),
            once((3, columns)),
            once(cosine.shape),
            once(sine.shape),
            once(query_mask.shape),
            once(key_mask.shape),
            once((tiles, 1, FF_TILE)),
            HBM,
            HBM,
            HBM,
        ],
        out_specs=(
            once((width + ONES_ROWS, tokens)),
            once((3, columns, tokens)),
            pl.BlockSpec((HEAD_DIM, tokens), lambda i: (head(i), 0)),
            pl.BlockSpec((HEAD_DIM, half), lambda i: (head(i), 0)),
            pl.BlockSpec((1, KEY_CHUNKS, tokens), lambda i: (head(i), 0, 0)),
            once((2 * tiles, 1, FF_TILE)),
            HBM,
            HBM,
            HBM,
            HBM,
            HBM,
        ),
        scratch_shapes=[
            vmem((tokens, HEAD_DIM + MASK_ROWS), bf16),
            vmem((2, tokens // KEY_CHUNKS, tokens), f32),
            vmem((2, tokens, tokens), bf16),
            vmem((heads, HEAD_DIM, half), bf16),
            vmem((tiles, 1, FF_TILE), f32),
            dma(2, KEY_CHUNKS),
            dma(2),
            dma(heads),
            dma(heads),
            dma(3, Gather.COPIES),
            dma(3, Gather.COPIES),
        ],
        compiler_params=params(3),
        cost_estimate=pl.CostEstimate(
            flops=6 * tokens * width * columns + 16 * heads * tokens * tokens * HEAD_DIM,
            bytes_accessed=60_000_000,
            transcendentals=heads * tokens * tokens,
        ),
        name="attend_forward",
    )(
        patches,
        gain[None, :],
        shift[None, :],
        weight,
        bias,
        cosine,
        sine,
        query_mask,
        key_mask,
        up_bias.reshape(tiles, 1, FF_TILE),
        proj,
        up,
        down,
    )


def attend_back_kernel(
    e_ref,
    q_ref,
    k_ref,
    v_ref,
    out_ref,
    total_ref,
    att_grad_ref,
    cos_ref,
    sin_ref,
    normed_ref,
    down_keep_ref,
    down_got_ref,
    up_keep_ref,
    up_got_ref,
    att_send_hbm,
    _,
    mine_ref,
    keep_ref,
    sum_ref,
    down_sum_ref,
    up_sum_ref,
    proj_sum_ref,
    other_ref,
    other_end_ref,
    got_ref,
    att_got_hbm,
    att_scr,
    up_scr,
    up_low,
    value_scr,
    v_scr,
    score_grad,
    turned,
    pair_scr,
    outgoing,
    outgoing_end,
    grad,
    outgoing_core,
    down_scr,
    down_last,
    up_first,
    up_last,
    send_sem,
    recv_sem,
    end_sem,
    core_send,
    core_recv,
    down_sem,
    down_last_sem,
    up_sem,
    up_last_sem,
    att_sem,
    att_load_sem,
):
    head, heads = pl.program_id(0), pl.num_programs(0)
    tokens = q_ref.shape[2]
    half = tokens // 2
    side = lax.axis_index("tensor")
    peer = {"tensor": 1 - side}
    core_partner, core = partner_of(0)
    slot = head % 2
    def exchange(index):
        return remote(
            outgoing.at[index % 4],
            other_ref.at[index],
            send_sem.at[index % 4],
            recv_sem.at[index],
            peer,
        )

    end_far = remote(outgoing_end, other_end_ref, end_sem.at[0], end_sem.at[1], peer)
    lanes = half // 128 * 128
    end_width = outgoing_end.shape[1] // heads

    def to_core(pair):
        at = pl.ds(pl.multiple_of(pair * 2 * HEAD_DIM, 2 * HEAD_DIM), 2 * HEAD_DIM)
        return remote(
            outgoing_core.at[pair % 2],
            got_ref.at[:, :, :, at],
            core_send.at[pair % 2],
            core_recv.at[pair],
            core_partner,
        )

    def hop(buffers, sems, pair, bit):
        at = pl.ds(2 * pair, 2)
        return remote(
            buffers.at[1, at],
            buffers.at[2, at],
            sems.at[0, pair],
            sems.at[1, pair],
            partner_of(bit)[0],
        )

    def start(keep, got, buffers, sems, pair, bit):
        at = pl.ds(2 * pair, 2)
        fold(keep, got, partner_of(bit)[1], buffers.at[0, at], buffers.at[1, at])
        hop(buffers, sems, pair, bit).start()

    def relay(source, source_sems, source_bit, buffers, sems, pair, bit):
        hop(source, source_sems, pair, source_bit).wait_recv()
        at = pl.ds(2 * pair, 2)
        start(source.at[0, at], source.at[2, at], buffers, sems, pair, bit)

    down_pairs, up_pairs = down_scr.shape[1] // 2, up_last.shape[1] // 2
    behind = heads - up_pairs

    late_heads = pl.ds(att_got_hbm.shape[0] // 2, att_got_hbm.shape[0] // 2)
    att_far = remote(
        att_send_hbm.at[late_heads], att_got_hbm.at[late_heads], att_sem.at[0], att_sem.at[1], peer
    )

    def att_load(index):
        at = pl.ds(pl.multiple_of(index * HEAD_DIM, HEAD_DIM), HEAD_DIM)
        return pltpu.make_async_copy(
            att_got_hbm.at[at], att_scr.at[index % 2], att_load_sem.at[index % 2]
        )

    @pl.when(head == 0)
    def _():
        att_load(0).start()
        greet(neighbours() + [partner_of(3)[0]])
        att_far.start()

    @pl.when(head >= 4)
    def _():
        exchange(head - 4).wait_send()

    @pl.when(head <= up_pairs)
    def _():
        start(up_keep_ref, up_got_ref, up_first, up_sem, head, 1)

    @pl.when(head < down_pairs)
    def _():
        start(down_keep_ref, down_got_ref, down_scr, down_sem, head, 2)

    @pl.when(head >= heads - down_pairs)
    def _():
        relay(
            down_scr, down_sem, 2, down_last, down_last_sem, head - (heads - down_pairs), 3
        )

    @pl.when(head >= behind)
    def _():
        relay(up_first, up_sem, 1, up_last, up_last_sem, head - behind, 2)

    @pl.when(head + 1 == heads // 2)
    def _():
        att_far.wait_recv()

    @pl.when(head + 1 < heads)
    def _():
        att_load(head + 1).start()

    att_load(head).wait()
    chunks = total_ref.shape[1]
    chunk = tokens // chunks
    att_mine, att_other = att_grad_ref[...].astype(f32), att_scr[slot].astype(f32)
    up_scr[:, :half] = jnp.where(side == 0, att_mine, att_other)
    up_scr[:, half:] = jnp.where(side == 0, att_other, att_mine)
    attended = out_ref[...].astype(f32)
    centre = []
    for part in range(chunks):
        up_low[part] = (up_scr[...] * total_ref[0, part : part + 1]).astype(bf16)
        centre.append(column_sum(up_low[part].astype(f32) * attended))
    v_scr[...] = v_ref[0].T
    cosine, sine = cos_ref[...], sin_ref[...]

    ends = {}

    def store(part, low, high):
        for row, value in ((0, low), (HALF_DIM, high)):
            left, right = value[:, :half], value[:, half:]
            mine_ref[part, row : row + HALF_DIM] = jnp.where(side == 0, left, right).astype(bf16)
            theirs = jnp.where(side == 0, right, left)
            outgoing[head % 4, part, row : row + HALF_DIM] = theirs[:, :lanes].astype(bf16)
            ends[part, row // HALF_DIM] = theirs[:, lanes:]
            begin = pl.multiple_of(part * 2 * HEAD_DIM + slot * HEAD_DIM + row, HALF_DIM)
            pair_scr[pl.ds(begin, HALF_DIM)] = value.astype(bf16)

    def unrotated(part, grad):
        low, high = grad[:HALF_DIM] * SCALING, grad[HALF_DIM:] * SCALING
        store(part, low * cosine + high * sine, high * cosine - low * sine)

    for part in range(chunks):
        at = slice(part * chunk, (part + 1) * chunk)
        value_scr[:, at] = dot(up_low[part], e_ref[0, at], 1, 1)
        prob_grad = dot(v_scr[at], up_low[part], 1, 0)
        score_grad[at] = (e_ref[0, at].astype(f32) * (prob_grad - centre[part])).astype(bf16)
    store(2, value_scr[:HALF_DIM], value_scr[HALF_DIM:])
    unrotated(0, dot(k_ref[0], score_grad[...], 1, 0))
    turned[...] = score_grad[...].T
    unrotated(1, dot(q_ref[0], turned[...], 1, 0))
    exchange(head).start()
    end = jnp.concatenate([ends[part, row] for part in range(3) for row in range(2)], axis=0)
    end = jnp.concatenate([end, jnp.zeros((end_width - end.shape[0], end.shape[1]), f32)], axis=0)
    begin = pl.multiple_of(head * end_width, end_width)
    outgoing_end[:, pl.ds(begin, end_width)] = end.T.astype(bf16)

    @pl.when(slot == 1)
    def _():
        pair = head // 2
        width = grad.shape[0] - ONES_ROWS
        grad[...] = dot(normed_ref[...], pair_scr[...], 1, 1)

        @pl.when(pair >= 2)
        def _():
            to_core(pair - 2).wait_send()

        for part in range(3):
            lanes = pl.ds(part * 2 * HEAD_DIM, 2 * HEAD_DIM)
            split_rows(
                grad.at[:, lanes], keep_ref.at[part], outgoing_core.at[pair % 2, part], core
            )
            sum_ref[part : part + 1] = grad[width : width + 1, lanes]
        to_core(pair).start()

    @pl.when(head == heads - 1)
    def _():
        end_far.start()
        for back in range(4):
            exchange(heads - 1 - back).wait_send()
        for back in range(2):
            to_core(heads // 2 - 1 - back).wait_send()
        for index in range(other_ref.shape[0] // 2):
            to_core(index).wait_recv()
        for pair in range(down_pairs):
            hop(down_scr, down_sem, pair, 2).wait_send()
            hop(down_last, down_last_sem, pair, 3).wait()
        down_sum_ref[...] = down_last[0].astype(f32) + down_last[2].astype(f32)
        for pair in range(up_pairs):
            hop(up_first, up_sem, pair, 1).wait_send()
            hop(up_last, up_last_sem, pair, 2).wait()
        up_sum_ref[...] = (up_last[0].astype(f32) + up_last[2].astype(f32)).astype(bf16)
        hop(up_first, up_sem, up_pairs, 1).wait()
        at = pl.ds(2 * up_pairs, 2)
        proj_sum_ref[...] = (up_first[0, at].astype(f32) + up_first[2, at].astype(f32)).astype(bf16)
        att_far.wait_send()
        end_far.wait()
        for index in range(other_ref.shape[0]):
            exchange(index).wait_recv()


def attend_backward(
    count,
    weights,
    qkv,
    attended,
    totals,
    att_grad,
    att_send,
    att_got,
    cosine,
    sine,
    normed,
    down_keep,
    down_got,
    up_keep,
    up_got,
):
    tokens = qkv.shape[2]
    half = tokens // 2
    heads = weights.shape[0]
    columns = heads * HEAD_DIM
    width = normed.shape[0] - ONES_ROWS
    rows = width // count
    split = (3, count // 2, rows)
    blocks = lambda bits: (count >> bits, rows, FF_TILE)
    pair = lambda lead, first, last: pl.BlockSpec(
        (2,) + lead, lambda i: (first + clamp(i, last), 0, 0, 0)
    )
    block = lambda part: pl.BlockSpec((1, HEAD_DIM, tokens), lambda i: (part, i, 0))
    half_block = pl.BlockSpec((HEAD_DIM, half), lambda i: (i, 0))
    lanes = half // 128 * 128
    pair_block = pl.BlockSpec(split + (2 * HEAD_DIM,), lambda i: (0, 0, 0, i // 2))
    vmem = pltpu.VMEM
    dma = lambda *shape: pltpu.SemaphoreType.DMA(shape)
    return pl.pallas_call(
        attend_back_kernel,
        grid=(heads,),
        out_shape=(
            jax.ShapeDtypeStruct((3, columns, half), bf16),
            jax.ShapeDtypeStruct(split + (columns,), bf16),
            jax.ShapeDtypeStruct((3, columns), f32),
            jax.ShapeDtypeStruct((heads,) + blocks(4), f32),
            jax.ShapeDtypeStruct((heads,) + blocks(3), bf16),
            jax.ShapeDtypeStruct((2,) + blocks(2), bf16),
            jax.ShapeDtypeStruct((heads, 3, HEAD_DIM, lanes), bf16),
            jax.ShapeDtypeStruct((half - lanes, heads * END_WIDTH), bf16),
            jax.ShapeDtypeStruct(split + (columns,), bf16),
            jax.ShapeDtypeStruct(att_got.shape, bf16),
        ),
        input_output_aliases={15: 9},
        in_specs=[
            pl.BlockSpec((1, tokens, tokens), lambda i: (i, 0, 0)),
            block(0),
            block(1),
            block(2),
            pl.BlockSpec((HEAD_DIM, tokens), lambda i: (i, 0)),
            pl.BlockSpec((1, totals.shape[1], tokens), lambda i: (i, 0, 0)),
            half_block,
            once(cosine.shape),
            once(sine.shape),
            once(normed.shape),
            pair(blocks(2), 0, heads // 2 - 1),
            pair(blocks(2), 0, heads // 2 - 1),
            pair(blocks(1), 0, heads // 2),
            pair(blocks(1), heads // 2, heads // 2),
            HBM,
            HBM,
        ],
        out_specs=(
            pl.BlockSpec((3, HEAD_DIM, half), lambda i: (0, i, 0)),
            pair_block,
            pl.BlockSpec((3, 2 * HEAD_DIM), lambda i: (0, i // 2)),
            once((heads,) + blocks(4)),
            once((heads,) + blocks(3)),
            once((2,) + blocks(2)),
            HBM,
            HBM,
            HBM,
            HBM,
        ),
        scratch_shapes=[
            vmem((2, HEAD_DIM, half), bf16),
            vmem((HEAD_DIM, tokens), f32),
            vmem((totals.shape[1], HEAD_DIM, tokens), bf16),
            vmem((HEAD_DIM, tokens), f32),
            vmem((tokens, HEAD_DIM), bf16),
            vmem((tokens, tokens), bf16),
            vmem((tokens, tokens), bf16),
            vmem((6 * HEAD_DIM, tokens), bf16),
            vmem((4, 3, HEAD_DIM, lanes), bf16),
            vmem((half - lanes, heads * END_WIDTH), bf16),
            vmem((width + ONES_ROWS, 6 * HEAD_DIM), f32),
            vmem((2,) + split + (2 * HEAD_DIM,), bf16),
            vmem((3, heads) + blocks(3), bf16),
            vmem((3, heads) + blocks(4), bf16),
            vmem((3, heads + 2) + blocks(2), bf16),
            vmem((3, heads) + blocks(3), bf16),
            dma(4),
            dma(heads),
            dma(2),
            dma(2),
            dma(heads // 2),
            dma(2, heads // 2),
            dma(2, heads // 2),
            dma(2, heads // 2 + 1),
            dma(2, heads // 2),
            dma(2),
            dma(2),
        ],
        compiler_params=params(0),
        cost_estimate=pl.CostEstimate(
            flops=32 * heads * tokens * tokens * HEAD_DIM,
            bytes_accessed=2 * heads * tokens * tokens,
            transcendentals=0,
        ),
        name="attend_backward",
    )(
        weights,
        qkv,
        qkv,
        qkv,
        attended,
        totals,
        att_grad,
        cosine,
        sine,
        normed,
        down_keep,
        down_got,
        up_keep,
        up_got,
        att_send,
        att_got,
    )


def normal_parts(value):
    a = jnp.abs(value)
    t = 1.0 / (1.0 + (0.3275911 / math.sqrt(2.0)) * a)
    bell = jnp.exp2(value * value * (-0.5 * LOG2E))
    c = [0.5 * x for x in (0.254829592, -0.284496736, 1.421413741, -1.453152027, 1.061405429)]
    tail = ((((c[4] * t + c[3]) * t + c[2]) * t + c[1]) * t + c[0]) * t * bell
    return jnp.where(value >= 0, 1.0 - tail, tail), bell * (1.0 / math.sqrt(2.0 * math.pi))


def split_rows(grad, keep_ref, send_ref, core):
    count, rows = keep_ref.shape[:2]
    for pair in range(count):
        for ref, odd in ((keep_ref, core), (send_ref, 1 - core)):
            begin = pl.multiple_of((2 * pair + odd) * rows, rows)
            ref[pair] = grad[pl.ds(begin, rows), :].astype(bf16)


def accumulate(step, total, term):
    @pl.when(step == 0)
    def _():
        total[...] = term

    @pl.when(step > 0)
    def _():
        total[...] += term


def feed_kernel(
    att_ref,
    att_other_ref,
    proj_ref,
    proj_other_ref,
    proj_bias_ref,
    gain_ref,
    shift_ref,
    down_bias_ref,
    up_bias_ref,
    patch_hbm,
    cot_hbm,
    up_hbm,
    up_other_hbm,
    down_hbm,
    _,
    qkv_hbm,
    grad_ref,
    att_grad_ref,
    att_scr,
    vector_ref,
    up_bias_grad_ref,
    keep_x_ref,
    keep_ref,
    out_hbm,
    att_got_hbm,
    got_hbm,
    got_x_hbm,
    down_other_hbm,
    qkv_other_hbm,
    n_scr,
    cot_scr,
    out_scr,
    total,
    act_scr,
    slope_scr,
    up_scr,
    down_scr,
    low_scr,
    grad_scr,
    keep_ring,
    outgoing,
    arrived,
    outgoing_x,
    load_sem,
    up_sem,
    down_sem,
    store_sem,
    row_sem,
    att_sem,
    send_sem,
    recv_sem,
    arrive_sem,
    send_x_sem,
    recv_x_sem,
    gather_send,
    gather_recv,
):
    step, last = pl.program_id(0), pl.num_programs(0) - 1
    tiles = act_scr.shape[0]
    half_tiles = tiles // 2
    half = n_scr.shape[0]
    side = lax.axis_index("tensor")
    peer = {"tensor": 1 - side}
    core_partner, core = partner_of(0)
    x_partner, x_side = partner_of(1)
    mine = pl.ds(pl.multiple_of(side * half, 16), half)
    gather_down = Gather(down_hbm, down_other_hbm, gather_send.at[0], gather_recv.at[0])
    gather_qkv = GatherZ(qkv_hbm, qkv_other_hbm, gather_send.at[1], gather_recv.at[1])
    patch_load = pltpu.make_async_copy(patch_hbm.at[mine], out_scr, load_sem.at[0])
    cot_load = pltpu.make_async_copy(cot_hbm.at[mine], cot_scr, load_sem.at[1])
    out_near = pltpu.make_async_copy(out_scr, out_hbm.at[mine], store_sem)
    out_far = remote(out_scr, out_hbm.at[mine], row_sem.at[0], row_sem.at[1], peer)
    early_heads = pl.ds(0, att_scr.shape[0] // 2)
    att_far = remote(
        att_scr.at[early_heads], att_got_hbm.at[early_heads], att_sem.at[0], att_sem.at[1], peer
    )

    def load_up(tile, act):
        for begin, source in ((0, up_hbm), (half_tiles, up_other_hbm)):

            @pl.when((tile >= begin) & (tile < begin + half_tiles))
            def _():
                at = pl.ds(pl.multiple_of((tile - begin) * FF_TILE, FF_TILE), FF_TILE)
                copy = pltpu.make_async_copy(
                    source.at[:, at], up_scr.at[tile % 2], up_sem.at[tile % 2]
                )
                getattr(copy, act)()

    def load_down(tile, act):
        for begin, source in ((0, down_hbm), (half_tiles, down_other_hbm)):

            @pl.when((tile >= begin) & (tile < begin + half_tiles))
            def _():
                at = pl.ds(pl.multiple_of((tile - begin) * FF_TILE, FF_TILE), FF_TILE)
                copy = pltpu.make_async_copy(
                    source.at[at], down_scr.at[tile % 2], down_sem.at[tile % 2]
                )
                getattr(copy, act)()

    def to_core(index):
        return remote(
            outgoing.at[index % 2],
            got_hbm.at[index],
            send_sem.at[index % 2],
            recv_sem.at[index],
            core_partner,
        )

    def to_x(index):
        return remote(
            outgoing_x.at[index],
            got_x_hbm.at[index],
            send_x_sem.at[index],
            recv_x_sem.at[index],
            x_partner,
        )

    def arrive(index):
        return pltpu.make_async_copy(
            got_hbm.at[index], arrived.at[index % 2], arrive_sem.at[index % 2]
        )

    @pl.when(step == 0)
    def _():
        patch_load.start()
        cot_load.start()
        load_up(0, "start")
        greet(neighbours())
        gather_down.start(1)
        gather_qkv.start(0)
        branch = dot(att_ref[...], proj_ref[...], 0, 0).astype(bf16).astype(f32)
        other = dot(att_other_ref[...], proj_other_ref[...], 0, 0).astype(bf16).astype(f32)
        patch_load.wait()
        residual = out_scr[...].astype(f32) + (branch + other + proj_bias_ref[...])
        grad_ref[...] = residual
        unit, _ = norm_parts(residual)
        n_scr[...] = (unit * gain_ref[...] + shift_ref[...]).astype(bf16)
        cot_load.wait()
        vector_ref[3:4] = column_sum(cot_scr[...].astype(f32))

    slot = step % 2

    for at, weight, stage in (
        (half_tiles - 1, gather_down, 2),
        (tiles, gather_down, 3),
        (tiles + 4, gather_qkv, 1),
        (2 * tiles + 4, gather_qkv, 2),
    ):

        @pl.when(step == at)
        def _():
            weight.advance(stage)

    @pl.when(step == tiles + half_tiles - 1)
    def _():
        gather_down.wait(3)

    first, second, third = step, step - tiles, step - 2 * tiles

    @pl.when(first + 1 < tiles)
    def _():
        load_up(first + 1, "start")

    @pl.when(first < tiles)
    def _():
        load_up(first, "wait")

    @pl.when((second + 1 >= 0) & (second + 1 < tiles))
    def _():
        load_down(second + 1, "start")

    @pl.when((second >= 0) & (second < tiles))
    def _():
        load_down(second, "wait")

    @pl.when((third + 1 >= 0) & (third + 1 < tiles))
    def _():
        load_up(third + 1, "start")
        load_down(third + 1, "start")

    @pl.when((third >= 0) & (third < tiles))
    def _():
        load_up(third, "wait")
        load_down(third, "wait")

    item = jnp.where(step < tiles, step, step - 2 * tiles)
    sends = (step < tiles) | (step >= 3 * tiles)

    @pl.when(sends & (item >= 2))
    def _():
        to_core(item - 2).wait_send()

    def send_gradient(value, keep):
        grad_scr[...] = value
        split_rows(grad_scr, keep, outgoing.at[slot], core)
        to_core(item).start()

    @pl.when(first < tiles)
    def _():
        upward = dot(n_scr[...], up_scr[slot], 1, 0) + up_bias_ref[clamp(first, tiles - 1)]
        share, density = normal_parts(upward)
        activated = (upward * share).astype(bf16)
        act_scr[clamp(first, tiles - 1)] = activated
        slope_scr[clamp(first, tiles - 1)] = (share + upward * density).astype(bf16)
        send_gradient(dot(cot_scr[...], activated, 0, 0), keep_ring.at[clamp(first, tiles - 1)])

    @pl.when((second >= 0) & (second < tiles))
    def _():
        accumulate(second, total, dot(act_scr[clamp(second, tiles - 1)], down_scr[slot], 1, 0))

    @pl.when(second == tiles - 1)
    def _():
        out_scr[...] = (grad_ref[...] + (total[...] + down_bias_ref[...])).astype(bf16)
        out_near.start()
        out_far.start()

    @pl.when((third >= 0) & (third < tiles))
    def _():
        tile = clamp(third, tiles - 1)
        act_grad = dot(cot_scr[...], down_scr[slot], 1, 1)
        upward_grad = (act_grad * slope_scr[tile].astype(f32)).astype(bf16)
        slope_scr[tile] = upward_grad
        up_bias_grad_ref[0] = column_sum(upward_grad.astype(f32))
        accumulate(third, total, dot(upward_grad, up_scr[slot], 1, 1))

    @pl.when(third == tiles - 1)
    def _():
        unit, scale = norm_parts(grad_ref[...])
        normed_grad = total[...]
        residual_grad = cot_scr[...].astype(f32) + norm_back(
            normed_grad, unit, scale, gain_ref[...]
        )
        low = residual_grad.astype(bf16)
        grad_ref[...] = residual_grad
        low_scr[...] = low
        att_scr[...] = dot(proj_other_ref[...], low, 1, 1).astype(bf16)
        att_far.start()
        att_grad_ref[...] = dot(proj_ref[...], low, 1, 1).astype(bf16)
        vector_ref[0:1] = column_sum(normed_grad * unit)
        vector_ref[1:2] = column_sum(normed_grad)
        vector_ref[2:3] = column_sum(low.astype(f32))

    fourth = step - 3 * tiles

    @pl.when((fourth >= 0) & (fourth < tiles))
    def _():
        value = dot(n_scr[...], slope_scr[clamp(fourth, tiles - 1)], 0, 0)
        send_gradient(value, keep_ref.at[0])

    @pl.when(fourth == tiles)
    def _():
        send_gradient(dot(low_scr[...], att_ref[...], 0, 1), keep_ref.at[0])

    @pl.when(fourth == tiles + 1)
    def _():
        send_gradient(dot(low_scr[...], att_other_ref[...], 0, 1), keep_ref.at[0])

    @pl.when((second + 1 >= 0) & (second + 1 < tiles))
    def _():
        to_core(second + 1).wait_recv()
        arrive(second + 1).start()

    @pl.when((second >= 0) & (second < tiles))
    def _():
        arrive(second).wait()
        tile = clamp(second, tiles - 1)
        fold(
            keep_ring.at[tile],
            arrived.at[tile % 2],
            x_side,
            keep_x_ref.at[0],
            outgoing_x.at[tile],
        )
        to_x(tile).start()

    @pl.when(step == last)
    def _():
        gather_qkv.wait(2)
        items = got_hbm.shape[0] - 1
        to_core(items - 2).wait_send()
        to_core(items - 1).wait_send()
        for index in range(tiles, items):
            to_core(index).wait_recv()
        for index in range(tiles):
            to_x(index).wait()
        att_far.wait()
        out_near.wait()
        out_far.wait()


def feed_forward(
    count,
    att_mine,
    att_other,
    proj,
    proj_other,
    proj_bias,
    gain,
    shift,
    down_bias,
    up_bias,
    patches,
    cot,
    up,
    up_other,
    down,
    down_part,
    qkv,
):
    tokens, width = patches.shape
    half = tokens // 2
    columns = proj.shape[0]
    tiles = 2 * up.shape[1] // FF_TILE
    items = 2 * tiles + 2
    row = once((1, width))
    left = (width // count, FF_TILE)
    tile = lambda first, lead, size: pl.BlockSpec(
        (1,) + lead, lambda i: (clamp(i - first, size - 1),) + (0,) * len(lead)
    )
    vmem = pltpu.VMEM
    dma = lambda *shape: pltpu.SemaphoreType.DMA(shape)
    return pl.pallas_call(
        feed_kernel,
        grid=(4 * tiles + 2,),
        in_specs=[
            once((columns, half)),
            once((columns, half)),
            once(proj.shape),
            once(proj.shape),
            row,
            row,
            row,
            row,
            once(up_bias.shape),
            HBM,
            HBM,
            HBM,
            HBM,
            HBM,
            HBM,
            HBM,
        ],
        out_specs=(
            once((half, width)),
            once((columns, half)),
            once((columns, half)),
            once((4, width)),
            tile(2 * tiles, (1, FF_TILE), tiles),
            tile(tiles, (count // 4,) + left, tiles),
            tile(3 * tiles, (count // 2,) + left, tiles + 2),
            HBM,
            HBM,
            HBM,
            HBM,
            HBM,
            HBM,
        ),
        out_shape=(
            jax.ShapeDtypeStruct((half, width), f32),
            jax.ShapeDtypeStruct((columns, half), bf16),
            jax.ShapeDtypeStruct((columns, half), bf16),
            jax.ShapeDtypeStruct((4, width), f32),
            jax.ShapeDtypeStruct((tiles, 1, FF_TILE), f32),
            jax.ShapeDtypeStruct((tiles, count // 4) + left, bf16),
            jax.ShapeDtypeStruct((tiles + 2, count // 2) + left, bf16),
            jax.ShapeDtypeStruct((tokens, width), bf16),
            jax.ShapeDtypeStruct((columns, half), bf16),
            jax.ShapeDtypeStruct((items + 1, count // 2) + left, bf16),
            jax.ShapeDtypeStruct((tiles, count // 4) + left, bf16),
            jax.ShapeDtypeStruct(down.shape, bf16),
            jax.ShapeDtypeStruct(qkv.shape, bf16),
        ),
        input_output_aliases={14: 11},
        scratch_shapes=[
            vmem((half, width), bf16),
            vmem((half, width), bf16),
            vmem((half, width), bf16),
            vmem((half, width), f32),
            vmem((tiles, half, FF_TILE), bf16),
            vmem((tiles, half, FF_TILE), bf16),
            vmem((2, width, FF_TILE), bf16),
            vmem((2, FF_TILE, width), bf16),
            vmem((half, width), bf16),
            vmem((width, FF_TILE), f32),
            vmem((tiles, count // 2) + left, bf16),
            vmem((2, count // 2) + left, bf16),
            vmem((2, count // 2) + left, bf16),
            vmem((tiles, count // 4) + left, bf16),
            dma(2),
            dma(2),
            dma(2),
            pltpu.SemaphoreType.DMA,
            dma(2),
            dma(2),
            dma(2),
            dma(items),
            dma(2),
            dma(tiles),
            dma(tiles),
            dma(2, Gather.COPIES),
            dma(2, Gather.COPIES),
        ],
        compiler_params=params(2),
        cost_estimate=pl.CostEstimate(
            flops=12 * half * width * tiles * FF_TILE,
            bytes_accessed=60_000_000,
            transcendentals=half * tiles * FF_TILE,
        ),
        name="feed_forward",
    )(
        att_mine,
        att_other,
        proj,
        proj_other,
        proj_bias[None, :],
        gain[None, :],
        shift[None, :],
        down_bias[None, :],
        up_bias,
        patches,
        cot,
        up,
        up_other,
        down,
        down_part,
        qkv,
    )


class Chain:
    def __init__(self, keep, got, bits, scratch):
        self.keep, self.got, self.bits, self.scratch = keep, got, list(bits), list(scratch)
        self.last = None

    def step(self):
        if self.last is not None:
            self.copy(*self.last).wait()
            self.last = None
        if not self.bits:
            return
        bit = self.bits.pop(0)
        keep, send, got, sem = self.scratch.pop(0)
        fold(self.keep, self.got, partner_of(bit)[1], keep, send)
        self.last = (bit, send, got, sem)
        self.copy(*self.last).start()
        self.keep, self.got = keep, got

    def finish(self):
        while self.bits:
            self.step()
        self.step()

    def copy(self, bit, send, got, sem):
        return remote(send, got, sem.at[0], sem.at[1], partner_of(bit)[0])

    def result(self, tile):
        value = self.keep[tile, 0].astype(f32)
        return value if self.got is None else value + self.got[tile, 0].astype(f32)


def input_back_kernel(
    bits,
    other_end_ref,
    gain_ref,
    vector_ref,
    down_sum,
    up_sum,
    proj_sum,
    qkv_keep,
    qkv_got,
    mine_hbm,
    other_hbm,
    w_hbm,
    w_other_hbm,
    x_hbm,
    grad_hbm,
    total_ref,
    down_ref,
    up_ref,
    proj_ref,
    qkv_ref,
    out_hbm,
    total,
    mine_ref,
    other_ref,
    w_ref,
    w_other_ref,
    x_scr,
    grad_scr,
    out_scr,
    vector_send,
    vector_got,
    vector_scr,
    vector_next,
    side_send,
    side_got,
    load_sem,
    store_sem,
    row_send,
    row_recv,
    vector_sem,
    side_sem,
    *scratch,
):
    step = pl.program_id(0)
    half, width = grad_scr.shape
    side = lax.axis_index("tensor")
    peer = {"tensor": 1 - side}
    mine = pl.ds(pl.multiple_of(side * half, 16), half)
    loads = [
        pltpu.make_async_copy(x_hbm.at[mine], x_scr, load_sem.at[0]),
        pltpu.make_async_copy(grad_hbm, grad_scr, load_sem.at[1]),
        pltpu.make_async_copy(w_hbm, w_ref, load_sem.at[2]),
        pltpu.make_async_copy(mine_hbm, mine_ref, load_sem.at[3]),
        pltpu.make_async_copy(w_other_hbm, w_other_ref, load_sem.at[4]),
        pltpu.make_async_copy(other_hbm, other_ref, load_sem.at[5]),
    ]
    stages, rest = [], list(scratch)
    for first in (4, 3, 2, 1):
        stages.append([tuple(rest[4 * i : 4 * i + 4]) for i in range(bits - first)])
        rest = rest[4 * (bits - first) :]
    down = Chain(down_sum, None, range(4, bits), stages[0])
    up = Chain(up_sum, None, range(3, bits), stages[1])
    proj = Chain(proj_sum, None, range(2, bits), stages[2])
    qkv = Chain(qkv_keep, qkv_got, range(1, bits), stages[3])
    tiles = down_ref.shape[1] // FF_TILE
    early_down = not down.bits

    def side_copy(at, size):
        return remote(
            side_send.at[pl.ds(at, size)],
            side_got.at[pl.ds(at, size)],
            side_sem.at[2 * (at // tiles)],
            side_sem.at[2 * (at // tiles) + 1],
            peer,
        )

    def other_side(parts, at):
        for number, part in enumerate(parts):
            side_send[at + number] = part.astype(bf16)
        side_copy(at, len(parts)).start()

    @pl.when(step == 0)
    def _():
        for load in loads:
            load.start()
        greet([peer] + [partner_of(bit)[0] for bit in range(bits)])
        if early_down:
            other_side([down.result(tiles + i) for i in range(tiles)], 0)
        for chain in (qkv, up, proj, down):
            chain.step()

    heads = other_ref.shape[0]
    lanes = other_ref.shape[3]
    gain = gain_ref[...]
    first_rows = lanes // 256 * 128
    blocks = ((0, first_rows), (first_rows, half))

    def rows_copies(block):
        begin, end = blocks[block]
        at = pl.ds(begin, end - begin)
        target = out_hbm.at[pl.ds(pl.multiple_of(side * half + begin, 16), end - begin)]
        return (
            remote(out_scr.at[at], target, row_send.at[block], row_recv.at[block], peer),
            pltpu.make_async_copy(out_scr.at[at], target, store_sem.at[block]),
        )

    def input_rows(block):
        begin, end = blocks[block]
        whole_end = min(end, lanes)
        near, far = 0.0, 0.0
        for part in range(3):
            near = near + dot(mine_ref[part, :, begin:end], w_ref[part], 0, 1)
            left = other_ref[:, part, :, begin:whole_end].reshape(
                heads * HEAD_DIM, whole_end - begin
            )
            far = far + dot(left, w_other_ref[part], 0, 1)
        if end > lanes:
            rest = 0.0
            for part in range(3):
                ends = [
                    other_end_ref[:, pl.ds(head * END_WIDTH, 3 * HEAD_DIM)][
                        :, part * HEAD_DIM : (part + 1) * HEAD_DIM
                    ]
                    for head in range(heads)
                ]
                rest = rest + dot(jnp.concatenate(ends, axis=1), w_other_ref[part], 1, 1)
            far = jnp.concatenate([far, rest], axis=0)
        normed_grad = near + far
        unit, scale = norm_parts(x_scr[begin:end].astype(f32))
        out = grad_scr[begin:end] + norm_back(normed_grad, unit, scale, gain)
        out_scr[begin:end] = out.astype(bf16)
        return column_sum(normed_grad * unit), column_sum(normed_grad)

    @pl.when(step == 0)
    def _():
        for load in loads:
            load.wait()
        sums = input_rows(0)
        for copy in rows_copies(0):
            copy.start()
        total[0:1], total[1:2] = sums

    @pl.when(step == 1)
    def _():
        sums = input_rows(1)
        sums = [total[number : number + 1] + sums[number] for number in range(2)]

        both = vector_got.shape[1]
        vector_send[:, : 2 * width] = jnp.concatenate(sums, axis=1)
        vector_send[:, 2 * width :] = vector_ref[1:2, 2 * width : both]
        vector_copy = remote(vector_send, vector_got, vector_sem.at[0], vector_sem.at[1], peer)
        vector_copy.start()
        for copy in rows_copies(1):
            copy.start()

        vector_bits = list(range(bits))

        def add_vectors():
            if not vector_bits:
                return
            bit = vector_bits.pop(0)
            copy = remote(
                vector_scr,
                vector_next.at[bit],
                vector_sem.at[2 * bit + 2],
                vector_sem.at[2 * bit + 3],
                partner_of(bit)[0],
            )
            copy.start()
            copy.wait()
            vector_scr[...] += vector_next[bit]

        qkv.step()
        while proj.bits:
            proj.step()
        vector_copy.wait()
        vector_scr[:, :both] = vector_got[...] + jnp.concatenate(
            sums + [vector_ref[0:1, 2 * width : both]], axis=1
        )
        vector_scr[:, both:] = vector_ref[0:1, both:]
        add_vectors()
        if not early_down:
            down.finish()
            other_side([down.result(tiles + i) for i in range(tiles)], 0)
        up.finish()
        other_side([up.result(tiles + i) for i in range(tiles)], tiles)
        add_vectors()
        qkv.step()
        proj.step()
        other_side([proj.result(1)], 2 * tiles)
        add_vectors()
        side_copy(0, tiles).wait()
        for tile in range(tiles):
            at = pl.ds(tile * FF_TILE, FF_TILE)
            down_ref[:, at] = down.result(tile) + side_got[tile].astype(f32)
        qkv.finish()
        for part in range(3):
            qkv_ref[part] = qkv.result(part)
        while vector_bits:
            add_vectors()
        total_ref[...] = vector_scr[...]
        side_copy(tiles, tiles).wait()
        for tile in range(tiles):
            at = pl.ds(tile * FF_TILE, FF_TILE)
            up_ref[:, at] = up.result(tile) + side_got[tiles + tile].astype(f32)
        side_copy(2 * tiles, 1).wait()
        proj_ref[...] = proj.result(0) + side_got[2 * tiles].astype(f32)
        for block in range(2):
            far, near = rows_copies(block)
            near.wait()
            far.wait()


def input_backward(
    count,
    mine,
    other,
    other_end,
    weight,
    weight_other,
    gain,
    vectors,
    down_sum,
    up_sum,
    proj_sum,
    qkv_keep,
    qkv_got,
    patches,
    residual_grad,
):
    tokens, width = patches.shape
    half = tokens // 2
    columns = mine.shape[1]
    heads = other.shape[0]
    bits = count.bit_length() - 1
    rows = width // count
    tiles = heads // 2
    size = vectors.shape[1]
    both = size - FF_TILE * 3
    vmem = pltpu.VMEM
    dma = lambda *shape: pltpu.SemaphoreType.DMA(shape)
    scratch = []
    for first, lead in ((4, heads), (3, heads), (2, 2), (1, 3)):
        for bit in range(first, bits):
            shape = (lead, count >> (bit + 1), rows, FF_TILE)
            scratch += [vmem(shape, bf16), vmem(shape, bf16), vmem(shape, bf16), dma(2)]
    return pl.pallas_call(
        functools.partial(input_back_kernel, bits),
        grid=(2,),
        in_specs=[
            once(other_end.shape),
            once((1, width)),
            once(vectors.shape),
            once(down_sum.shape),
            once(up_sum.shape),
            once(proj_sum.shape),
            once(qkv_keep.shape),
            once(qkv_got.shape),
            HBM,
            HBM,
            HBM,
            HBM,
            HBM,
            HBM,
        ],
        out_specs=(
            once((1, size)),
            once((rows, tiles * FF_TILE)),
            once((rows, tiles * FF_TILE)),
            once((rows, columns)),
            once((3, rows, columns)),
            HBM,
        ),
        out_shape=(
            jax.ShapeDtypeStruct((1, size), f32),
            jax.ShapeDtypeStruct((rows, tiles * FF_TILE), f32),
            jax.ShapeDtypeStruct((rows, tiles * FF_TILE), f32),
            jax.ShapeDtypeStruct((rows, columns), f32),
            jax.ShapeDtypeStruct((3, rows, columns), f32),
            jax.ShapeDtypeStruct((tokens, width), bf16),
        ),
        scratch_shapes=[
            vmem((2, width), f32),
            vmem(mine.shape, bf16),
            vmem(other.shape, bf16),
            vmem(weight.shape, bf16),
            vmem(weight_other.shape, bf16),
            vmem((half, width), bf16),
            vmem((half, width), f32),
            vmem((half, width), bf16),
            vmem((1, both), f32),
            vmem((1, both), f32),
            vmem((1, size), f32),
            vmem((bits, 1, size), f32),
            vmem((2 * tiles + 1, rows, FF_TILE), bf16),
            vmem((2 * tiles + 1, rows, FF_TILE), bf16),
            dma(6),
            dma(2),
            dma(2),
            dma(2),
            dma(2 * bits + 2),
            dma(6),
        ]
        + scratch,
        compiler_params=params(1),
        cost_estimate=pl.CostEstimate(
            flops=12 * half * width * columns, bytes_accessed=20_000_000, transcendentals=0
        ),
        name="input_backward",
    )(
        other_end,
        gain[None, :],
        vectors,
        down_sum,
        up_sum,
        proj_sum,
        qkv_keep,
        qkv_got,
        mine,
        other,
        weight,
        weight_other,
        patches,
        residual_grad,
    )


def result_kernel(sizes, vector_ref, *refs):
    count = (len(refs) - len(sizes)) // 2
    sources, targets = refs[:count], refs[count : 2 * count]
    for source, target in zip(sources[-2:], targets[-2:]):
        target[...] = source[...]

    @pl.when(pl.program_id(0) == 0)
    def _():
        for source, target in zip(sources[:-2], targets[:-2]):
            target[...] = source[...]
        begin = 0
        for size, target in zip(sizes, refs[2 * count :]):
            for row in range(size // 128):
                at = pl.ds(begin + row * 128, 128)
                target[row : row + 1, :] = vector_ref[:, at]
            begin += size


def results(vectors, sizes, arrays, rows):
    step = rows[0].shape[0] // RESULT_STEPS
    long_block = pl.BlockSpec((step, rows[0].shape[1]), lambda i: (i, 0))
    specs = [once(x.shape) for x in arrays] + [long_block] * len(rows)
    shapes = [(size // 128, 128) for size in sizes]
    out = pl.pallas_call(
        functools.partial(result_kernel, sizes),
        grid=(RESULT_STEPS,),
        in_specs=[once(vectors.shape)] + specs,
        out_specs=specs + [once(x) for x in shapes],
        out_shape=[jax.ShapeDtypeStruct(x.shape, x.dtype) for x in list(arrays) + list(rows)]
        + [jax.ShapeDtypeStruct(x, f32) for x in shapes],
        compiler_params=params(),
        name="results",
    )(vectors, *arrays, *rows)
    count = len(arrays) + len(rows)
    return out[:count], [x.reshape(-1) for x in out[count:]]


def on_device(
    count,
    patches,
    cotangent,
    clip_lengths,
    attn_gain,
    attn_shift,
    qkv_weight,
    qkv_bias,
    proj_weight,
    proj_bias,
    mlp_gain,
    mlp_shift,
    up_weight,
    up_bias,
    down_weight,
    down_bias,
):
    tokens, width = patches.shape
    local_width = proj_weight.shape[0]

    qkv_parts = jnp.transpose(qkv_weight, (1, 0, 2))

    clip_len = clip_lengths[0, 0]
    cosine, sine = rotary_angles(jnp.arange(tokens, dtype=jnp.int32) % clip_len)
    query_mask, key_mask = clip_masks(clip_len, tokens)
    (
        normed,
        qkv,
        attended,
        att_mine,
        totals,
        up_biases,
        weights,
        att_other,
        proj_other,
        up_other,
        down_part,
    ) = attend_forward(
        patches,
        attn_gain,
        attn_shift,
        qkv_parts,
        qkv_bias,
        cosine,
        sine,
        query_mask,
        key_mask,
        up_bias,
        proj_weight,
        up_weight,
        down_weight,
    )
    (
        residual_grad,
        att_grad_mine,
        att_grad_send,
        vectors,
        up_bias_grad,
        down_keep,
        up_keep,
        block_out,
        att_grad_got,
        up_got,
        down_got,
        _,
        qkv_other,
    ) = feed_forward(
        count,
        att_mine,
        att_other,
        proj_weight,
        proj_other,
        proj_bias,
        mlp_gain,
        mlp_shift,
        down_bias,
        up_biases,
        patches,
        cotangent,
        up_weight,
        up_other,
        down_weight,
        down_part,
        qkv_parts,
    )
    (
        mixed_mine,
        qkv_keep,
        qkv_bias_grad,
        down_sum,
        up_sum,
        proj_sum,
        mixed_other,
        mixed_end,
        qkv_got,
        _,
    ) = attend_backward(
        count,
        weights,
        qkv,
        attended,
        totals,
        att_grad_mine,
        att_grad_send,
        att_grad_got,
        cosine,
        sine,
        normed,
        down_keep,
        down_got,
        up_keep,
        up_got,
    )

    hidden = up_bias.shape[0]
    vectors = vectors.reshape(1, -1)
    up_bias_grad = up_bias_grad.reshape(2, hidden)
    ends = jnp.zeros((2, 2 * width), f32)
    vectors = jnp.concatenate(
        [
            ends,
            jnp.concatenate([vectors, vectors]),
            up_bias_grad,
            jnp.concatenate([qkv_bias_grad.reshape(1, -1)] * 2),
        ],
        axis=1,
    )
    vectors, down_grad, up_grad, proj_grad, qkv_grad, patch_grad = input_backward(
        count,
        mixed_mine,
        mixed_other,
        mixed_end,
        qkv_parts,
        qkv_other,
        attn_gain,
        vectors,
        down_sum,
        up_sum,
        proj_sum,
        qkv_keep,
        qkv_got,
        patches,
        residual_grad,
    )
    sizes = [width] * 6 + [hidden, 3 * local_width]
    (down_grad, up_grad, proj_grad, qkv_grad, block_out, patch_grad), pieces = results(
        vectors, sizes, [down_grad, up_grad, proj_grad, qkv_grad], [block_out, patch_grad]
    )
    attn_gain_grad, attn_shift_grad, mlp_gain_grad, mlp_shift_grad = pieces[:4]
    proj_bias_grad, down_bias_grad, up_bias_grad, qkv_bias_grad = pieces[4:]
    return (
        block_out,
        patch_grad,
        attn_gain_grad,
        attn_shift_grad,
        jnp.transpose(qkv_grad, (1, 0, 2)),
        qkv_bias_grad.reshape(3, local_width),
        proj_grad.T,
        proj_bias_grad,
        mlp_gain_grad,
        mlp_shift_grad,
        up_grad,
        up_bias_grad,
        down_grad.T,
        down_bias_grad,
    )


def solution(mesh):
    return jax.shard_map(
        functools.partial(on_device, mesh.shape["dp"]),
        mesh=mesh,
        in_specs=(
            P("dp", None),
            P("dp", None),
            P("dp", None),
            P(),
            P(),
            P(None, None, "tensor"),
            P(None, "tensor"),
            P("tensor", None),
            P(),
            P(),
            P(),
            P(None, "tensor"),
            P("tensor"),
            P("tensor", None),
            P(),
        ),
        out_specs=(
            P("dp", None),
            P("dp", None),
            P(),
            P(),
            P("dp", None, "tensor"),
            P(None, "tensor"),
            P("tensor", "dp"),
            P(),
            P(),
            P(),
            P("dp", "tensor"),
            P("tensor"),
            P("tensor", "dp"),
            P(),
        ),
        check_vma=False,
    )
```

```python
import functools
import math

import jax
import jax.numpy as jnp
from jax import lax
from jax.experimental import pallas as pl
from jax.experimental.pallas import tpu as pltpu
from jax.sharding import PartitionSpec as P

HEAD_DIM = 64
HALF_DIM = HEAD_DIM // 2
GRID = 14
IMG = 196
EPS = 1e-06
SCALING = HEAD_DIM ** (-0.5)
LOG2E = math.log2(math.e)
KEY_CHUNKS = 2
MASK_ROWS = 16
END_WIDTH = 256
RESULT_STEPS = 2
ONES_ROWS = 16
FF_TILE = 512
FORBIDDEN = -1e30
VMEM_LIMIT = 62 * 1024 * 1024

MESH = pl.DeviceIdType.MESH

bf16 = jnp.bfloat16
f32 = jnp.float32


def dot(left, right, left_dim, right_dim):
    return lax.dot_general(
        left, right, (((left_dim,), (right_dim,)), ((), ())), preferred_element_type=f32
    )


def rotary_angles(offsets):
    pair_count = HALF_DIM
    side_pairs = pair_count * 11 // 32
    time_pairs = pair_count - 2 * side_pairs
    pair_index = jnp.arange(pair_count, dtype=jnp.int32)
    time_pair = pair_index < time_pairs
    height_pair = (pair_index >= time_pairs) & (pair_index < time_pairs + side_pairs)
    group_begin = jnp.where(
        time_pair, 0, jnp.where(height_pair, time_pairs, time_pairs + side_pairs)
    )
    group_size = jnp.where(time_pair, time_pairs, side_pairs)
    inverse = jnp.power(
        10000.0, -(pair_index - group_begin).astype(f32) / group_size.astype(f32)
    )
    frame_place = (offsets // IMG).astype(f32)
    row_place = (offsets % IMG // GRID).astype(f32)
    column_place = (offsets % GRID).astype(f32)
    position = jnp.where(
        time_pair[:, None],
        frame_place[None, :],
        jnp.where(height_pair[:, None], row_place[None, :], column_place[None, :]),
    )
    angles = position * inverse[:, None]
    return (jnp.cos(angles), jnp.sin(angles))


def params(collective_id=None):
    if collective_id is None:
        return pltpu.CompilerParams(vmem_limit_bytes=VMEM_LIMIT)
    return pltpu.CompilerParams(
        vmem_limit_bytes=VMEM_LIMIT, collective_id=collective_id, has_side_effects=True
    )


def greet(partners):
    barrier = pltpu.get_barrier_semaphore()
    for partner in partners:
        pl.semaphore_signal(barrier, inc=1, device_id=partner, device_id_type=MESH)
    pl.semaphore_wait(barrier, len(partners))


def partner_of(bit):
    index = lax.axis_index("dp")
    mine = (index // (1 << bit)) % 2
    return {"dp": index + (1 << bit) * (1 - 2 * mine)}, mine


def fold(keep, got, mine, next_keep, next_send):
    lead = (slice(None),) * (len(keep.shape) - 3)
    for pair in range(keep.shape[-3] // 2):
        for ref, odd in ((next_keep, mine), (next_send, 1 - mine)):
            at = lead + (2 * pair + odd,)
            value = keep[at]
            if got is not None:
                value = value.astype(f32) + got[at].astype(f32)
            ref[lead + (pair,)] = value.astype(bf16)


def remote(source, target, send_sem, recv_sem, partner):
    return pltpu.make_async_remote_copy(
        src_ref=source,
        dst_ref=target,
        send_sem=send_sem,
        recv_sem=recv_sem,
        device_id=partner,
        device_id_type=MESH,
    )


def whole_block(shape, **kwargs):
    return pl.BlockSpec(shape, lambda *_: (0,) * len(shape), **kwargs)


def once(shape):
    return whole_block(shape, pipeline_mode=pl.Buffered(1))


HBM = pl.BlockSpec(memory_space=pl.ANY)


def clamp(value, last):
    return jnp.minimum(jnp.maximum(value, 0), last)


def norm_parts(values):
    centre = values - jnp.mean(values, axis=1, keepdims=True)
    spread = jnp.mean(centre * centre, axis=1, keepdims=True)
    scale = lax.rsqrt(spread + EPS)
    return centre * scale, scale


def norm_back(grad, unit, scale, gain):
    c = grad * gain
    mean = jnp.mean(c, axis=1, keepdims=True)
    along = jnp.mean(c * unit, axis=1, keepdims=True)
    return scale * (c - mean - unit * along)


def column_sum(values):
    return jnp.sum(values, axis=0, keepdims=True)


def clip_masks(clip_len, tokens):
    token = jnp.arange(tokens, dtype=jnp.int32)[None, :] // IMG
    row = jnp.arange(MASK_ROWS, dtype=jnp.int32)[:, None]
    same = token == row
    images = clip_len < tokens
    forbid = images & jnp.logical_not(same) & (row < tokens // IMG)
    return jnp.where(forbid, FORBIDDEN, 0.0).astype(bf16), same.astype(bf16)


class Gather:
    STAGES = ((0,), (1, 2), (3, 4, 5, 6), (7, 8, 9, 10))
    COPIES = 11
    ROUTES = (
        (None, 0, 0, None),
        (0, 0, 0, 2),
        (1, 0, 0, 1),
        (0, 0, 0, 1),
        (0, 0, 1, 1),
        (1, 0, 0, 2),
        (1, 1, 0, 2),
        (None, 0, 0, 0),
        (None, 1, 0, 0),
        (None, 0, 1, 0),
        (None, 1, 1, 0),
    )

    def __init__(self, weight, other, send_sem, recv_sem):
        self.weight, self.other = weight, other
        self.send_sem, self.recv_sem = send_sem, recv_sem

    def place(self, x, z):
        core, mine_x, mine_z = (partner_of(bit)[1] for bit in range(3))
        x = mine_x + x * (1 - 2 * mine_x)
        return core + 2 * x + 4 * (mine_z + z * (1 - 2 * mine_z)), 8

    def copy(self, number):
        half, x, z, bit = self.ROUTES[number]
        index, parts = self.place(x, z)
        rows = self.other.shape[-2] // parts
        begin = index * rows
        if half is not None:
            rows //= 2
            begin = begin + half * rows
        at = (slice(None),) * (len(self.other.shape) - 2)
        at = at + (pl.ds(pl.multiple_of(begin, rows), rows),)
        source = self.weight if number == 0 else self.other
        return remote(
            source.at[at],
            self.other.at[at],
            self.send_sem.at[number],
            self.recv_sem.at[number],
            {"tensor": 1 - lax.axis_index("tensor")} if bit is None else partner_of(bit)[0],
        )

    def start(self, stage):
        for number in self.STAGES[stage]:
            self.copy(number).start()

    def wait(self, stage):
        for number in self.STAGES[stage]:
            self.copy(number).wait()

    def advance(self, stage):
        self.wait(stage - 1)
        self.start(stage)


class GatherZ(Gather):
    STAGES = ((0,), (1,), (2, 3))
    ROUTES = ((None, 0, 0, None), (None, 0, 0, 2), (None, 0, 0, 0), (None, 0, 1, 0))

    def place(self, x, z):
        core, mine_z = partner_of(0)[1], partner_of(2)[1]
        return core + 2 * (mine_z + z * (1 - 2 * mine_z)), 4


def neighbours():
    return [{"tensor": 1 - lax.axis_index("tensor")}] + [partner_of(bit)[0] for bit in range(3)]


def attend_kernel(
    x_ref,
    gain_ref,
    shift_ref,
    w_ref,
    b_ref,
    cos_ref,
    sin_ref,
    qm_ref,
    km_ref,
    up_bias_ref,
    proj_hbm,
    up_hbm,
    down_hbm,
    normed_ref,
    qkv_ref,
    att_ref,
    mine_ref,
    factor_ref,
    biases_ref,
    e_hbm,
    other_hbm,
    proj_other,
    up_other,
    down_other,
    k_scr,
    s_scr,
    e_scr,
    outgoing,
    bias_got,
    e_sem,
    bias_sem,
    send_sem,
    recv_sem,
    gather_send,
    gather_recv,
):
    step, last = pl.program_id(0), pl.num_programs(0) - 1
    tokens, width = x_ref.shape
    half = tokens // 2
    chunk = tokens // KEY_CHUNKS
    heads = e_hbm.shape[0]
    side = lax.axis_index("tensor")
    peer = {"tensor": 1 - side}
    proj = Gather(proj_hbm, proj_other, gather_send.at[0], gather_recv.at[0])
    up = Gather(up_hbm, up_other, gather_send.at[1], gather_recv.at[1])
    down = Gather(down_hbm, down_other, gather_send.at[2], gather_recv.at[2])

    bias_far = remote(up_bias_ref, bias_got, bias_sem.at[0], bias_sem.at[1], peer)

    @pl.when(step == 0)
    def _():
        greet(neighbours())
        bias_far.start()
        proj.start(0)
        up.start(0)
        unit, _ = norm_parts(x_ref[...].astype(f32))
        normed_ref[:width] = (unit * gain_ref[...] + shift_ref[...]).astype(bf16).T
        normed_ref[width:] = jnp.ones((ONES_ROWS, tokens), bf16)

    for at, weight, stage in (
        (2, proj, 1),
        (3, down, 0),
        (4, proj, 2),
        (4, up, 1),
        (6, proj, 3),
        (6, up, 2),
        (9, up, 3),
    ):

        @pl.when(step == at)
        def _():
            if stage:
                weight.advance(stage)
            else:
                weight.start(stage)

    @pl.when(step < 3)
    def _():
        rows = w_ref.shape[2]
        bias = jnp.broadcast_to(b_ref[pl.ds(step, 1), :], (8, rows)).T[:, :1]
        mixed = dot(w_ref[0], normed_ref[:width], 0, 0) + bias

        @pl.when(step < 2)
        def _():
            cosine, sine = cos_ref[...], sin_ref[...]
            for begin in range(0, rows, HEAD_DIM):
                middle, end = begin + HALF_DIM, begin + HEAD_DIM
                low, high = mixed[begin:middle], mixed[middle:end]
                qkv_ref[step, begin:middle, :] = (low * cosine - high * sine).astype(bf16)
                qkv_ref[step, middle:end, :] = (high * cosine + low * sine).astype(bf16)

        @pl.when(step == 2)
        def _():
            qkv_ref[step] = mixed.astype(bf16)

    head = step - 3
    slot = head % 2

    def store(index, part):
        at = pl.ds(part * chunk, chunk)
        return pltpu.make_async_copy(
            e_scr.at[index % 2, at], e_hbm.at[index, at], e_sem.at[index % 2, part]
        )

    def exchange(index):
        at = pl.ds(pl.multiple_of(index * HEAD_DIM, HEAD_DIM), HEAD_DIM)
        return remote(
            outgoing.at[index],
            other_hbm.at[at],
            send_sem.at[index],
            recv_sem.at[index],
            peer,
        )

    @pl.when(head >= 2)
    def _():
        for part in range(KEY_CHUNKS):
            store(head - 2, part).wait()

    @pl.when(head >= 0)
    def _():
        at = pl.ds(pl.multiple_of(clamp(head, heads - 1) * HEAD_DIM, HEAD_DIM), HEAD_DIM)
        queries = jnp.concatenate([qkv_ref[0, at], qm_ref[...]], axis=0)
        k_scr[...] = jnp.concatenate([qkv_ref[1, at], km_ref[...]], axis=0).T
        values = jnp.concatenate([qkv_ref[2, at], jnp.ones((16, tokens), bf16)], axis=0)
        top, out, tops = None, None, []
        s_scr[0] = dot(k_scr[:chunk], queries, 1, 0)
        for part in range(KEY_CHUNKS):
            begin, end = part * chunk, (part + 1) * chunk
            if part + 1 < KEY_CHUNKS:
                s_scr[(part + 1) % 2] = dot(k_scr[end : end + chunk], queries, 1, 0)
            scores = s_scr[part % 2]
            here = jnp.max(scores, axis=0, keepdims=True)
            new_top = here if top is None else jnp.maximum(top, here)
            weights = jnp.exp2((scores - new_top) * (SCALING * LOG2E)).astype(bf16)
            e_scr[slot, begin:end] = weights
            store(head, part).start()
            term = dot(values[:, begin:end], weights, 1, 0)
            if out is None:
                out = term
            else:
                out = out * jnp.exp2((top - new_top) * (SCALING * LOG2E)) + term
            top = new_top
            tops.append(top)
        scale = 1.0 / out[HEAD_DIM : HEAD_DIM + 1]
        for part in range(KEY_CHUNKS):
            factor_ref[0, part : part + 1] = scale * jnp.exp2(
                (tops[part] - top) * (SCALING * LOG2E)
            )
        attended = out[:HEAD_DIM] * scale
        att_ref[...] = attended.astype(bf16)
        left, right = attended[:, :half], attended[:, half:]
        mine_ref[...] = jnp.where(side == 0, left, right).astype(bf16)
        outgoing[clamp(head, heads - 1)] = jnp.where(side == 0, right, left).astype(bf16)
        exchange(head).start()

    @pl.when(step == last)
    def _():
        for back in (2, 1):
            for part in range(KEY_CHUNKS):
                store(heads - back, part).wait()
        for index in range(heads):
            exchange(index).wait()
        bias_far.wait()
        biases_ref[: bias_got.shape[0]] = up_bias_ref[...]
        biases_ref[bias_got.shape[0] :] = bias_got[...]
        for weight, stage in ((proj, 3), (up, 3), (down, 0)):
            weight.wait(stage)


def attend_forward(
    patches,
    gain,
    shift,
    weight,
    bias,
    cosine,
    sine,
    query_mask,
    key_mask,
    up_bias,
    proj,
    up,
    down,
):
    tokens, width = patches.shape
    columns = weight.shape[2]
    heads = columns // HEAD_DIM
    half = tokens // 2
    head = lambda i: clamp(i - 3, heads - 1)
    tiles = up_bias.shape[0] // FF_TILE
    vmem = pltpu.VMEM
    dma = lambda *shape: pltpu.SemaphoreType.DMA(shape)
    return pl.pallas_call(
        attend_kernel,
        grid=(3 + heads,),
        out_shape=(
            jax.ShapeDtypeStruct((width + ONES_ROWS, tokens), bf16),
            jax.ShapeDtypeStruct((3, columns, tokens), bf16),
            jax.ShapeDtypeStruct((columns, tokens), bf16),
            jax.ShapeDtypeStruct((columns, half), bf16),
            jax.ShapeDtypeStruct((heads, KEY_CHUNKS, tokens), f32),
            jax.ShapeDtypeStruct((2 * tiles, 1, FF_TILE), f32),
            jax.ShapeDtypeStruct((heads, tokens, tokens), bf16),
            jax.ShapeDtypeStruct((columns, half), bf16),
            jax.ShapeDtypeStruct(proj.shape, bf16),
            jax.ShapeDtypeStruct(up.shape, bf16),
            jax.ShapeDtypeStruct(down.shape, bf16),
        ),
        in_specs=[
            once((tokens, width)),
            once((1, width)),
            once((1, width)),
            pl.BlockSpec((1, width, columns), lambda i: (clamp(i, 2), 0, 0)),
            once((3, columns)),
            once(cosine.shape),
            once(sine.shape),
            once(query_mask.shape),
            once(key_mask.shape),
            once((tiles, 1, FF_TILE)),
            HBM,
            HBM,
            HBM,
        ],
        out_specs=(
            once((width + ONES_ROWS, tokens)),
            once((3, columns, tokens)),
            pl.BlockSpec((HEAD_DIM, tokens), lambda i: (head(i), 0)),
            pl.BlockSpec((HEAD_DIM, half), lambda i: (head(i), 0)),
            pl.BlockSpec((1, KEY_CHUNKS, tokens), lambda i: (head(i), 0, 0)),
            once((2 * tiles, 1, FF_TILE)),
            HBM,
            HBM,
            HBM,
            HBM,
            HBM,
        ),
        scratch_shapes=[
            vmem((tokens, HEAD_DIM + MASK_ROWS), bf16),
            vmem((2, tokens // KEY_CHUNKS, tokens), f32),
            vmem((2, tokens, tokens), bf16),
            vmem((heads, HEAD_DIM, half), bf16),
            vmem((tiles, 1, FF_TILE), f32),
            dma(2, KEY_CHUNKS),
            dma(2),
            dma(heads),
            dma(heads),
            dma(3, Gather.COPIES),
            dma(3, Gather.COPIES),
        ],
        compiler_params=params(3),
        cost_estimate=pl.CostEstimate(
            flops=6 * tokens * width * columns + 16 * heads * tokens * tokens * HEAD_DIM,
            bytes_accessed=60_000_000,
            transcendentals=heads * tokens * tokens,
        ),
        name="attend_forward",
    )(
        patches,
        gain[None, :],
        shift[None, :],
        weight,
        bias,
        cosine,
        sine,
        query_mask,
        key_mask,
        up_bias.reshape(tiles, 1, FF_TILE),
        proj,
        up,
        down,
    )


def attend_back_kernel(
    e_ref,
    q_ref,
    k_ref,
    v_ref,
    out_ref,
    total_ref,
    att_grad_ref,
    cos_ref,
    sin_ref,
    normed_ref,
    down_keep_ref,
    down_got_ref,
    up_keep_ref,
    up_got_ref,
    att_send_hbm,
    _,
    mine_ref,
    keep_ref,
    sum_ref,
    down_sum_ref,
    up_sum_ref,
    proj_sum_ref,
    other_ref,
    other_end_ref,
    got_ref,
    att_got_hbm,
    att_scr,
    up_scr,
    up_low,
    value_scr,
    v_scr,
    score_grad,
    turned,
    pair_scr,
    outgoing,
    outgoing_end,
    grad,
    outgoing_core,
    down_scr,
    down_last,
    up_first,
    up_last,
    send_sem,
    recv_sem,
    end_sem,
    core_send,
    core_recv,
    down_sem,
    down_last_sem,
    up_sem,
    up_last_sem,
    att_sem,
    att_load_sem,
):
    head, heads = pl.program_id(0), pl.num_programs(0)
    tokens = q_ref.shape[2]
    half = tokens // 2
    side = lax.axis_index("tensor")
    peer = {"tensor": 1 - side}
    core_partner, core = partner_of(0)
    slot = head % 2
    def exchange(index):
        return remote(
            outgoing.at[index % 4],
            other_ref.at[index],
            send_sem.at[index % 4],
            recv_sem.at[index],
            peer,
        )

    end_far = remote(outgoing_end, other_end_ref, end_sem.at[0], end_sem.at[1], peer)
    lanes = half // 128 * 128
    end_width = outgoing_end.shape[1] // heads

    def to_core(pair):
        at = pl.ds(pl.multiple_of(pair * 2 * HEAD_DIM, 2 * HEAD_DIM), 2 * HEAD_DIM)
        return remote(
            outgoing_core.at[pair % 2],
            got_ref.at[:, :, :, at],
            core_send.at[pair % 2],
            core_recv.at[pair],
            core_partner,
        )

    def hop(buffers, sems, pair, bit):
        at = pl.ds(2 * pair, 2)
        return remote(
            buffers.at[1, at],
            buffers.at[2, at],
            sems.at[0, pair],
            sems.at[1, pair],
            partner_of(bit)[0],
        )

    def start(keep, got, buffers, sems, pair, bit):
        at = pl.ds(2 * pair, 2)
        fold(keep, got, partner_of(bit)[1], buffers.at[0, at], buffers.at[1, at])
        hop(buffers, sems, pair, bit).start()

    def relay(source, source_sems, source_bit, buffers, sems, pair, bit):
        hop(source, source_sems, pair, source_bit).wait_recv()
        at = pl.ds(2 * pair, 2)
        start(source.at[0, at], source.at[2, at], buffers, sems, pair, bit)

    down_pairs, up_pairs = down_scr.shape[1] // 2, up_last.shape[1] // 2
    behind = heads - up_pairs

    late_heads = pl.ds(att_got_hbm.shape[0] // 2, att_got_hbm.shape[0] // 2)
    att_far = remote(
        att_send_hbm.at[late_heads], att_got_hbm.at[late_heads], att_sem.at[0], att_sem.at[1], peer
    )

    def att_load(index):
        at = pl.ds(pl.multiple_of(index * HEAD_DIM, HEAD_DIM), HEAD_DIM)
        return pltpu.make_async_copy(
            att_got_hbm.at[at], att_scr.at[index % 2], att_load_sem.at[index % 2]
        )

    @pl.when(head == 0)
    def _():
        att_load(0).start()
        greet(neighbours() + [partner_of(3)[0]])
        att_far.start()

    @pl.when(head >= 4)
    def _():
        exchange(head - 4).wait_send()

    @pl.when(head <= up_pairs)
    def _():
        start(up_keep_ref, up_got_ref, up_first, up_sem, head, 1)

    @pl.when(head < down_pairs)
    def _():
        start(down_keep_ref, down_got_ref, down_scr, down_sem, head, 2)

    @pl.when(head >= heads - down_pairs)
    def _():
        relay(
            down_scr, down_sem, 2, down_last, down_last_sem, head - (heads - down_pairs), 3
        )

    @pl.when(head >= behind)
    def _():
        relay(up_first, up_sem, 1, up_last, up_last_sem, head - behind, 2)

    @pl.when(head + 1 == heads // 2)
    def _():
        att_far.wait_recv()

    @pl.when(head + 1 < heads)
    def _():
        att_load(head + 1).start()

    att_load(head).wait()
    chunks = total_ref.shape[1]
    chunk = tokens // chunks
    att_mine, att_other = att_grad_ref[...].astype(f32), att_scr[slot].astype(f32)
    up_scr[:, :half] = jnp.where(side == 0, att_mine, att_other)
    up_scr[:, half:] = jnp.where(side == 0, att_other, att_mine)
    attended = out_ref[...].astype(f32)
    centre = []
    for part in range(chunks):
        up_low[part] = (up_scr[...] * total_ref[0, part : part + 1]).astype(bf16)
        centre.append(column_sum(up_low[part].astype(f32) * attended))
    v_scr[...] = v_ref[0].T
    cosine, sine = cos_ref[...], sin_ref[...]

    ends = {}

    def store(part, low, high):
        for row, value in ((0, low), (HALF_DIM, high)):
            left, right = value[:, :half], value[:, half:]
            mine_ref[part, row : row + HALF_DIM] = jnp.where(side == 0, left, right).astype(bf16)
            theirs = jnp.where(side == 0, right, left)
            outgoing[head % 4, part, row : row + HALF_DIM] = theirs[:, :lanes].astype(bf16)
            ends[part, row // HALF_DIM] = theirs[:, lanes:]
            begin = pl.multiple_of(part * 2 * HEAD_DIM + slot * HEAD_DIM + row, HALF_DIM)
            pair_scr[pl.ds(begin, HALF_DIM)] = value.astype(bf16)

    def unrotated(part, grad):
        low, high = grad[:HALF_DIM] * SCALING, grad[HALF_DIM:] * SCALING
        store(part, low * cosine + high * sine, high * cosine - low * sine)

    for part in range(chunks):
        at = slice(part * chunk, (part + 1) * chunk)
        value_scr[:, at] = dot(up_low[part], e_ref[0, at], 1, 1)
        prob_grad = dot(v_scr[at], up_low[part], 1, 0)
        score_grad[at] = (e_ref[0, at].astype(f32) * (prob_grad - centre[part])).astype(bf16)
    store(2, value_scr[:HALF_DIM], value_scr[HALF_DIM:])
    unrotated(0, dot(k_ref[0], score_grad[...], 1, 0))
    turned[...] = score_grad[...].T
    unrotated(1, dot(q_ref[0], turned[...], 1, 0))
    exchange(head).start()
    end = jnp.concatenate([ends[part, row] for part in range(3) for row in range(2)], axis=0)
    end = jnp.concatenate([end, jnp.zeros((end_width - end.shape[0], end.shape[1]), f32)], axis=0)
    begin = pl.multiple_of(head * end_width, end_width)
    outgoing_end[:, pl.ds(begin, end_width)] = end.T.astype(bf16)

    @pl.when(slot == 1)
    def _():
        pair = head // 2
        width = grad.shape[0] - ONES_ROWS
        grad[...] = dot(normed_ref[...], pair_scr[...], 1, 1)

        @pl.when(pair >= 2)
        def _():
            to_core(pair - 2).wait_send()

        for part in range(3):
            lanes = pl.ds(part * 2 * HEAD_DIM, 2 * HEAD_DIM)
            split_rows(
                grad.at[:, lanes], keep_ref.at[part], outgoing_core.at[pair % 2, part], core
            )
            sum_ref[part : part + 1] = grad[width : width + 1, lanes]
        to_core(pair).start()

    @pl.when(head == heads - 1)
    def _():
        end_far.start()
        for back in range(4):
            exchange(heads - 1 - back).wait_send()
        for back in range(2):
            to_core(heads // 2 - 1 - back).wait_send()
        for index in range(other_ref.shape[0] // 2):
            to_core(index).wait_recv()
        for pair in range(down_pairs):
            hop(down_scr, down_sem, pair, 2).wait_send()
            hop(down_last, down_last_sem, pair, 3).wait()
        down_sum_ref[...] = down_last[0].astype(f32) + down_last[2].astype(f32)
        for pair in range(up_pairs):
            hop(up_first, up_sem, pair, 1).wait_send()
            hop(up_last, up_last_sem, pair, 2).wait()
        up_sum_ref[...] = (up_last[0].astype(f32) + up_last[2].astype(f32)).astype(bf16)
        hop(up_first, up_sem, up_pairs, 1).wait()
        at = pl.ds(2 * up_pairs, 2)
        proj_sum_ref[...] = (up_first[0, at].astype(f32) + up_first[2, at].astype(f32)).astype(bf16)
        att_far.wait_send()
        end_far.wait()
        for index in range(other_ref.shape[0]):
            exchange(index).wait_recv()


def attend_backward(
    count,
    weights,
    qkv,
    attended,
    totals,
    att_grad,
    att_send,
    att_got,
    cosine,
    sine,
    normed,
    down_keep,
    down_got,
    up_keep,
    up_got,
):
    tokens = qkv.shape[2]
    half = tokens // 2
    heads = weights.shape[0]
    columns = heads * HEAD_DIM
    width = normed.shape[0] - ONES_ROWS
    rows = width // count
    split = (3, count // 2, rows)
    blocks = lambda bits: (count >> bits, rows, FF_TILE)
    pair = lambda lead, first, last: pl.BlockSpec(
        (2,) + lead, lambda i: (first + clamp(i, last), 0, 0, 0)
    )
    block = lambda part: pl.BlockSpec((1, HEAD_DIM, tokens), lambda i: (part, i, 0))
    half_block = pl.BlockSpec((HEAD_DIM, half), lambda i: (i, 0))
    lanes = half // 128 * 128
    pair_block = pl.BlockSpec(split + (2 * HEAD_DIM,), lambda i: (0, 0, 0, i // 2))
    vmem = pltpu.VMEM
    dma = lambda *shape: pltpu.SemaphoreType.DMA(shape)
    return pl.pallas_call(
        attend_back_kernel,
        grid=(heads,),
        out_shape=(
            jax.ShapeDtypeStruct((3, columns, half), bf16),
            jax.ShapeDtypeStruct(split + (columns,), bf16),
            jax.ShapeDtypeStruct((3, columns), f32),
            jax.ShapeDtypeStruct((heads,) + blocks(4), f32),
            jax.ShapeDtypeStruct((heads,) + blocks(3), bf16),
            jax.ShapeDtypeStruct((2,) + blocks(2), bf16),
            jax.ShapeDtypeStruct((heads, 3, HEAD_DIM, lanes), bf16),
            jax.ShapeDtypeStruct((half - lanes, heads * END_WIDTH), bf16),
            jax.ShapeDtypeStruct(split + (columns,), bf16),
            jax.ShapeDtypeStruct(att_got.shape, bf16),
        ),
        input_output_aliases={15: 9},
        in_specs=[
            pl.BlockSpec((1, tokens, tokens), lambda i: (i, 0, 0)),
            block(0),
            block(1),
            block(2),
            pl.BlockSpec((HEAD_DIM, tokens), lambda i: (i, 0)),
            pl.BlockSpec((1, totals.shape[1], tokens), lambda i: (i, 0, 0)),
            half_block,
            once(cosine.shape),
            once(sine.shape),
            once(normed.shape),
            pair(blocks(2), 0, heads // 2 - 1),
            pair(blocks(2), 0, heads // 2 - 1),
            pair(blocks(1), 0, heads // 2),
            pair(blocks(1), heads // 2, heads // 2),
            HBM,
            HBM,
        ],
        out_specs=(
            pl.BlockSpec((3, HEAD_DIM, half), lambda i: (0, i, 0)),
            pair_block,
            pl.BlockSpec((3, 2 * HEAD_DIM), lambda i: (0, i // 2)),
            once((heads,) + blocks(4)),
            once((heads,) + blocks(3)),
            once((2,) + blocks(2)),
            HBM,
            HBM,
            HBM,
            HBM,
        ),
        scratch_shapes=[
            vmem((2, HEAD_DIM, half), bf16),
            vmem((HEAD_DIM, tokens), f32),
            vmem((totals.shape[1], HEAD_DIM, tokens), bf16),
            vmem((HEAD_DIM, tokens), f32),
            vmem((tokens, HEAD_DIM), bf16),
            vmem((tokens, tokens), bf16),
            vmem((tokens, tokens), bf16),
            vmem((6 * HEAD_DIM, tokens), bf16),
            vmem((4, 3, HEAD_DIM, lanes), bf16),
            vmem((half - lanes, heads * END_WIDTH), bf16),
            vmem((width + ONES_ROWS, 6 * HEAD_DIM), f32),
            vmem((2,) + split + (2 * HEAD_DIM,), bf16),
            vmem((3, heads) + blocks(3), bf16),
            vmem((3, heads) + blocks(4), bf16),
            vmem((3, heads + 2) + blocks(2), bf16),
            vmem((3, heads) + blocks(3), bf16),
            dma(4),
            dma(heads),
            dma(2),
            dma(2),
            dma(heads // 2),
            dma(2, heads // 2),
            dma(2, heads // 2),
            dma(2, heads // 2 + 1),
            dma(2, heads // 2),
            dma(2),
            dma(2),
        ],
        compiler_params=params(0),
        cost_estimate=pl.CostEstimate(
            flops=32 * heads * tokens * tokens * HEAD_DIM,
            bytes_accessed=2 * heads * tokens * tokens,
            transcendentals=0,
        ),
        name="attend_backward",
    )(
        weights,
        qkv,
        qkv,
        qkv,
        attended,
        totals,
        att_grad,
        cosine,
        sine,
        normed,
        down_keep,
        down_got,
        up_keep,
        up_got,
        att_send,
        att_got,
    )


def normal_parts(value):
    a = jnp.abs(value)
    t = 1.0 / (1.0 + (0.3275911 / math.sqrt(2.0)) * a)
    bell = jnp.exp2(value * value * (-0.5 * LOG2E))
    c = [0.5 * x for x in (0.254829592, -0.284496736, 1.421413741, -1.453152027, 1.061405429)]
    tail = ((((c[4] * t + c[3]) * t + c[2]) * t + c[1]) * t + c[0]) * t * bell
    return jnp.where(value >= 0, 1.0 - tail, tail), bell * (1.0 / math.sqrt(2.0 * math.pi))


def split_rows(grad, keep_ref, send_ref, core):
    count, rows = keep_ref.shape[:2]
    for pair in range(count):
        for ref, odd in ((keep_ref, core), (send_ref, 1 - core)):
            begin = pl.multiple_of((2 * pair + odd) * rows, rows)
            ref[pair] = grad[pl.ds(begin, rows), :].astype(bf16)


def accumulate(step, total, term):
    @pl.when(step == 0)
    def _():
        total[...] = term

    @pl.when(step > 0)
    def _():
        total[...] += term


def feed_kernel(
    att_ref,
    att_other_ref,
    proj_ref,
    proj_other_ref,
    proj_bias_ref,
    gain_ref,
    shift_ref,
    down_bias_ref,
    up_bias_ref,
    patch_hbm,
    cot_hbm,
    up_hbm,
    up_other_hbm,
    down_hbm,
    _,
    qkv_hbm,
    grad_ref,
    att_grad_ref,
    att_scr,
    vector_ref,
    up_bias_grad_ref,
    keep_x_ref,
    keep_ref,
    out_hbm,
    att_got_hbm,
    got_hbm,
    got_x_hbm,
    down_other_hbm,
    qkv_other_hbm,
    n_scr,
    cot_scr,
    out_scr,
    total,
    act_scr,
    slope_scr,
    up_scr,
    down_scr,
    low_scr,
    grad_scr,
    keep_ring,
    outgoing,
    arrived,
    outgoing_x,
    load_sem,
    up_sem,
    down_sem,
    store_sem,
    row_sem,
    att_sem,
    send_sem,
    recv_sem,
    arrive_sem,
    send_x_sem,
    recv_x_sem,
    gather_send,
    gather_recv,
):
    step, last = pl.program_id(0), pl.num_programs(0) - 1
    tiles = act_scr.shape[0]
    half_tiles = tiles // 2
    half = n_scr.shape[0]
    side = lax.axis_index("tensor")
    peer = {"tensor": 1 - side}
    core_partner, core = partner_of(0)
    x_partner, x_side = partner_of(1)
    mine = pl.ds(pl.multiple_of(side * half, 16), half)
    gather_down = Gather(down_hbm, down_other_hbm, gather_send.at[0], gather_recv.at[0])
    gather_qkv = GatherZ(qkv_hbm, qkv_other_hbm, gather_send.at[1], gather_recv.at[1])
    patch_load = pltpu.make_async_copy(patch_hbm.at[mine], out_scr, load_sem.at[0])
    cot_load = pltpu.make_async_copy(cot_hbm.at[mine], cot_scr, load_sem.at[1])
    out_near = pltpu.make_async_copy(out_scr, out_hbm.at[mine], store_sem)
    out_far = remote(out_scr, out_hbm.at[mine], row_sem.at[0], row_sem.at[1], peer)
    early_heads = pl.ds(0, att_scr.shape[0] // 2)
    att_far = remote(
        att_scr.at[early_heads], att_got_hbm.at[early_heads], att_sem.at[0], att_sem.at[1], peer
    )

    def load_up(tile, act):
        for begin, source in ((0, up_hbm), (half_tiles, up_other_hbm)):

            @pl.when((tile >= begin) & (tile < begin + half_tiles))
            def _():
                at = pl.ds(pl.multiple_of((tile - begin) * FF_TILE, FF_TILE), FF_TILE)
                copy = pltpu.make_async_copy(
                    source.at[:, at], up_scr.at[tile % 2], up_sem.at[tile % 2]
                )
                getattr(copy, act)()

    def load_down(tile, act):
        for begin, source in ((0, down_hbm), (half_tiles, down_other_hbm)):

            @pl.when((tile >= begin) & (tile < begin + half_tiles))
            def _():
                at = pl.ds(pl.multiple_of((tile - begin) * FF_TILE, FF_TILE), FF_TILE)
                copy = pltpu.make_async_copy(
                    source.at[at], down_scr.at[tile % 2], down_sem.at[tile % 2]
                )
                getattr(copy, act)()

    def to_core(index):
        return remote(
            outgoing.at[index % 2],
            got_hbm.at[index],
            send_sem.at[index % 2],
            recv_sem.at[index],
            core_partner,
        )

    def to_x(index):
        return remote(
            outgoing_x.at[index],
            got_x_hbm.at[index],
            send_x_sem.at[index],
            recv_x_sem.at[index],
            x_partner,
        )

    def arrive(index):
        return pltpu.make_async_copy(
            got_hbm.at[index], arrived.at[index % 2], arrive_sem.at[index % 2]
        )

    @pl.when(step == 0)
    def _():
        patch_load.start()
        cot_load.start()
        load_up(0, "start")
        greet(neighbours())
        gather_down.start(1)
        gather_qkv.start(0)
        branch = dot(att_ref[...], proj_ref[...], 0, 0).astype(bf16).astype(f32)
        other = dot(att_other_ref[...], proj_other_ref[...], 0, 0).astype(bf16).astype(f32)
        patch_load.wait()
        residual = out_scr[...].astype(f32) + (branch + other + proj_bias_ref[...])
        grad_ref[...] = residual
        unit, _ = norm_parts(residual)
        n_scr[...] = (unit * gain_ref[...] + shift_ref[...]).astype(bf16)
        cot_load.wait()
        vector_ref[3:4] = column_sum(cot_scr[...].astype(f32))

    slot = step % 2

    for at, weight, stage in (
        (half_tiles - 1, gather_down, 2),
        (tiles, gather_down, 3),
        (tiles + 4, gather_qkv, 1),
        (2 * tiles + 4, gather_qkv, 2),
    ):

        @pl.when(step == at)
        def _():
            weight.advance(stage)

    @pl.when(step == tiles + half_tiles - 1)
    def _():
        gather_down.wait(3)

    first, second, third = step, step - tiles, step - 2 * tiles

    @pl.when(first + 1 < tiles)
    def _():
        load_up(first + 1, "start")

    @pl.when(first < tiles)
    def _():
        load_up(first, "wait")

    @pl.when((second + 1 >= 0) & (second + 1 < tiles))
    def _():
        load_down(second + 1, "start")

    @pl.when((second >= 0) & (second < tiles))
    def _():
        load_down(second, "wait")

    @pl.when((third + 1 >= 0) & (third + 1 < tiles))
    def _():
        load_up(third + 1, "start")
        load_down(third + 1, "start")

    @pl.when((third >= 0) & (third < tiles))
    def _():
        load_up(third, "wait")
        load_down(third, "wait")

    item = jnp.where(step < tiles, step, step - 2 * tiles)
    sends = (step < tiles) | (step >= 3 * tiles)

    @pl.when(sends & (item >= 2))
    def _():
        to_core(item - 2).wait_send()

    def send_gradient(value, keep):
        grad_scr[...] = value
        split_rows(grad_scr, keep, outgoing.at[slot], core)
        to_core(item).start()

    @pl.when(first < tiles)
    def _():
        upward = dot(n_scr[...], up_scr[slot], 1, 0) + up_bias_ref[clamp(first, tiles - 1)]
        share, density = normal_parts(upward)
        activated = (upward * share).astype(bf16)
        act_scr[clamp(first, tiles - 1)] = activated
        slope_scr[clamp(first, tiles - 1)] = (share + upward * density).astype(bf16)
        send_gradient(dot(cot_scr[...], activated, 0, 0), keep_ring.at[clamp(first, tiles - 1)])

    @pl.when((second >= 0) & (second < tiles))
    def _():
        accumulate(second, total, dot(act_scr[clamp(second, tiles - 1)], down_scr[slot], 1, 0))

    @pl.when(second == tiles - 1)
    def _():
        out_scr[...] = (grad_ref[...] + (total[...] + down_bias_ref[...])).astype(bf16)
        out_near.start()
        out_far.start()

    @pl.when((third >= 0) & (third < tiles))
    def _():
        tile = clamp(third, tiles - 1)
        act_grad = dot(cot_scr[...], down_scr[slot], 1, 1)
        upward_grad = (act_grad * slope_scr[tile].astype(f32)).astype(bf16)
        slope_scr[tile] = upward_grad
        up_bias_grad_ref[0] = column_sum(upward_grad.astype(f32))
        accumulate(third, total, dot(upward_grad, up_scr[slot], 1, 1))

    @pl.when(third == tiles - 1)
    def _():
        unit, scale = norm_parts(grad_ref[...])
        normed_grad = total[...]
        residual_grad = cot_scr[...].astype(f32) + norm_back(
            normed_grad, unit, scale, gain_ref[...]
        )
        low = residual_grad.astype(bf16)
        grad_ref[...] = residual_grad
        low_scr[...] = low
        att_scr[...] = dot(proj_other_ref[...], low, 1, 1).astype(bf16)
        att_far.start()
        att_grad_ref[...] = dot(proj_ref[...], low, 1, 1).astype(bf16)
        vector_ref[0:1] = column_sum(normed_grad * unit)
        vector_ref[1:2] = column_sum(normed_grad)
        vector_ref[2:3] = column_sum(low.astype(f32))

    fourth = step - 3 * tiles

    @pl.when((fourth >= 0) & (fourth < tiles))
    def _():
        value = dot(n_scr[...], slope_scr[clamp(fourth, tiles - 1)], 0, 0)
        send_gradient(value, keep_ref.at[0])

    @pl.when(fourth == tiles)
    def _():
        send_gradient(dot(low_scr[...], att_ref[...], 0, 1), keep_ref.at[0])

    @pl.when(fourth == tiles + 1)
    def _():
        send_gradient(dot(low_scr[...], att_other_ref[...], 0, 1), keep_ref.at[0])

    @pl.when((second + 1 >= 0) & (second + 1 < tiles))
    def _():
        to_core(second + 1).wait_recv()
        arrive(second + 1).start()

    @pl.when((second >= 0) & (second < tiles))
    def _():
        arrive(second).wait()
        tile = clamp(second, tiles - 1)
        fold(
            keep_ring.at[tile],
            arrived.at[tile % 2],
            x_side,
            keep_x_ref.at[0],
            outgoing_x.at[tile],
        )
        to_x(tile).start()

    @pl.when(step == last)
    def _():
        gather_qkv.wait(2)
        items = got_hbm.shape[0] - 1
        to_core(items - 2).wait_send()
        to_core(items - 1).wait_send()
        for index in range(tiles, items):
            to_core(index).wait_recv()
        for index in range(tiles):
            to_x(index).wait()
        att_far.wait()
        out_near.wait()
        out_far.wait()


def feed_forward(
    count,
    att_mine,
    att_other,
    proj,
    proj_other,
    proj_bias,
    gain,
    shift,
    down_bias,
    up_bias,
    patches,
    cot,
    up,
    up_other,
    down,
    down_part,
    qkv,
):
    tokens, width = patches.shape
    half = tokens // 2
    columns = proj.shape[0]
    tiles = 2 * up.shape[1] // FF_TILE
    items = 2 * tiles + 2
    row = once((1, width))
    left = (width // count, FF_TILE)
    tile = lambda first, lead, size: pl.BlockSpec(
        (1,) + lead, lambda i: (clamp(i - first, size - 1),) + (0,) * len(lead)
    )
    vmem = pltpu.VMEM
    dma = lambda *shape: pltpu.SemaphoreType.DMA(shape)
    return pl.pallas_call(
        feed_kernel,
        grid=(4 * tiles + 2,),
        in_specs=[
            once((columns, half)),
            once((columns, half)),
            once(proj.shape),
            once(proj.shape),
            row,
            row,
            row,
            row,
            once(up_bias.shape),
            HBM,
            HBM,
            HBM,
            HBM,
            HBM,
            HBM,
            HBM,
        ],
        out_specs=(
            once((half, width)),
            once((columns, half)),
            once((columns, half)),
            once((4, width)),
            tile(2 * tiles, (1, FF_TILE), tiles),
            tile(tiles, (count // 4,) + left, tiles),
            tile(3 * tiles, (count // 2,) + left, tiles + 2),
            HBM,
            HBM,
            HBM,
            HBM,
            HBM,
            HBM,
        ),
        out_shape=(
            jax.ShapeDtypeStruct((half, width), f32),
            jax.ShapeDtypeStruct((columns, half), bf16),
            jax.ShapeDtypeStruct((columns, half), bf16),
            jax.ShapeDtypeStruct((4, width), f32),
            jax.ShapeDtypeStruct((tiles, 1, FF_TILE), f32),
            jax.ShapeDtypeStruct((tiles, count // 4) + left, bf16),
            jax.ShapeDtypeStruct((tiles + 2, count // 2) + left, bf16),
            jax.ShapeDtypeStruct((tokens, width), bf16),
            jax.ShapeDtypeStruct((columns, half), bf16),
            jax.ShapeDtypeStruct((items + 1, count // 2) + left, bf16),
            jax.ShapeDtypeStruct((tiles, count // 4) + left, bf16),
            jax.ShapeDtypeStruct(down.shape, bf16),
            jax.ShapeDtypeStruct(qkv.shape, bf16),
        ),
        input_output_aliases={14: 11},
        scratch_shapes=[
            vmem((half, width), bf16),
            vmem((half, width), bf16),
            vmem((half, width), bf16),
            vmem((half, width), f32),
            vmem((tiles, half, FF_TILE), bf16),
            vmem((tiles, half, FF_TILE), bf16),
            vmem((2, width, FF_TILE), bf16),
            vmem((2, FF_TILE, width), bf16),
            vmem((half, width), bf16),
            vmem((width, FF_TILE), f32),
            vmem((tiles, count // 2) + left, bf16),
            vmem((2, count // 2) + left, bf16),
            vmem((2, count // 2) + left, bf16),
            vmem((tiles, count // 4) + left, bf16),
            dma(2),
            dma(2),
            dma(2),
            pltpu.SemaphoreType.DMA,
            dma(2),
            dma(2),
            dma(2),
            dma(items),
            dma(2),
            dma(tiles),
            dma(tiles),
            dma(2, Gather.COPIES),
            dma(2, Gather.COPIES),
        ],
        compiler_params=params(2),
        cost_estimate=pl.CostEstimate(
            flops=12 * half * width * tiles * FF_TILE,
            bytes_accessed=60_000_000,
            transcendentals=half * tiles * FF_TILE,
        ),
        name="feed_forward",
    )(
        att_mine,
        att_other,
        proj,
        proj_other,
        proj_bias[None, :],
        gain[None, :],
        shift[None, :],
        down_bias[None, :],
        up_bias,
        patches,
        cot,
        up,
        up_other,
        down,
        down_part,
        qkv,
    )


class Chain:
    def __init__(self, keep, got, bits, scratch):
        self.keep, self.got, self.bits, self.scratch = keep, got, list(bits), list(scratch)
        self.last = None

    def step(self):
        if self.last is not None:
            self.copy(*self.last).wait()
            self.last = None
        if not self.bits:
            return
        bit = self.bits.pop(0)
        keep, send, got, sem = self.scratch.pop(0)
        fold(self.keep, self.got, partner_of(bit)[1], keep, send)
        self.last = (bit, send, got, sem)
        self.copy(*self.last).start()
        self.keep, self.got = keep, got

    def finish(self):
        while self.bits:
            self.step()
        self.step()

    def copy(self, bit, send, got, sem):
        return remote(send, got, sem.at[0], sem.at[1], partner_of(bit)[0])

    def result(self, tile):
        value = self.keep[tile, 0].astype(f32)
        return value if self.got is None else value + self.got[tile, 0].astype(f32)


def input_back_kernel(
    bits,
    other_end_ref,
    gain_ref,
    vector_ref,
    down_sum,
    up_sum,
    proj_sum,
    qkv_keep,
    qkv_got,
    mine_hbm,
    other_hbm,
    w_hbm,
    w_other_hbm,
    x_hbm,
    grad_hbm,
    total_ref,
    down_ref,
    up_ref,
    proj_ref,
    qkv_ref,
    out_hbm,
    total,
    mine_ref,
    other_ref,
    w_ref,
    w_other_ref,
    x_scr,
    grad_scr,
    out_scr,
    vector_send,
    vector_got,
    vector_scr,
    vector_next,
    side_send,
    side_got,
    load_sem,
    store_sem,
    row_send,
    row_recv,
    vector_sem,
    side_sem,
    *scratch,
):
    step = pl.program_id(0)
    half, width = grad_scr.shape
    side = lax.axis_index("tensor")
    peer = {"tensor": 1 - side}
    mine = pl.ds(pl.multiple_of(side * half, 16), half)
    loads = [
        pltpu.make_async_copy(x_hbm.at[mine], x_scr, load_sem.at[0]),
        pltpu.make_async_copy(grad_hbm, grad_scr, load_sem.at[1]),
        pltpu.make_async_copy(w_hbm, w_ref, load_sem.at[2]),
        pltpu.make_async_copy(mine_hbm, mine_ref, load_sem.at[3]),
        pltpu.make_async_copy(w_other_hbm, w_other_ref, load_sem.at[4]),
        pltpu.make_async_copy(other_hbm, other_ref, load_sem.at[5]),
    ]
    stages, rest = [], list(scratch)
    for first in (4, 3, 2, 1):
        stages.append([tuple(rest[4 * i : 4 * i + 4]) for i in range(bits - first)])
        rest = rest[4 * (bits - first) :]
    down = Chain(down_sum, None, range(4, bits), stages[0])
    up = Chain(up_sum, None, range(3, bits), stages[1])
    proj = Chain(proj_sum, None, range(2, bits), stages[2])
    qkv = Chain(qkv_keep, qkv_got, range(1, bits), stages[3])
    tiles = down_ref.shape[1] // FF_TILE
    early_down = not down.bits

    def side_copy(at, size):
        return remote(
            side_send.at[pl.ds(at, size)],
            side_got.at[pl.ds(at, size)],
            side_sem.at[2 * (at // tiles)],
            side_sem.at[2 * (at // tiles) + 1],
            peer,
        )

    def other_side(parts, at):
        for number, part in enumerate(parts):
            side_send[at + number] = part.astype(bf16)
        side_copy(at, len(parts)).start()

    @pl.when(step == 0)
    def _():
        for load in loads:
            load.start()
        greet([peer] + [partner_of(bit)[0] for bit in range(bits)])
        if early_down:
            other_side([down.result(tiles + i) for i in range(tiles)], 0)
        for chain in (qkv, up, proj, down):
            chain.step()

    heads = other_ref.shape[0]
    lanes = other_ref.shape[3]
    gain = gain_ref[...]
    first_rows = lanes // 256 * 128
    blocks = ((0, first_rows), (first_rows, half))

    def rows_copies(block):
        begin, end = blocks[block]
        at = pl.ds(begin, end - begin)
        target = out_hbm.at[pl.ds(pl.multiple_of(side * half + begin, 16), end - begin)]
        return (
            remote(out_scr.at[at], target, row_send.at[block], row_recv.at[block], peer),
            pltpu.make_async_copy(out_scr.at[at], target, store_sem.at[block]),
        )

    def input_rows(block):
        begin, end = blocks[block]
        whole_end = min(end, lanes)
        near, far = 0.0, 0.0
        for part in range(3):
            near = near + dot(mine_ref[part, :, begin:end], w_ref[part], 0, 1)
            left = other_ref[:, part, :, begin:whole_end].reshape(
                heads * HEAD_DIM, whole_end - begin
            )
            far = far + dot(left, w_other_ref[part], 0, 1)
        if end > lanes:
            rest = 0.0
            for part in range(3):
                ends = [
                    other_end_ref[:, pl.ds(head * END_WIDTH, 3 * HEAD_DIM)][
                        :, part * HEAD_DIM : (part + 1) * HEAD_DIM
                    ]
                    for head in range(heads)
                ]
                rest = rest + dot(jnp.concatenate(ends, axis=1), w_other_ref[part], 1, 1)
            far = jnp.concatenate([far, rest], axis=0)
        normed_grad = near + far
        unit, scale = norm_parts(x_scr[begin:end].astype(f32))
        out = grad_scr[begin:end] + norm_back(normed_grad, unit, scale, gain)
        out_scr[begin:end] = out.astype(bf16)
        return column_sum(normed_grad * unit), column_sum(normed_grad)

    @pl.when(step == 0)
    def _():
        for load in loads:
            load.wait()
        sums = input_rows(0)
        for copy in rows_copies(0):
            copy.start()
        total[0:1], total[1:2] = sums

    @pl.when(step == 1)
    def _():
        sums = input_rows(1)
        sums = [total[number : number + 1] + sums[number] for number in range(2)]

        both = vector_got.shape[1]
        vector_send[:, : 2 * width] = jnp.concatenate(sums, axis=1)
        vector_send[:, 2 * width :] = vector_ref[1:2, 2 * width : both]
        vector_copy = remote(vector_send, vector_got, vector_sem.at[0], vector_sem.at[1], peer)
        vector_copy.start()
        for copy in rows_copies(1):
            copy.start()

        vector_bits = list(range(bits))

        def add_vectors():
            if not vector_bits:
                return
            bit = vector_bits.pop(0)
            copy = remote(
                vector_scr,
                vector_next.at[bit],
                vector_sem.at[2 * bit + 2],
                vector_sem.at[2 * bit + 3],
                partner_of(bit)[0],
            )
            copy.start()
            copy.wait()
            vector_scr[...] += vector_next[bit]

        qkv.step()
        while proj.bits:
            proj.step()
        vector_copy.wait()
        vector_scr[:, :both] = vector_got[...] + jnp.concatenate(
            sums + [vector_ref[0:1, 2 * width : both]], axis=1
        )
        vector_scr[:, both:] = vector_ref[0:1, both:]
        add_vectors()
        if not early_down:
            down.finish()
            other_side([down.result(tiles + i) for i in range(tiles)], 0)
        up.finish()
        other_side([up.result(tiles + i) for i in range(tiles)], tiles)
        add_vectors()
        qkv.step()
        proj.step()
        other_side([proj.result(1)], 2 * tiles)
        add_vectors()
        side_copy(0, tiles).wait()
        for tile in range(tiles):
            at = pl.ds(tile * FF_TILE, FF_TILE)
            down_ref[:, at] = down.result(tile) + side_got[tile].astype(f32)
        qkv.finish()
        for part in range(3):
            qkv_ref[part] = qkv.result(part)
        while vector_bits:
            add_vectors()
        total_ref[...] = vector_scr[...]
        side_copy(tiles, tiles).wait()
        for tile in range(tiles):
            at = pl.ds(tile * FF_TILE, FF_TILE)
            up_ref[:, at] = up.result(tile) + side_got[tiles + tile].astype(f32)
        side_copy(2 * tiles, 1).wait()
        proj_ref[...] = proj.result(0) + side_got[2 * tiles].astype(f32)
        for block in range(2):
            far, near = rows_copies(block)
            near.wait()
            far.wait()


def input_backward(
    count,
    mine,
    other,
    other_end,
    weight,
    weight_other,
    gain,
    vectors,
    down_sum,
    up_sum,
    proj_sum,
    qkv_keep,
    qkv_got,
    patches,
    residual_grad,
):
    tokens, width = patches.shape
    half = tokens // 2
    columns = mine.shape[1]
    heads = other.shape[0]
    bits = count.bit_length() - 1
    rows = width // count
    tiles = heads // 2
    size = vectors.shape[1]
    both = size - FF_TILE * 3
    vmem = pltpu.VMEM
    dma = lambda *shape: pltpu.SemaphoreType.DMA(shape)
    scratch = []
    for first, lead in ((4, heads), (3, heads), (2, 2), (1, 3)):
        for bit in range(first, bits):
            shape = (lead, count >> (bit + 1), rows, FF_TILE)
            scratch += [vmem(shape, bf16), vmem(shape, bf16), vmem(shape, bf16), dma(2)]
    return pl.pallas_call(
        functools.partial(input_back_kernel, bits),
        grid=(2,),
        in_specs=[
            once(other_end.shape),
            once((1, width)),
            once(vectors.shape),
            once(down_sum.shape),
            once(up_sum.shape),
            once(proj_sum.shape),
            once(qkv_keep.shape),
            once(qkv_got.shape),
            HBM,
            HBM,
            HBM,
            HBM,
            HBM,
            HBM,
        ],
        out_specs=(
            once((1, size)),
            once((rows, tiles * FF_TILE)),
            once((rows, tiles * FF_TILE)),
            once((rows, columns)),
            once((3, rows, columns)),
            HBM,
        ),
        out_shape=(
            jax.ShapeDtypeStruct((1, size), f32),
            jax.ShapeDtypeStruct((rows, tiles * FF_TILE), f32),
            jax.ShapeDtypeStruct((rows, tiles * FF_TILE), f32),
            jax.ShapeDtypeStruct((rows, columns), f32),
            jax.ShapeDtypeStruct((3, rows, columns), f32),
            jax.ShapeDtypeStruct((tokens, width), bf16),
        ),
        scratch_shapes=[
            vmem((2, width), f32),
            vmem(mine.shape, bf16),
            vmem(other.shape, bf16),
            vmem(weight.shape, bf16),
            vmem(weight_other.shape, bf16),
            vmem((half, width), bf16),
            vmem((half, width), f32),
            vmem((half, width), bf16),
            vmem((1, both), f32),
            vmem((1, both), f32),
            vmem((1, size), f32),
            vmem((bits, 1, size), f32),
            vmem((2 * tiles + 1, rows, FF_TILE), bf16),
            vmem((2 * tiles + 1, rows, FF_TILE), bf16),
            dma(6),
            dma(2),
            dma(2),
            dma(2),
            dma(2 * bits + 2),
            dma(6),
        ]
        + scratch,
        compiler_params=params(1),
        cost_estimate=pl.CostEstimate(
            flops=12 * half * width * columns, bytes_accessed=20_000_000, transcendentals=0
        ),
        name="input_backward",
    )(
        other_end,
        gain[None, :],
        vectors,
        down_sum,
        up_sum,
        proj_sum,
        qkv_keep,
        qkv_got,
        mine,
        other,
        weight,
        weight_other,
        patches,
        residual_grad,
    )


def result_kernel(sizes, vector_ref, *refs):
    count = (len(refs) - len(sizes)) // 2
    sources, targets = refs[:count], refs[count : 2 * count]
    for source, target in zip(sources[-2:], targets[-2:]):
        target[...] = source[...]

    @pl.when(pl.program_id(0) == 0)
    def _():
        for source, target in zip(sources[:-2], targets[:-2]):
            target[...] = source[...]
        begin = 0
        for (rows, columns), target in zip(sizes, refs[2 * count :]):
            for row in range(rows):
                target[row : row + 1, :] = vector_ref[:, pl.ds(begin, columns)]
                begin += columns


def results(vectors, sizes, arrays, rows):
    step = rows[0].shape[0] // RESULT_STEPS
    long_block = pl.BlockSpec((step, rows[0].shape[1]), lambda i: (i, 0))
    specs = [once(x.shape) for x in arrays] + [long_block] * len(rows)
    out = pl.pallas_call(
        functools.partial(result_kernel, sizes),
        grid=(RESULT_STEPS,),
        in_specs=[once(vectors.shape)] + specs,
        out_specs=specs + [once(x) for x in sizes],
        out_shape=[jax.ShapeDtypeStruct(x.shape, x.dtype) for x in list(arrays) + list(rows)]
        + [jax.ShapeDtypeStruct(x, f32) for x in sizes],
        compiler_params=params(),
        name="results",
    )(vectors, *arrays, *rows)
    count = len(arrays) + len(rows)
    return out[:count], list(out[count:])


def on_device(
    count,
    patches,
    cotangent,
    clip_lengths,
    attn_gain,
    attn_shift,
    qkv_weight,
    qkv_bias,
    proj_weight,
    proj_bias,
    mlp_gain,
    mlp_shift,
    up_weight,
    up_bias,
    down_weight,
    down_bias,
):
    tokens, width = patches.shape
    local_width = proj_weight.shape[0]

    qkv_parts = jnp.transpose(qkv_weight, (1, 0, 2))

    clip_len = clip_lengths[0, 0]
    cosine, sine = rotary_angles(jnp.arange(tokens, dtype=jnp.int32) % clip_len)
    query_mask, key_mask = clip_masks(clip_len, tokens)
    (
        normed,
        qkv,
        attended,
        att_mine,
        totals,
        up_biases,
        weights,
        att_other,
        proj_other,
        up_other,
        down_part,
    ) = attend_forward(
        patches,
        attn_gain,
        attn_shift,
        qkv_parts,
        qkv_bias,
        cosine,
        sine,
        query_mask,
        key_mask,
        up_bias,
        proj_weight,
        up_weight,
        down_weight,
    )
    (
        residual_grad,
        att_grad_mine,
        att_grad_send,
        vectors,
        up_bias_grad,
        down_keep,
        up_keep,
        block_out,
        att_grad_got,
        up_got,
        down_got,
        _,
        qkv_other,
    ) = feed_forward(
        count,
        att_mine,
        att_other,
        proj_weight,
        proj_other,
        proj_bias,
        mlp_gain,
        mlp_shift,
        down_bias,
        up_biases,
        patches,
        cotangent,
        up_weight,
        up_other,
        down_weight,
        down_part,
        qkv_parts,
    )
    (
        mixed_mine,
        qkv_keep,
        qkv_bias_grad,
        down_sum,
        up_sum,
        proj_sum,
        mixed_other,
        mixed_end,
        qkv_got,
        _,
    ) = attend_backward(
        count,
        weights,
        qkv,
        attended,
        totals,
        att_grad_mine,
        att_grad_send,
        att_grad_got,
        cosine,
        sine,
        normed,
        down_keep,
        down_got,
        up_keep,
        up_got,
    )

    hidden = up_bias.shape[0]
    vectors = vectors.reshape(1, -1)
    up_bias_grad = up_bias_grad.reshape(2, hidden)
    ends = jnp.zeros((2, 2 * width), f32)
    vectors = jnp.concatenate(
        [
            ends,
            jnp.concatenate([vectors, vectors]),
            up_bias_grad,
            jnp.concatenate([qkv_bias_grad.reshape(1, -1)] * 2),
        ],
        axis=1,
    )
    vectors, down_grad, up_grad, proj_grad, qkv_grad, patch_grad = input_backward(
        count,
        mixed_mine,
        mixed_other,
        mixed_end,
        qkv_parts,
        qkv_other,
        attn_gain,
        vectors,
        down_sum,
        up_sum,
        proj_sum,
        qkv_keep,
        qkv_got,
        patches,
        residual_grad,
    )
    sizes = [(width // 128, 128)] * 6 + [(hidden // 128, 128), (3, local_width)]
    (down_grad, up_grad, proj_grad, qkv_grad, block_out, patch_grad), pieces = results(
        vectors, sizes, [down_grad, up_grad, proj_grad, qkv_grad], [block_out, patch_grad]
    )
    qkv_bias_grad = pieces.pop()
    attn_gain_grad, attn_shift_grad, mlp_gain_grad, mlp_shift_grad = (
        x.reshape(-1) for x in pieces[:4]
    )
    proj_bias_grad, down_bias_grad, up_bias_grad = (x.reshape(-1) for x in pieces[4:])
    return (
        block_out,
        patch_grad,
        attn_gain_grad,
        attn_shift_grad,
        jnp.transpose(qkv_grad, (1, 0, 2)),
        qkv_bias_grad,
        proj_grad.T,
        proj_bias_grad,
        mlp_gain_grad,
        mlp_shift_grad,
        up_grad,
        up_bias_grad,
        down_grad.T,
        down_bias_grad,
    )


def solution(mesh):
    return jax.shard_map(
        functools.partial(on_device, mesh.shape["dp"]),
        mesh=mesh,
        in_specs=(
            P("dp", None),
            P("dp", None),
            P("dp", None),
            P(),
            P(),
            P(None, None, "tensor"),
            P(None, "tensor"),
            P("tensor", None),
            P(),
            P(),
            P(),
            P(None, "tensor"),
            P("tensor"),
            P("tensor", None),
            P(),
        ),
        out_specs=(
            P("dp", None),
            P("dp", None),
            P(),
            P(),
            P("dp", None, "tensor"),
            P(None, "tensor"),
            P("tensor", "dp"),
            P(),
            P(),
            P(),
            P("dp", "tensor"),
            P("tensor"),
            P("tensor", "dp"),
            P(),
        ),
        check_vma=False,
    )
```
